32 devices in a mesh: groups: 2 (over x), gx: 16 (over z, y, core).
Axes of the slice: x: 2, y: 2, z: 4, core: 2. Of those that a mesh axis runs over, the one named last changes fastest.
Arguments:
- velocity: float32 [3, 32, 4, 32, 128], P(None, ('groups', 'gx')), parts along dimension 1, may hold values from -6 to 6
- stress: float32 [6, 32, 4, 32, 128], P(None, ('groups', 'gx')), parts along dimension 1, may hold values from -6 to 6
- memory: float32 [6, 32, 4, 32, 128], P(None, ('groups', 'gx')), parts along dimension 1, may hold values from -4 to 4
- lame_lambda: float32 [32, 4, 32, 128], P(('groups', 'gx')), parts along dimension 0, may hold values from 1.5 to 2.5
- lame_mu: float32 [32, 4, 32, 128], P(('groups', 'gx')), parts along dimension 0, may hold values from 0.1 to 0.5
- buoyancy: float32 [32, 4, 32, 128], P(('groups', 'gx')), parts along dimension 0, may hold values from 0.7 to 1
- decay: float32 [32, 4, 32, 128], P(('groups', 'gx')), parts along dimension 0, may hold values from 0.3 to 0.95
- loss: float32 [32, 4, 32, 128], P(('groups', 'gx')), parts along dimension 0, may hold values from 0.1 to 1
- tile_lambda: bfloat16 [256, 256], P(('groups', 'gx')), parts along dimension 0, may hold values from 3 to 4.5
- tile_mu: bfloat16 [256, 256], P(('groups', 'gx')), parts along dimension 0, may hold values from 1 to 2
- tile_buoy: bfloat16 [256, 256], P(('groups', 'gx')), parts along dimension 0, may hold values from 0.3984375 to 0.59765625
- tile_dest: int32 [256], P(('groups', 'gx')), parts along dimension 0, may hold values from -1 to 15, as said below
- brick_tiles: int32 [32, 64], P(('groups', 'gx')), parts along dimension 0, may hold values from -1 to 127, as said below
- src_index: int32 [512], P(('groups', 'gx')), parts along dimension 0, may hold values from 0 to 16383
- src_wave: float32 [512, 2], P(('groups', 'gx')), parts along dimension 0, may hold values from -6 to 6
Outputs:
- new_velocity: float32 [3, 32, 4, 32, 128], P(None, ('groups', 'gx')), parts along dimension 1
- new_stress: float32 [6, 32, 4, 32, 128], P(None, ('groups', 'gx')), parts along dimension 1
- new_memory: float32 [6, 32, 4, 32, 128], P(None, ('groups', 'gx')), parts along dimension 1
The draws below stay inside these ranges and needn't reach their ends.
There are 2 independent parts, one for each index of `groups`. The reference program is written for one: setup_inputs(seed, part) draws one part's arguments, and reference() takes and returns one part's arrays. A program takes and returns all parts, laid end to end along the dimension named above; each array names one. Nothing has to cross between parts.
Inputs may be any that keep to these rules, and one draw needn't show every extreme that they name: `tile_dest`: the 8 tiles stored on one device name distinct bricks; a brick receives at most 8 tiles, and some brick exactly 8 in every draw. `brick_tiles`: row b holds, at distinct positions, exactly the tiles whose tile_dest is b, each once.
All inputs are finite; a program needn't handle non-finite values.
Results may differ from the reference program's by a relative error of at most 0.00075.
Values may be sent and summed in bfloat16 or wider, within the bound.
No kernel may reach another device: no remote copies, remote signals or barrier semaphores. Data moves between devices by JAX's collectives and lax.ppermute only.
A program may use at most 64 MiB of HBM per device.

```python
import jax
import jax.numpy as jnp
from jax import lax

BX = 4
BY = 32
NZ = 128
PY = 8
TY = 8
TZ = 8
STEPS = 2
ELEMS_DEV = 16
PX = 2
BRICKS = 16
TILES_DEV = 8
TILES = 128
SUBS_Y = 4
SUBS_Z = 16
SUBS = 64
TCELLS = 256
NX = 8
NY = 256
ELEMS = 256


def route_tables(key):
    offset_key, place_key, heavy_key, chosen_key, load_key = jax.random.split(key, 5)
    middle = BRICKS // 2
    drawn = jax.random.permutation(offset_key, BRICKS - 4) + 2
    drawn = jnp.where(drawn >= middle, drawn + 1, drawn)
    others = drawn[:TILES_DEV - 3].astype(jnp.int32)
    offsets = jnp.concatenate([jnp.array([1, BRICKS - 1, middle], jnp.int32), others]).astype(jnp.int32)
    places = jax.random.permutation(place_key, SUBS)[:TILES_DEV].astype(jnp.int32)
    heavy = jax.random.randint(heavy_key, (BRICKS,), 0, 2) == 0
    chosen = jax.random.randint(chosen_key, (), 0, BRICKS)
    heavy = heavy | (jnp.arange(BRICKS) == chosen)
    lighter = jax.random.randint(load_key, (BRICKS,), TILES_DEV // 2, TILES_DEV + 1)
    loads = jnp.where(heavy, TILES_DEV, lighter).astype(jnp.int32)
    return (offsets, places, loads)


def draw_tile_dest(key, part):
    offsets, places, loads = route_tables(jax.random.fold_in(key, 11))
    source = jnp.arange(BRICKS, dtype=jnp.int32)[:, None]
    target = (source + offsets[None, :]) % BRICKS
    slot_ids = jnp.arange(TILES_DEV, dtype=jnp.int32)[None, :]
    live = slot_ids < loads[target]
    return jnp.where(live, target, -1).reshape(-1).astype(jnp.int32)


def draw_brick_tiles(key, part):
    offsets, places, loads = route_tables(jax.random.fold_in(key, 11))
    bricks = jnp.arange(BRICKS, dtype=jnp.int32)[:, None]
    slot_ids = jnp.arange(TILES_DEV, dtype=jnp.int32)[None, :]
    source = (bricks - offsets[None, :]) % BRICKS
    idents = source * TILES_DEV + slot_ids
    values = jnp.where(slot_ids < loads[:, None], idents, -1).astype(jnp.int32)
    table = jnp.full((BRICKS, SUBS), -1, jnp.int32)
    return table.at[:, places].set(values)


def place_ends(entries, stream_key, low, largest):
    longest = entries.shape.index(max(entries.shape))
    spots = []
    for shift in (0, 1):
        where = [jax.random.randint(jax.random.fold_in(stream_key, axis), (), 0, length) for axis, length in enumerate(entries.shape)]
        where[longest] = (where[longest] + shift) % entries.shape[longest]
        spots.append(tuple(where))
    return entries.at[spots[0]].set(low).at[spots[1]].set(largest)


def shard_levels(rng, extent, pieces, least, high):
    gain = 1.0
    for dim, shards_of in pieces:
        heights = jax.random.uniform(jax.random.fold_in(jax.random.fold_in(rng, 6), dim), (shards_of,), jnp.float32, least / len(pieces), high / len(pieces))
        gain = gain * jnp.repeat(jnp.exp(heights), extent[dim] // shards_of).reshape((-1,) + (1,) * (len(extent) - 1 - dim))
    return gain


def noise(rng, dims, scale, bound, cuts=(), kind=jnp.bfloat16):
    entries = jax.random.normal(rng, dims, jnp.float32) * scale
    if len(cuts) > 0:
        entries = shard_levels(rng, dims, cuts, -0.22, 0.18) * entries
    return jnp.clip(entries, min=-bound, max=bound).astype(kind)


def setup_inputs(seed: int = 0, part: int = 0) -> dict:
    streams_of = jax.random.split(jax.random.key(seed), 16)
    part_keys = jax.random.split(jax.random.fold_in(streams_of[15], part), 16)
    return {
        "velocity": noise(part_keys[0], (3, BRICKS, BX, BY, NZ), 1.0, 6.0, ((1, 16),), jnp.float32),
        "stress": noise(part_keys[1], (6, BRICKS, BX, BY, NZ), 1.0, 6.0, ((1, 16),), jnp.float32),
        "memory": noise(part_keys[2], (6, BRICKS, BX, BY, NZ), 0.5, 4.0, ((1, 16),), jnp.float32),
        "lame_lambda": jnp.clip(1.5 + 1.0 * jax.random.uniform(part_keys[3], (BRICKS, BX, BY, NZ), jnp.float32) ** shard_levels(part_keys[3], (BRICKS, BX, BY, NZ), ((0, 16),), -0.2, 0.2), 1.5, 2.5),
        "lame_mu": jnp.clip(0.1 + 0.4 * jax.random.uniform(part_keys[4], (BRICKS, BX, BY, NZ), jnp.float32) ** shard_levels(part_keys[4], (BRICKS, BX, BY, NZ), ((0, 16),), -0.2, 0.2), 0.1, 0.5),
        "buoyancy": jnp.clip(0.7 + 0.3 * jax.random.uniform(part_keys[5], (BRICKS, BX, BY, NZ), jnp.float32) ** shard_levels(part_keys[5], (BRICKS, BX, BY, NZ), ((0, 16),), -0.2, 0.2), 0.7, 1.0),
        "decay": jnp.clip(0.3 + 0.65 * jax.random.uniform(part_keys[6], (BRICKS, BX, BY, NZ), jnp.float32) ** shard_levels(part_keys[6], (BRICKS, BX, BY, NZ), ((0, 16),), -0.2, 0.2), 0.3, 0.95),
        "loss": jnp.clip(0.1 + 0.9 * jax.random.uniform(part_keys[7], (BRICKS, BX, BY, NZ), jnp.float32) ** shard_levels(part_keys[7], (BRICKS, BX, BY, NZ), ((0, 16),), -0.2, 0.2), 0.1, 1.0),
        "tile_lambda": jnp.clip(3.0 + 1.5 * jax.random.uniform(part_keys[8], (TILES, TCELLS), jnp.float32) ** shard_levels(part_keys[8], (TILES, TCELLS), ((0, 16),), -0.2, 0.2), 3.0, 4.5).astype(jnp.bfloat16),
        "tile_mu": jnp.clip(1.0 + 1.0 * jax.random.uniform(part_keys[9], (TILES, TCELLS), jnp.float32) ** shard_levels(part_keys[9], (TILES, TCELLS), ((0, 16),), -0.2, 0.2), 1.0, 2.0).astype(jnp.bfloat16),
        "tile_buoy": jnp.clip(0.3984375 + 0.19921875 * jax.random.uniform(part_keys[10], (TILES, TCELLS), jnp.float32) ** shard_levels(part_keys[10], (TILES, TCELLS), ((0, 16),), -0.2, 0.2), 0.3984375, 0.59765625).astype(jnp.bfloat16),
        "tile_dest": draw_tile_dest(jax.random.fold_in(jax.random.fold_in(streams_of[15], part), 71), part),
        "brick_tiles": draw_brick_tiles(jax.random.fold_in(jax.random.fold_in(streams_of[15], part), 71), part),
        "src_index": place_ends(jax.random.randint(part_keys[13], (ELEMS,), 0, BX * BY * NZ), jax.random.fold_in(part_keys[13], 1), 0, (BX * BY * NZ) - 1).astype(jnp.int32),
        "src_wave": noise(part_keys[14], (ELEMS, STEPS), 1.0, 6.0, ((0, 16),), jnp.float32),
    }


courant = 0.25


def forward_diff(values, along):
    rest = lax.slice_in_dim(values, 1, values.shape[along], axis=along)
    padding = jnp.zeros_like(lax.slice_in_dim(values, 0, 1, axis=along))
    return jnp.concatenate([rest, padding], axis=along) - values


def backward_diff(values, along):
    padding = jnp.zeros_like(lax.slice_in_dim(values, 0, 1, axis=along))
    rest = lax.slice_in_dim(values, 0, values.shape[along] - 1, axis=along)
    return values - jnp.concatenate([padding, rest], axis=along)


def to_grid(values):
    lead = values.shape[:-4]
    shaped = values.reshape(lead + (PX, PY, BX, BY, NZ))
    count = len(lead)
    order = tuple(range(count)) + (count, count + 2, count + 1, count + 3, count + 4)
    return shaped.transpose(order).reshape(lead + (NX, NY, NZ))


def from_grid(values):
    lead = values.shape[:-3]
    shaped = values.reshape(lead + (PX, BX, PY, BY, NZ))
    count = len(lead)
    order = tuple(range(count)) + (count, count + 2, count + 1, count + 3, count + 4)
    return shaped.transpose(order).reshape(lead + (BRICKS, BX, BY, NZ))


def to_helix(grid_field):
    return from_grid(grid_field).transpose(1, 0, 2, 3).reshape(BX, BRICKS * BY, NZ)


def from_helix(cycle_field):
    return to_grid(cycle_field.reshape(BX, BRICKS, BY, NZ).transpose(1, 0, 2, 3))


def helix_forward(values):
    cycle_field = to_helix(values)
    return from_helix(jnp.roll(cycle_field, -1, axis=1) - cycle_field)


def helix_backward(values):
    cycle_field = to_helix(values)
    return from_helix(cycle_field - jnp.roll(cycle_field, 1, axis=1))


def bone_field(background, tiles, brick_tiles, tile_dest):
    safe_ids = jnp.where(brick_tiles >= 0, brick_tiles, 0).astype(jnp.int32)
    owner_ok = jnp.take(tile_dest, safe_ids, axis=0) == jnp.arange(BRICKS, dtype=jnp.int32)[:, None]
    live = (brick_tiles >= 0) & owner_ok
    picked = jnp.take(tiles, safe_ids, axis=0).astype(jnp.float32)
    picked = picked.reshape(BRICKS, SUBS_Y, SUBS_Z, BX, TY, TZ).transpose(0, 3, 1, 4, 2, 5).reshape(BRICKS, BX, BY, NZ)
    inside = jnp.broadcast_to(live.reshape(BRICKS, SUBS_Y, SUBS_Z)[:, None, :, None, :, None], (BRICKS, BX, SUBS_Y, TY, SUBS_Z, TZ)).reshape(BRICKS, BX, BY, NZ)
    return to_grid(jnp.where(inside, picked, background))


def reference(velocity, stress, memory, lame_lambda, lame_mu, buoyancy, decay, loss, tile_lambda, tile_mu, tile_buoy, tile_dest, brick_tiles, src_index, src_wave):
    lame = bone_field(lame_lambda, tile_lambda, brick_tiles, tile_dest)
    shear = bone_field(lame_mu, tile_mu, brick_tiles, tile_dest)
    buoy_field = bone_field(buoyancy, tile_buoy, brick_tiles, tile_dest)
    decay_grid = to_grid(decay)
    loss_grid = to_grid(loss)
    velocity = to_grid(velocity)
    stress = to_grid(stress)
    memory = to_grid(memory)
    owners = jnp.arange(ELEMS, dtype=jnp.int32) // ELEMS_DEV
    cells = owners * (BX * BY * NZ) + src_index
    for step_index in range(STEPS):
        grad_x = forward_diff(stress[0], 0) + helix_backward(stress[3]) + backward_diff(stress[4], 2)
        grad_y = backward_diff(stress[3], 0) + helix_forward(stress[1]) + backward_diff(stress[5], 2)
        grad_z = backward_diff(stress[4], 0) + helix_backward(stress[5]) + forward_diff(stress[2], 2)
        velocity = velocity + courant * buoy_field * jnp.stack([grad_x, grad_y, grad_z])
        strain_x = backward_diff(velocity[0], 0)
        strain_y = helix_backward(velocity[1])
        strain_z = backward_diff(velocity[2], 2)
        dilation = strain_x + strain_y + strain_z
        rates = jnp.stack([
            lame * dilation + 2.0 * shear * strain_x,
            lame * dilation + 2.0 * shear * strain_y,
            lame * dilation + 2.0 * shear * strain_z,
            shear * (helix_forward(velocity[0]) + forward_diff(velocity[1], 0)),
            shear * (forward_diff(velocity[0], 2) + forward_diff(velocity[2], 0)),
            shear * (forward_diff(velocity[1], 2) + helix_forward(velocity[2]))])
        memory = decay_grid * memory - (1.0 - decay_grid) * loss_grid * rates
        stress = stress + courant * (rates + memory)
        source = jnp.zeros((BRICKS * BX * BY * NZ,), jnp.float32).at[cells].add(src_wave[:, step_index]).reshape(BRICKS, BX, BY, NZ)
        stress = stress.at[:3].add(to_grid(source)[None])
    return from_grid(velocity), from_grid(stress), from_grid(memory)
```

```python
import functools

import jax
import jax.numpy as jnp
from jax import lax
from jax.experimental import pallas as pl
from jax.experimental.pallas import tpu as pltpu
from jax.sharding import PartitionSpec as P

PY = 8
TY = 8
TZ = 8
courant = 0.25

F32 = jnp.float32
BF16 = jnp.bfloat16
XX, YY, ZZ, XY, XZ, YZ = range(6)
STRESS, VEL, HELD, GAIN, LAME, MU, BUOY = 0, 6, 9, 15, 16, 17, 18
FIELDS = 19
LAST = [(STRESS + c, i) for c in (XX, XY, XZ) for i in (2, 3)] + [(STRESS + c, 3) for c in (YY, ZZ, YZ)]
LAST += [(VEL, 2), (VEL, 3), (VEL + 1, 3), (VEL + 2, 3), (BUOY, 2), (BUOY, 3)]
LAST += [(HELD + c, 3) for c in (XX, XY, XZ)] + [(GAIN, 3), (LAME, 3), (MU, 3)]
FIRST = [(STRESS + c, i) for c in range(6) for i in (0, 1)]
FIRST += [(VEL, 0), (VEL + 1, 0), (VEL + 1, 1), (VEL + 2, 0), (VEL + 2, 1), (BUOY, 0), (BUOY, 1)]
FIRST += [(HELD + c, 0) for c in range(6)] + [(GAIN, 0), (LAME, 0), (MU, 0)]
LONGEST = max(len(LAST), len(FIRST))
ROWS = 32
EXT = ROWS + 8
LANES = 128
BLOCK = FIELDS * 8 + 8


def pair_near(i):
    return i ^ 1


def pair_far(i, n):
    return (i - 1) % n if i % 2 == 0 else (i + 1) % n


def is_merged(n):
    return n == 2 * PY


def tile_offsets(n):
    if is_merged(n):
        return [0, -1, 1, PY, PY - 1, PY + 1]
    return [0, -1, 1, -PY, -PY - 1, -PY + 1, PY, PY - 1, PY + 1]


def slot_count(n):
    return 8 if is_merged(n) else 16


def roll(x, by, axis):
    size = x.shape[axis]
    by = by % size
    return x if by == 0 else pltpu.roll(x, by, axis)


def sublane(shape):
    return lax.broadcasted_iota(jnp.int32, shape, 0)


def lane(shape):
    return lax.broadcasted_iota(jnp.int32, shape, 1)


def place_sources(into, index, wave, step, count):
    into[...] = jnp.zeros_like(into)
    lanes = lane((1, LANES))
    for e in range(count):
        cell = index[e]
        row = lax.shift_right_logical(cell, 7)
        here = jnp.where(lanes == (cell & (LANES - 1)), wave[e, step], 0.0)
        into[pl.ds(row, 1), :] = into[pl.ds(row, 1), :] + here


def pack_kernel(n, *refs):
    merged = is_merged(n)
    (vel, st, mem, lam, mu, bu, dec, los, t_lam, t_mu, t_bu, dest, tiles, index, wave) = refs[:15]
    outs = refs[15:]
    out_a, out_b, out_d, out_e, out_t, out_map = outs[:6]
    out_c = outs[6 : 7 if merged else 8]
    held, gain, source = outs[7 if merged else 8 :]
    b = lax.axis_index("gx")
    even = lax.rem(b, 2) == 0
    place_sources(source, index, wave, 0, index.shape[0])
    for i in range(4):
        d = dec[0, i]
        gain[i] = courant * (1.0 - (1.0 - d) * los[0, i])
        kept = courant * d
        for c in range(6):
            value = st[c, 0, i] + kept * mem[c, 0, i]
            if c < 3:
                value = value + source[i * ROWS : (i + 1) * ROWS, :]
            held[c, i] = value

    def get(f, i, rows=slice(None)):
        if f < VEL:
            return st[f, 0, i, rows]
        if f < HELD:
            return vel[f - VEL, 0, i, rows]
        if f < GAIN:
            return held[f - HELD, i, rows]
        if f == GAIN:
            return gain[i, rows]
        return (lam, mu, bu)[f - LAME][0, i, rows]

    sub = sublane((8, LANES))
    top, bottom = slice(0, 8), slice(ROWS - 8, ROWS)

    per = t_lam.shape[0]
    rows_z = LANES // TZ
    table = tiles[...]
    spots = table.shape[1]
    owner = jnp.where(table >= 0, jnp.floor((table.astype(F32) + 0.5) * (1.0 / per)) + 1.0, 0.0)
    spot = lane((8, spots))
    wide = jnp.where(spot // rows_z == sublane((8, spots)), jnp.broadcast_to(owner, (8, spots)), 0.0)
    spread = (lax.rem(sublane((spots, LANES)), rows_z) == lane((spots, LANES)) // TZ).astype(BF16)
    owners = jnp.dot(wide.astype(BF16), spread, preferred_element_type=F32) - 1.0
    out_map[...] = owners

    def edge_rows(f):
        if f == FIELDS:
            lo = jnp.broadcast_to(owners[0:1], (8, LANES))
            hi = jnp.broadcast_to(owners[ROWS // TY - 1 : ROWS // TY], (8, LANES))
            return lo, hi
        lo, hi = get(f, 0, top), roll(get(f, 0, bottom), 2, 0)
        for i in range(1, 4):
            mine = sub // 2 == i
            lo = jnp.where(mine, roll(get(f, i, top), 2 * i, 0), lo)
            hi = jnp.where(mine, roll(get(f, i, bottom), 2 * i + 2, 0), hi)
        return lo, hi

    for f in range(0, FIELDS + 1, 2):
        near, far = [], []
        for g in (f, f + 1):
            lo, hi = edge_rows(g)
            near.append(jnp.where(even, hi, lo))
            far.append(jnp.where(even, lo, hi))
        near, far = jnp.concatenate(near, 0), jnp.concatenate(far, 0)
        out_a[f * 8 : f * 8 + 16, :] = near
        out_b[f * 8 : f * 8 + 16, :] = far
        out_e[f * 8 : f * 8 + 16, :] = near.astype(BF16)
        out_d[f * 8 : f * 8 + 16, :] = far.astype(BF16)

    def write_layers(out, which):
        for k, (f, i) in enumerate(which):
            out[k * ROWS : (k + 1) * ROWS, :] = get(f, i).astype(BF16)

    if merged:
        out = out_c[0]
        first_x = b < PY

        @pl.when(first_x)
        def _():
            write_layers(out, LAST)
            rest = (LONGEST - len(LAST)) * ROWS
            if rest:
                out[len(LAST) * ROWS : LONGEST * ROWS, :] = jnp.zeros((rest, LANES), BF16)

        @pl.when(jnp.logical_not(first_x))
        def _():
            write_layers(out, FIRST)
            rest = (LONGEST - len(FIRST)) * ROWS
            if rest:
                out[len(FIRST) * ROWS : LONGEST * ROWS, :] = jnp.zeros((rest, LANES), BF16)

        def other_edge(f):
            if f == FIELDS:
                return owners
            parts = []
            for a in (0, 1):
                lo = jnp.where(first_x, get(f, a, top), get(f, a + 2, top))
                hi = jnp.where(first_x, get(f, a, bottom), get(f, a + 2, bottom))
                parts.append(jnp.where(lax.rem(sub, 4) < 2, roll(lo, 4 * a, 0), roll(hi, 4 * a + 4, 0)))
            return jnp.where(sub < 4, parts[0], parts[1])

        for f in range(0, FIELDS + 1, 2):
            both = jnp.concatenate([other_edge(f), other_edge(f + 1)], 0)
            out[LONGEST * ROWS + f * 8 : LONGEST * ROWS + f * 8 + 16, :] = both.astype(BF16)
    else:
        for out, which in zip(out_c, (LAST, FIRST)):
            write_layers(out, which)
            twice = jnp.concatenate([owners, owners], 0).astype(BF16)
            out[len(which) * ROWS : len(which) * ROWS + 16, :] = twice

    slots = slot_count(n)
    offsets = tile_offsets(n)
    total = n * slots
    at = lane((1, per))
    stored = jnp.full((1, per), -1, jnp.int32)
    for t in range(per):
        stored = jnp.where(at == t, dest[t], stored)
    row = sublane((total, per))
    slot = lax.rem(row, slots)
    shift = jnp.full((total, per), -4 * n, jnp.int32)
    for k, off in enumerate(offsets):
        shift = jnp.where(slot == k, off % n, shift)
    brick = row // slots + shift
    brick = jnp.where(brick >= n, brick - n, brick)
    route = (brick == stored).astype(BF16)
    for p, source_tiles in enumerate((t_lam, t_mu, t_bu)):
        picked = jnp.dot(route, source_tiles[...], preferred_element_type=F32)
        for d in range(n):
            here = picked[d * slots : (d + 1) * slots]
            both = jnp.concatenate([here[:, :LANES], here[:, LANES:]], 0).astype(BF16)
            base = (d * 6 + 2 * p) * slots
            out_t[base : base + 2 * slots, :] = both


def wave_kernel(n, *refs):
    merged = is_merged(n)
    (vel, st, mem, lam, mu, bu, dec, los, index, wave, maps, got_a, got_b, got_t) = refs[:14]
    refs = refs[14:]
    sides = 1 if merged else 2
    got_c, got_d, got_e = refs[:sides], refs[sides : 2 * sides], refs[2 * sides : 3 * sides]
    new_v, new_s, new_m, source, rows_t, spread_rows, tile_rows = refs[3 * sides :]
    b = lax.axis_index("gx")
    even = lax.rem(b, 2) == 0
    first_x = b < PY
    slots = slot_count(n)
    sub = sublane((8, LANES))

    def halo_blocks(near, far, f):
        x = near[f * 8 : f * 8 + 8, :]
        y = far[f * 8 : f * 8 + 8, :]
        return jnp.where(even, x, y), jnp.where(even, y, x)

    def halo_rows(blocks, i):
        after, before = blocks
        return jnp.where(sub < 2, roll(after, -2 * i, 0), roll(before, 6 - 2 * i, 0))

    def widen(ref):
        rows = ref.shape[0]
        return jnp.concatenate([ref[r : r + 16, :].astype(F32) for r in range(0, rows, 16)], 0)

    rows_t[...] = got_t[...].astype(F32)
    chunk = 6 * slots
    col = lane((16, LANES))
    line = sublane((16, LANES))
    on_line = col // TZ == line
    spread = (lax.rem(sublane((LANES, LANES)), TZ) == lax.rem(lane((LANES, LANES)), TZ)).astype(BF16)

    def tile_block(first, prop, pick):
        for s in range(16):
            for half in (0, 1):

                def row_of(k):
                    at = (first + s) * chunk + (2 * prop + half) * slots + k
                    return jnp.broadcast_to(rows_t[pl.ds(at, 1), :], (16, LANES))

                if len(pick) == 1:
                    value = row_of(pick[0])
                else:
                    value = jnp.where(lax.rem(line, TY) < 2, row_of(pick[1]), row_of(pick[0]))
                at = s * 32 + half * 16
                spread_rows[at : at + 16, :] = jnp.where(on_line, value, 0.0).astype(BF16)
        tile_rows[...] = jnp.dot(spread_rows[...], spread, preferred_element_type=F32)

    def overlay(prop, pick, wanted):
        def take(first, values):
            tile_block(first, prop, pick)
            done = []
            for value, (_, owner, i) in zip(values, wanted):
                for s in range(16):
                    here = tile_rows[s * 32 + i * 8 : s * 32 + i * 8 + 8, :]
                    value = jnp.where(owner == (first + s) * 1.0, here, value)
                done.append(value)
            return done

        values = [w[0] for w in wanted]
        if n == 16:
            return take(0, values)
        return lax.fori_loop(0, n // 16, lambda g, v: take(g * 16, v), values)

    column = {}
    rows_y = ROWS // TY

    def own(f, i):
        if f < VEL:
            return st[f, 0, i]
        if f < HELD:
            return vel[f - VEL, 0, i]
        if f < GAIN:
            value = st[f - HELD, 0, i] + courant * dec[0, i] * mem[f - HELD, 0, i]
            if f < HELD + 3:
                value = value + source[i * ROWS : (i + 1) * ROWS, :]
            return value
        if f == GAIN:
            return courant * (1.0 - (1.0 - dec[0, i]) * los[0, i])
        return (lam, mu, bu)[f - LAME][0, i]

    def finish(mains, halos, main_map, halo_map, pick_main, pick_halo, name):
        for f in range(FIELDS):
            layers = sorted(i for g, i in mains if g == f)
            if not layers:
                continue
            main = [mains[f, i] for i in layers]
            halo = [halos[f, i] for i in layers]
            if f >= LAME:
                wanted = []
                for i, m in zip(layers, main):
                    for p in range(rows_y):
                        owner = jnp.broadcast_to(main_map[p : p + 1], (8, LANES))
                        wanted.append((m[p * 8 : (p + 1) * 8], owner, i))
                laid = overlay(f - LAME, (pick_main,), wanted)
                main = [jnp.concatenate(laid[k * rows_y : (k + 1) * rows_y], 0) for k in range(len(layers))]
                halo = overlay(f - LAME, pick_halo, [(h, halo_map, i) for i, h in zip(layers, halo)])
            for i, m, h in zip(layers, main, halo):
                column[name, f, i] = jnp.concatenate([m, h], 0)

    place_sources(source, index, wave, 0, index.shape[0])
    mains, halos = {}, {}
    for f in range(FIELDS):
        blocks = halo_blocks(got_a, got_b, f)
        for i in range(4):
            mains[f, i] = own(f, i)
            halos[f, i] = halo_rows(blocks, i)
    after, before = halo_blocks(got_a, got_b, FIELDS)
    finish(mains, halos, maps[...], jnp.where(sub < 4, after, before), 0, (1, 2), "own")

    for side, (name, which) in enumerate((("before", LAST), ("after", FIRST))):
        mains, halos = {}, {}
        if merged:
            message = got_c[0]
            near, far = widen(got_e[0]), widen(got_d[0])
            base = LONGEST * ROWS
            edges = widen(message.at[base : base + BLOCK])
            whole = first_x if name == "after" else jnp.logical_not(first_x)
            main_map = edges[FIELDS * 8 : FIELDS * 8 + 8]
            picks = 3, (4, 5)
        else:
            message = got_c[side]
            near, far = widen(got_e[side]), widen(got_d[side])
            base = len(which) * ROWS
            main_map = message[base : base + 16, :].astype(F32)[0:8]
            picks = 3 + 3 * side, (4 + 3 * side, 5 + 3 * side)
        for k, (f, i) in enumerate(which):
            main = message[k * ROWS : (k + 1) * ROWS, :].astype(F32)
            if merged:
                edge = edges[f * 8 : f * 8 + 8]
                a = i % 2
                head = jnp.where(sub < 2, roll(edge, -4 * a, 0), 0.0)
                tail = jnp.where(sub >= 6, roll(edge, 4 - 4 * a, 0), 0.0)
                only = jnp.concatenate([head, jnp.zeros((ROWS - 16, LANES), F32), tail], 0)
                main = jnp.where(whole, main, only)
            mains[f, i] = main
            halos[f, i] = halo_rows(halo_blocks(near, far, f), i)
        after, before = halo_blocks(near, far, FIELDS)
        finish(mains, halos, main_map, jnp.where(sub < 4, after, before), picks[0], picks[1], name)

    def layers_of(f):
        names = [("before", 2), ("before", 3)] + [("own", i) for i in range(4)] + [("after", 0), ("after", 1)]
        return [column.get((name, f, i)) for name, i in names]

    s0 = [layers_of(STRESS + c) for c in range(6)]
    v0 = [layers_of(VEL + c) for c in range(3)]
    held = [layers_of(HELD + c) for c in range(6)]
    gain, lame, shear, buoy = (layers_of(f) for f in (GAIN, LAME, MU, BUOY))

    tall = sublane((EXT, LANES))
    wide = lane((EXT, LANES))

    def linked(test):
        def of(step):
            q = lax.rem(b + step + n, n)
            return jnp.where(test(q), 1, 0)

        flags = jnp.where(tall < ROWS, of(0), jnp.where(tall < ROWS + 4, of(1), of(-1)))
        return flags == 1

    link_before = linked(lambda q: q >= PY)
    link_after = linked(lambda q: q < n - PY)

    def x_next(a, l):
        if l == 1:
            return jnp.where(link_before, a[2], 0.0)
        if l == 5:
            return jnp.where(link_after, a[6], 0.0)
        return a[l + 1]

    def x_prev(a, l):
        if l == 2:
            return jnp.where(link_before, a[1], 0.0)
        if l == 6:
            return jnp.where(link_after, a[5], 0.0)
        return a[l - 1]

    def y_next(a):
        return roll(a, -1, 0)

    def y_prev(a):
        return roll(a, 1, 0)

    def z_next(a):
        return jnp.where(wide == LANES - 1, 0.0, roll(a, -1, 1))

    def z_prev(a):
        return jnp.where(wide == 0, 0.0, roll(a, 1, 1))

    def move(v, s, spans):
        new = [[None] * 8 for _ in range(3)]
        for l in spans[0]:
            grad = (x_next(s[XX], l) - s[XX][l]) + (s[XY][l] - y_prev(s[XY][l])) + (s[XZ][l] - z_prev(s[XZ][l]))
            new[0][l] = v[0][l] + courant * buoy[l] * grad
        for l in spans[1]:
            grad = (s[XY][l] - x_prev(s[XY], l)) + (y_next(s[YY][l]) - s[YY][l]) + (s[YZ][l] - z_prev(s[YZ][l]))
            new[1][l] = v[1][l] + courant * buoy[l] * grad
            grad = (s[XZ][l] - x_prev(s[XZ], l)) + (s[YZ][l] - y_prev(s[YZ][l])) + (z_next(s[ZZ][l]) - s[ZZ][l])
            new[2][l] = v[2][l] + courant * buoy[l] * grad
        return new

    def rates_at(v, l, wanted):
        out = [None] * 6
        ex = v[0][l] - x_prev(v[0], l)
        ey = v[1][l] - y_prev(v[1][l])
        ez = v[2][l] - z_prev(v[2][l])
        spread_part = lame[l] * (ex + ey + ez)
        twice = 2.0 * shear[l]
        for c, e in ((XX, ex), (YY, ey), (ZZ, ez)):
            if c in wanted:
                out[c] = spread_part + twice * e
        if XY in wanted:
            out[XY] = shear[l] * ((y_next(v[0][l]) - v[0][l]) + (x_next(v[1], l) - v[1][l]))
        if XZ in wanted:
            out[XZ] = shear[l] * ((z_next(v[0][l]) - v[0][l]) + (x_next(v[2], l) - v[2][l]))
        if YZ in wanted:
            out[YZ] = shear[l] * ((z_next(v[1][l]) - v[1][l]) + (y_next(v[2][l]) - v[2][l]))
        return out

    v1 = move(v0, s0, (range(0, 7), range(1, 8)))
    s1 = [[None] * 8 for _ in range(6)]
    m1 = {}
    for l in range(1, 7):
        wanted = (XX, XY, XZ) if l == 1 else range(6)
        rates = rates_at(v1, l, wanted)
        for c in wanted:
            s1[c][l] = held[c][l] + gain[l] * rates[c]
            if 2 <= l < 6:
                d = dec[0, l - 2]
                m1[c, l] = d * mem[c, 0, l - 2] - (1.0 - d) * los[0, l - 2] * rates[c][:ROWS]
    v2 = move(v1, s1, (range(1, 6), range(2, 7)))
    place_sources(source, index, wave, 1, index.shape[0])
    for l in range(2, 6):
        i = l - 2
        rates = rates_at(v2, l, range(6))
        d = dec[0, i]
        lost = (1.0 - d) * los[0, i]
        for c in range(3):
            new_v[c, 0, i] = v2[c][l][:ROWS]
        for c in range(6):
            rate = rates[c][:ROWS]
            m2 = d * m1[c, l] - lost * rate
            new_m[c, 0, i] = m2
            value = s1[c][l][:ROWS] + courant * (rate + m2)
            if c < 3:
                value = value + source[i * ROWS : (i + 1) * ROWS, :]
            new_s[c, 0, i] = value


def body(
    velocity,
    stress,
    memory,
    lame_lambda,
    lame_mu,
    buoyancy,
    decay,
    loss,
    tile_lambda,
    tile_mu,
    tile_buoy,
    tile_dest,
    brick_tiles,
    src_index,
    src_wave,
):
    n = lax.axis_size("gx")
    merged = is_merged(n)
    slots = slot_count(n)
    on_core = pl.BlockSpec(memory_space=pltpu.VMEM)
    scalars = pl.BlockSpec(memory_space=pltpu.SMEM)
    fields = (velocity, stress, memory, lame_lambda, lame_mu, buoyancy, decay, loss)
    if merged:
        c_rows = [LONGEST * ROWS + BLOCK]
    else:
        c_rows = [len(LAST) * ROWS + 16, len(FIRST) * ROWS + 16]
    packed = pl.pallas_call(
        functools.partial(pack_kernel, n),
        out_shape=[
            jax.ShapeDtypeStruct((BLOCK, LANES), F32),
            jax.ShapeDtypeStruct((BLOCK, LANES), F32),
            jax.ShapeDtypeStruct((BLOCK, LANES), BF16),
            jax.ShapeDtypeStruct((BLOCK, LANES), BF16),
            jax.ShapeDtypeStruct((n * 6 * slots, LANES), BF16),
            jax.ShapeDtypeStruct((8, LANES), F32),
        ]
        + [jax.ShapeDtypeStruct((r, LANES), BF16) for r in c_rows],
        in_specs=[on_core] * 11 + [scalars, on_core, scalars, scalars],
        out_specs=[on_core] * (6 + len(c_rows)),
        scratch_shapes=[
            pltpu.VMEM((6, 4, ROWS, LANES), F32),
            pltpu.VMEM((4, ROWS, LANES), F32),
            pltpu.VMEM((4 * ROWS, LANES), F32),
        ],
        compiler_params=pltpu.CompilerParams(vmem_limit_bytes=40 * 1024 * 1024),
        name="pack",
    )(*fields, tile_lambda, tile_mu, tile_buoy, tile_dest, brick_tiles, src_index, src_wave)
    out_a, out_b, out_d, out_e, out_t, own_map = packed[:6]
    out_c = packed[6:]

    def permute(array, source_of):
        return lax.ppermute(array, "gx", [(source_of(i), i) for i in range(n)])

    starts = [PY] if merged else [-PY, PY]
    got_c = [permute(c, lambda i, o=o: (i + o) % n) for c, o in zip(out_c, starts)]
    got_d = [permute(out_d, lambda i, o=o: pair_far((i + o) % n, n)) for o in starts]
    got_e = [permute(out_e, lambda i, o=o: pair_near((i + o) % n)) for o in starts]
    got_b = permute(out_b, lambda i: pair_far(i, n))
    got_a = permute(out_a, pair_near)
    got_t = lax.all_to_all(out_t, "gx", split_axis=0, concat_axis=0, tiled=True)

    return pl.pallas_call(
        functools.partial(wave_kernel, n),
        out_shape=[
            jax.ShapeDtypeStruct(velocity.shape, F32),
            jax.ShapeDtypeStruct(stress.shape, F32),
            jax.ShapeDtypeStruct(memory.shape, F32),
        ],
        in_specs=[on_core] * 8 + [scalars, scalars] + [on_core] * (4 + 3 * len(starts)),
        out_specs=[on_core] * 3,
        scratch_shapes=[
            pltpu.VMEM((4 * ROWS, LANES), F32),
            pltpu.VMEM((n * 6 * slots, LANES), F32),
            pltpu.VMEM((16 * 32, LANES), BF16),
            pltpu.VMEM((16 * 32, LANES), F32),
        ],
        compiler_params=pltpu.CompilerParams(vmem_limit_bytes=48 * 1024 * 1024),
        name="wave",
    )(*fields, src_index, src_wave, own_map, got_a, got_b, got_t, *got_c, *got_d, *got_e)


def solution(mesh):
    split = ("groups", "gx")
    whole = P(None, split, None, None, None)
    field = P(split, None, None, None)
    return jax.shard_map(
        body,
        mesh=mesh,
        in_specs=(whole,) * 3
        + (field,) * 5
        + (P(split, None),) * 3
        + (P(split), P(split, None), P(split), P(split, None)),
        out_specs=(whole,) * 3,
        check_vma=False,
    )
```

```python
import functools

import jax
import jax.numpy as jnp
from jax import lax
from jax.experimental import pallas as pl
from jax.experimental.pallas import tpu as pltpu
from jax.sharding import PartitionSpec as P

PY = 8
TY = 8
TZ = 8
courant = 0.25

F32 = jnp.float32
BF16 = jnp.bfloat16
XX, YY, ZZ, XY, XZ, YZ = range(6)
STRESS, VEL, HELD, GAIN, LAME, MU, BUOY = 0, 6, 9, 15, 16, 17, 18
FIELDS = 19
LAST = [(STRESS + c, i) for c in (XX, XY, XZ) for i in (2, 3)] + [(STRESS + c, 3) for c in (YY, ZZ, YZ)]
LAST += [(VEL, 2), (VEL, 3), (VEL + 1, 3), (VEL + 2, 3), (BUOY, 2), (BUOY, 3)]
LAST += [(HELD + c, 3) for c in (XX, XY, XZ)] + [(GAIN, 3), (LAME, 3), (MU, 3)]
FIRST = [(STRESS + c, i) for c in range(6) for i in (0, 1)]
FIRST += [(VEL, 0), (VEL + 1, 0), (VEL + 1, 1), (VEL + 2, 0), (VEL + 2, 1), (BUOY, 0), (BUOY, 1)]
FIRST += [(HELD + c, 0) for c in range(6)] + [(GAIN, 0), (LAME, 0), (MU, 0)]
BELOW_LAST = [(STRESS + c, 3) for c in range(6) if c != ZZ] + [(VEL, 3), (VEL + 1, 3), (HELD + XY, 3), (GAIN, 3)]
BELOW_LAST = [(f, i, -1) for f, i in BELOW_LAST + [(MU, 3), (BUOY, 3), (STRESS + XY, 2)]] + [(STRESS + XY, 3, -2)]
ABOVE_LAST = [(STRESS + c, 3) for c in range(6)] + [(VEL, 3), (VEL + 2, 3), (HELD + XZ, 3), (GAIN, 3)]
ABOVE_LAST = [(f, i, 0) for f, i in ABOVE_LAST + [(MU, 3), (BUOY, 3), (STRESS + XZ, 2)]] + [(STRESS + XZ, 3, 1)]
BELOW_FIRST = [(STRESS + c, 0) for c in range(6)] + [(VEL + 1, 0), (VEL + 2, 0), (HELD + YZ, 0), (GAIN, 0)]
BELOW_FIRST = [(f, i, -1) for f, i in BELOW_FIRST + [(MU, 0), (BUOY, 0), (STRESS + YZ, 1)]] + [(STRESS + YZ, 0, -2)]
ABOVE_FIRST = [(STRESS + c, 0) for c in range(6)] + [(VEL + c, 0) for c in range(3)] + [(HELD + XX, 0), (HELD + YY, 0)]
ABOVE_FIRST += [(GAIN, 0), (LAME, 0), (MU, 0), (BUOY, 0), (STRESS + XX, 1), (STRESS + YY, 1)]
ABOVE_FIRST = [(f, i, 0) for f, i in ABOVE_FIRST] + [(STRESS + XX, 0, 1), (STRESS + YY, 0, 1)]
BELOW = BELOW_LAST + BELOW_FIRST
ABOVE = ABOVE_LAST + ABOVE_FIRST
ENDS_FIRST = [(STRESS + YY, 0, 0)] + [(f, 0, -1) for f in (STRESS + XY, STRESS + YY, STRESS + YZ, VEL + 1, BUOY)]
ENDS_LAST = [(f, 3, 0) for f in (STRESS + XX, STRESS + XY, STRESS + XZ, STRESS + YY, VEL, BUOY)]
ENDS_LAST += [(STRESS + XY, 3, -1), (STRESS + YZ, 3, -1)]
ENDS_MAP = 8
LONGEST = max(len(LAST), len(FIRST))
ROWS = 32
EXT = ROWS + 8
LANES = 128
BLOCK = FIELDS * 8 + 8
CORNER = -(-(max(len(BELOW), len(ABOVE)) + 1) // 16) * 16


def pair_near(i):
    return i ^ 1


def pair_far(i, n):
    return (i - 1) % n if i % 2 == 0 else (i + 1) % n


def is_merged(n):
    return n == 2 * PY


def sides_of(n):
    return [PY] if is_merged(n) else [-PY, PY]


def tile_offsets(n):
    return [k for o in [0] + sides_of(n) for k in (o, o + 1, o - 1)]


def tile_chunk(n):
    return -(-(9 + 7 * len(sides_of(n))) // 16) * 16


def roll(x, by, axis):
    size = x.shape[axis]
    by = by % size
    return x if by == 0 else pltpu.roll(x, by, axis)


def sublane(shape):
    return lax.broadcasted_iota(jnp.int32, shape, 0)


def lane(shape):
    return lax.broadcasted_iota(jnp.int32, shape, 1)


def place_sources(into, index, wave, step, count):
    into[...] = jnp.zeros_like(into)
    lanes = lane((1, LANES))
    for e in range(count):
        cell = index[e]
        row = lax.shift_right_logical(cell, 7)
        strength = jnp.broadcast_to(wave[step : step + 1, e : e + 1], (1, LANES))
        here = jnp.where(lanes == (cell & (LANES - 1)), strength, 0.0)
        into[pl.ds(row, 1), :] = into[pl.ds(row, 1), :] + here


def pack_kernel(n, per, *refs):
    merged = is_merged(n)
    count = 7 if merged else 8
    far_refs, outs = refs[:11], refs[11 : 11 + 5 + count - 6]
    refs = refs[11 + 5 + count - 6 :]
    out_a, out_b, out_d, out_e, out_map = outs[:5]
    out_c = outs[5:]
    near_refs, sems = refs[:11], refs[11]
    held, gain, source, corner = refs[12:]
    copies = [pltpu.make_async_copy(x, y, sems.at[k]) for k, (x, y) in enumerate(zip(far_refs, near_refs))]
    for copy in copies:
        copy.start()
    dec, los, index, wave, st, mem, vel, lam, mu, bu, tiles = near_refs
    b = lax.axis_index("gx")
    even = lax.rem(b, 2) == 0
    for copy in copies[:4]:
        copy.wait()
    place_sources(source, index, wave, 0, index.shape[0])
    for copy in copies[4:6]:
        copy.wait()
    for i in range(4):
        d = dec[0, i]
        gain[i] = courant * (1.0 - (1.0 - d) * los[0, i])
        kept = courant * d
        for c in range(6):
            value = st[c, 0, i] + kept * mem[c, 0, i]
            if c < 3:
                value = value + source[i * ROWS : (i + 1) * ROWS, :]
            held[c, i] = value
    for copy in copies[6:]:
        copy.wait()

    def get(f, i, rows=slice(None)):
        if f < VEL:
            return st[f, 0, i, rows]
        if f < HELD:
            return vel[f - VEL, 0, i, rows]
        if f < GAIN:
            return held[f - HELD, i, rows]
        if f == GAIN:
            return gain[i, rows]
        return (lam, mu, bu)[f - LAME][0, i, rows]

    sub = sublane((8, LANES))
    top, bottom = slice(0, 8), slice(ROWS - 8, ROWS)

    rows_z = LANES // TZ
    table = tiles[...]
    spots = table.shape[1]
    owner = jnp.where(table >= 0, jnp.floor((table.astype(F32) + 0.5) * (1.0 / per)) + 1.0, 0.0)
    spot = lane((8, spots))
    wide = jnp.where(spot // rows_z == sublane((8, spots)), jnp.broadcast_to(owner, (8, spots)), 0.0)
    spread = (lax.rem(sublane((spots, LANES)), rows_z) == lane((spots, LANES)) // TZ).astype(BF16)
    owners = jnp.dot(wide.astype(BF16), spread, preferred_element_type=F32) - 1.0
    out_map[...] = owners
    last = ROWS // TY - 1

    def edge_rows(f):
        if f == FIELDS:
            return jnp.broadcast_to(owners[0:1], (8, LANES)), jnp.broadcast_to(owners[last : last + 1], (8, LANES))
        lo, hi = get(f, 0, top), roll(get(f, 0, bottom), 2, 0)
        for i in range(1, 4):
            mine = sub // 2 == i
            lo = jnp.where(mine, roll(get(f, i, top), 2 * i, 0), lo)
            hi = jnp.where(mine, roll(get(f, i, bottom), 2 * i + 2, 0), hi)
        return lo, hi

    for f in range(FIELDS + 1):
        lo, hi = edge_rows(f)
        out_a[f * 8 : f * 8 + 8, :] = jnp.where(even, hi, lo)
        out_b[f * 8 : f * 8 + 8, :] = jnp.where(even, lo, hi)

    def write_corner(out, rows, strip):
        corner[...] = jnp.zeros_like(corner)
        for k, (f, i, r) in enumerate(rows):
            corner[k : k + 1, :] = get(f, i, slice(r % ROWS, r % ROWS + 1))
        corner[len(rows) : len(rows) + 1, :] = owners[strip : strip + 1]
        out[...] = corner[...].astype(BF16)

    @pl.when(even)
    def _():
        write_corner(out_e, BELOW, last)
        write_corner(out_d, ABOVE, 0)

    @pl.when(jnp.logical_not(even))
    def _():
        write_corner(out_e, ABOVE, 0)
        write_corner(out_d, BELOW, last)

    def write_layers(out, which, rest, ends):
        for k, (f, i) in enumerate(which):
            out[k * ROWS : (k + 1) * ROWS, :] = get(f, i).astype(BF16)
        if rest:
            out[len(which) * ROWS : (len(which) + rest) * ROWS, :] = jnp.zeros((rest * ROWS, LANES), BF16)
        corner[0:16, :] = jnp.zeros((16, LANES), F32)
        for k, (f, i, r) in enumerate(ends):
            corner[k : k + 1, :] = get(f, i, slice(r % ROWS, r % ROWS + 1))
        corner[ENDS_MAP : ENDS_MAP + last + 1, :] = owners[0 : last + 1]
        base = (len(which) + rest) * ROWS
        out[base : base + 16, :] = corner[0:16, :].astype(BF16)

    if merged:

        @pl.when(b < PY)
        def _():
            write_layers(out_c[0], LAST, LONGEST - len(LAST), ENDS_FIRST)

        @pl.when(b >= PY)
        def _():
            write_layers(out_c[0], FIRST, LONGEST - len(FIRST), ENDS_LAST)
    else:
        write_layers(out_c[0], LAST, 0, [])
        write_layers(out_c[1], FIRST, 0, [])


def route_kernel(n, after, t_lam, t_mu, t_bu, dest, out, near_lam, near_mu, near_bu, near_dest, rows, sems):
    pairs = ((t_lam, near_lam), (t_mu, near_mu), (t_bu, near_bu), (dest, near_dest))
    copies = [pltpu.make_async_copy(x, y, sems.at[k]) for k, (x, y) in enumerate(pairs)]
    for copy in copies:
        copy.start()
    for copy in copies:
        copy.wait()
    offsets = tile_offsets(n)
    chunk = tile_chunk(n)
    per = t_lam.shape[0]
    total = n * len(offsets)
    at = lane((1, per))
    stored = jnp.full((1, per), -1, jnp.int32)
    for t in range(per):
        stored = jnp.where(at == t, near_dest[t], stored)
    row = sublane((total, per))
    brick = lax.rem(row, n)
    for k, off in enumerate(offsets):
        brick = jnp.where(row // n == k, brick + off % n, brick)
    brick = jnp.where(brick >= n, brick - n, brick)
    route = (brick == stored).astype(BF16)
    cell, spot = sublane((2 * LANES, LANES)), lane((2 * LANES, LANES))
    half = lax.rem(spot, 64)
    cells = half // 16 * 64 + lax.rem(half, 16)
    low = jnp.logical_and(spot < 64, cell == cells).astype(BF16)
    high = jnp.logical_and(spot >= 64, cell == cells + 48).astype(BF16)
    left = lane((n, LANES)) < 64
    if chunk > 9 + 7 * len(sides_of(n)):
        rows[...] = jnp.zeros_like(rows)

    def put(j, value):
        rows[pl.ds(j, n, stride=chunk), :] = value

    for p, near in enumerate((near_lam, near_mu, near_bu)):
        tile = near[...]
        whole = jnp.dot(route, tile, preferred_element_type=F32)
        first = jnp.dot(route, jnp.dot(tile, low, preferred_element_type=F32).astype(BF16), preferred_element_type=F32)
        final = jnp.dot(route, jnp.dot(tile, high, preferred_element_type=F32).astype(BF16), preferred_element_type=F32)

        def slot(x, k):
            return x[k * n : (k + 1) * n]

        put(2 * p, slot(whole, 0)[:, :LANES])
        put(2 * p + 1, slot(whole, 0)[:, LANES:])
        put(6 + p, slot(first, 1) + slot(final, 2))
        for g in range(len(sides_of(n))):
            side = slot(whole, 3 + 3 * g)
            base = 9 + 7 * g
            if p < 2:
                put(base + p, jnp.where(left, side[:, :LANES], side[:, LANES:]))
            else:
                put(base + 2, side[:, :LANES])
                put(base + 3, side[:, LANES:])
            put(base + 4 + p, slot(first, 4 + 3 * g) + slot(final, 5 + 3 * g))
    out[...] = rows[...].astype(BF16)


def wave_kernel(n, *refs):
    merged = is_merged(n)
    (vel, st, mem, lam, mu, bu, dec, los, index, wave, maps, got_a, got_b, got_t) = refs[:14]
    refs = refs[14:]
    sides = len(sides_of(n))
    got_c, got_d, got_e = refs[:sides], refs[sides : 2 * sides], refs[2 * sides : 3 * sides]
    new_v, new_s, new_m, source, rows_t, spread_rows, tile_rows, near_rows, far_rows, end_rows = refs[3 * sides :]
    b = lax.axis_index("gx")
    even = lax.rem(b, 2) == 0
    first_x = b < PY
    chunk = tile_chunk(n)
    sub = sublane((8, LANES))

    def halo_blocks(near, far, f):
        x = near[f * 8 : f * 8 + 8, :]
        y = far[f * 8 : f * 8 + 8, :]
        return jnp.where(even, x, y), jnp.where(even, y, x)

    def halo_rows(blocks, i):
        after, before = blocks
        return jnp.where(sub < 2, roll(after, -2 * i, 0), roll(before, 6 - 2 * i, 0))

    rows_t[...] = got_t[...].astype(F32)
    col = lane((16, LANES))
    line = sublane((16, LANES))
    on_line = col // TZ == line
    spread = (lax.rem(sublane((LANES, LANES)), TZ) == lax.rem(lane((LANES, LANES)), TZ)).astype(BF16)

    def overlay(row, halves, wanted):
        def take(first, values):
            for s in range(16):
                for h in range(halves):
                    value = rows_t[pl.ds((first + s) * chunk + row + h, 1), :]
                    value = jnp.where(on_line, jnp.broadcast_to(value, (16, LANES)), 0.0)
                    at = (s * halves + h) * 16
                    spread_rows[at : at + 16, :] = value.astype(BF16)
            size = 16 * halves * 16
            tile_rows[0:size, :] = jnp.dot(spread_rows[0:size, :], spread, preferred_element_type=F32)
            done = []
            for value, (_, owner, at) in zip(values, wanted):
                for s in range(16):
                    here = tile_rows[s * halves * 16 + at : s * halves * 16 + at + 8, :]
                    value = jnp.where(owner == (first + s) * 1.0, here, value)
                done.append(value)
            return done

        values = [w[0] for w in wanted]
        if n == 16:
            return take(0, values)
        return lax.fori_loop(0, n // 16, lambda g, v: take(g * 16, v), values)

    column = {}
    rows_y = ROWS // TY

    def own(f, i):
        if f < VEL:
            return st[f, 0, i]
        if f < HELD:
            return vel[f - VEL, 0, i]
        if f < GAIN:
            value = st[f - HELD, 0, i] + courant * dec[0, i] * mem[f - HELD, 0, i]
            if f < HELD + 3:
                value = value + source[i * ROWS : (i + 1) * ROWS, :]
            return value
        if f == GAIN:
            return courant * (1.0 - (1.0 - dec[0, i]) * los[0, i])
        return (lam, mu, bu)[f - LAME][0, i]

    def main_tiles(mains, owners, row, halves, line_of):
        wanted = []
        for i, m in mains.items():
            for p in range(rows_y):
                owner = jnp.broadcast_to(owners[p : p + 1], (8, LANES))
                wanted.append((m[p * 8 : (p + 1) * 8], owner, line_of(i)))
        laid = overlay(row, halves, wanted)
        return {i: jnp.concatenate(laid[k * rows_y : (k + 1) * rows_y], 0) for k, i in enumerate(mains)}

    def halo_tiles(halos, after, before, row):
        zeros = jnp.zeros((8, LANES), F32)
        blocks = overlay(row, 1, [(zeros, after, 0), (zeros, before, 8)])
        covered = jnp.where(sub < 4, after, before) >= 0.0
        return {i: jnp.where(covered, halo_rows(blocks, i), h) for i, h in halos.items()}

    place_sources(source, index, wave, 0, index.shape[0])
    after, before = halo_blocks(got_a, got_b, FIELDS)
    for f in range(FIELDS):
        blocks = halo_blocks(got_a, got_b, f)
        main = {i: own(f, i) for i in range(4)}
        halo = {i: halo_rows(blocks, i) for i in range(4)}
        if f >= LAME:
            p = f - LAME
            main = main_tiles(main, maps[...], 2 * p, 2, lambda i: i * 8)
            halo = halo_tiles(halo, after, before, 6 + p)
        for i in range(4):
            column["own", f, i] = jnp.concatenate([main[i], halo[i]], 0)

    def corner_rows(table, rows, f, i, far_edge):
        value = None
        for k, (g, j, r) in enumerate(rows):
            if (g, j) == (f, i):
                row = jnp.broadcast_to(table[k : k + 1, :], (8, LANES))
                value = jnp.where(sub == (r % 8), row, 0.0 if value is None else value)
        return value

    for side, (name, which) in enumerate((("before", LAST), ("after", FIRST))):
        group = 0 if merged else side
        message = got_c[group]
        base = (LONGEST if merged else len(which)) * ROWS
        if merged:
            whole = first_x if name == "after" else jnp.logical_not(first_x)
        if group == side:
            near, far = got_e[group][...].astype(F32), got_d[group][...].astype(F32)
            near_rows[...] = jnp.where(even, near, far)
            far_rows[...] = jnp.where(even, far, near)
            end_rows[...] = message[base : base + 16, :].astype(F32)
        ends = ENDS_LAST if name == "before" else ENDS_FIRST
        after = jnp.broadcast_to(near_rows[len(ABOVE) : len(ABOVE) + 1, :], (8, LANES))
        before = jnp.broadcast_to(far_rows[len(BELOW) : len(BELOW) + 1, :], (8, LANES))
        owners = end_rows[ENDS_MAP : ENDS_MAP + 8, :]
        row = 9 + 7 * group
        mains, halos = {}, {}
        for k, (f, i) in enumerate(which):
            main = message[k * ROWS : (k + 1) * ROWS, :].astype(F32)
            if merged:
                only = [jnp.zeros((8, LANES), F32) for _ in range(rows_y)]
                for e, (g, j, r) in enumerate(ends):
                    if (g, j) == (f, i):
                        at = r % ROWS
                        line_rows = jnp.broadcast_to(end_rows[e : e + 1, :], (8, LANES))
                        only[at // 8] = jnp.where(sub == at % 8, line_rows, only[at // 8])
                main = jnp.where(whole, main, jnp.concatenate(only, 0))
            mains[f, i] = main
            above = corner_rows(near_rows, ABOVE, f, i, False)
            below = corner_rows(far_rows, BELOW, f, i, True)
            if above is None and below is None:
                halos[f, i] = jnp.zeros((8, LANES), F32)
            elif above is None or below is None:
                halos[f, i] = below if above is None else above
            else:
                halos[f, i] = jnp.where(sub < 4, above, below)
        for f in range(FIELDS):
            layers = sorted(i for g, i in which if g == f)
            main = {i: mains[f, i] for i in layers}
            halo = {i: halos[f, i] for i in layers}
            if f == BUOY:
                main = main_tiles(main, owners, row + 2, 2, lambda i: i * 8)
            elif f >= LAME:
                main = main_tiles(main, owners, row + f - LAME, 1, lambda i: 8 if i else 0)
            if f >= LAME:
                halo = halo_tiles(halo, after, before, row + 4 + f - LAME)
            for i in layers:
                column[name, f, i] = jnp.concatenate([main[i], halo[i]], 0)

    def layers_of(f):
        names = [("before", 2), ("before", 3)] + [("own", i) for i in range(4)] + [("after", 0), ("after", 1)]
        return [column.get((name, f, i)) for name, i in names]

    s0 = [layers_of(STRESS + c) for c in range(6)]
    v0 = [layers_of(VEL + c) for c in range(3)]
    held = [layers_of(HELD + c) for c in range(6)]
    gain, lame, shear, buoy = (layers_of(f) for f in (GAIN, LAME, MU, BUOY))

    tall = sublane((EXT, LANES))
    wide = lane((EXT, LANES))

    def linked(test):
        def of(step):
            q = lax.rem(b + step + n, n)
            return jnp.where(test(q), 1, 0)

        flags = jnp.where(tall < ROWS, of(0), jnp.where(tall < ROWS + 4, of(1), of(-1)))
        return flags == 1

    link_before = linked(lambda q: q >= PY)
    link_after = linked(lambda q: q < n - PY)

    def x_next(a, l):
        if l == 1:
            return jnp.where(link_before, a[2], 0.0)
        if l == 5:
            return jnp.where(link_after, a[6], 0.0)
        return a[l + 1]

    def x_prev(a, l):
        if l == 2:
            return jnp.where(link_before, a[1], 0.0)
        if l == 6:
            return jnp.where(link_after, a[5], 0.0)
        return a[l - 1]

    def y_next(a):
        return roll(a, -1, 0)

    def y_prev(a):
        return roll(a, 1, 0)

    def z_next(a):
        return jnp.where(wide == LANES - 1, 0.0, roll(a, -1, 1))

    def z_prev(a):
        return jnp.where(wide == 0, 0.0, roll(a, 1, 1))

    def move(v, s, spans):
        new = [[None] * 8 for _ in range(3)]
        for l in spans[0]:
            grad = (x_next(s[XX], l) - s[XX][l]) + (s[XY][l] - y_prev(s[XY][l])) + (s[XZ][l] - z_prev(s[XZ][l]))
            new[0][l] = v[0][l] + courant * buoy[l] * grad
        for l in spans[1]:
            grad = (s[XY][l] - x_prev(s[XY], l)) + (y_next(s[YY][l]) - s[YY][l]) + (s[YZ][l] - z_prev(s[YZ][l]))
            new[1][l] = v[1][l] + courant * buoy[l] * grad
            grad = (s[XZ][l] - x_prev(s[XZ], l)) + (s[YZ][l] - y_prev(s[YZ][l])) + (z_next(s[ZZ][l]) - s[ZZ][l])
            new[2][l] = v[2][l] + courant * buoy[l] * grad
        return new

    def rates_at(v, l, wanted):
        out = [None] * 6
        ex = v[0][l] - x_prev(v[0], l)
        ey = v[1][l] - y_prev(v[1][l])
        ez = v[2][l] - z_prev(v[2][l])
        spread_part = lame[l] * (ex + ey + ez)
        twice = 2.0 * shear[l]
        for c, e in ((XX, ex), (YY, ey), (ZZ, ez)):
            if c in wanted:
                out[c] = spread_part + twice * e
        if XY in wanted:
            out[XY] = shear[l] * ((y_next(v[0][l]) - v[0][l]) + (x_next(v[1], l) - v[1][l]))
        if XZ in wanted:
            out[XZ] = shear[l] * ((z_next(v[0][l]) - v[0][l]) + (x_next(v[2], l) - v[2][l]))
        if YZ in wanted:
            out[YZ] = shear[l] * ((z_next(v[1][l]) - v[1][l]) + (y_next(v[2][l]) - v[2][l]))
        return out

    v1 = move(v0, s0, (range(0, 7), range(1, 8)))
    s1 = [[None] * 8 for _ in range(6)]
    m1 = {}
    for l in range(1, 7):
        wanted = (XX, XY, XZ) if l == 1 else range(6)
        rates = rates_at(v1, l, wanted)
        for c in wanted:
            s1[c][l] = held[c][l] + gain[l] * rates[c]
            if 2 <= l < 6:
                d = dec[0, l - 2]
                m1[c, l] = d * mem[c, 0, l - 2] - (1.0 - d) * los[0, l - 2] * rates[c][:ROWS]
    v2 = move(v1, s1, (range(1, 6), range(2, 7)))
    place_sources(source, index, wave, 1, index.shape[0])
    for l in range(2, 6):
        i = l - 2
        rates = rates_at(v2, l, range(6))
        d = dec[0, i]
        lost = (1.0 - d) * los[0, i]
        for c in range(3):
            new_v[c, 0, i] = v2[c][l][:ROWS]
        for c in range(6):
            rate = rates[c][:ROWS]
            m2 = d * m1[c, l] - lost * rate
            new_m[c, 0, i] = m2
            value = s1[c][l][:ROWS] + courant * (rate + m2)
            if c < 3:
                value = value + source[i * ROWS : (i + 1) * ROWS, :]
            new_s[c, 0, i] = value


def body(
    velocity,
    stress,
    memory,
    lame_lambda,
    lame_mu,
    buoyancy,
    decay,
    loss,
    tile_lambda,
    tile_mu,
    tile_buoy,
    tile_dest,
    brick_tiles,
    src_index,
    src_wave,
):
    n = lax.axis_size("gx")
    merged = is_merged(n)
    sides = sides_of(n)
    on_core = pl.BlockSpec(memory_space=pltpu.VMEM)
    scalars = pl.BlockSpec(memory_space=pltpu.SMEM)
    away = pl.BlockSpec(memory_space=pltpu.HBM)
    waves = src_wave.T
    fields = (velocity, stress, memory, lame_lambda, lame_mu, buoyancy, decay, loss)
    if merged:
        c_rows = [LONGEST * ROWS + 16]
    else:
        c_rows = [len(LAST) * ROWS + 16, len(FIRST) * ROWS + 16]
    inputs = (decay, loss, src_index, waves, stress, memory, velocity, lame_lambda, lame_mu, buoyancy, brick_tiles)
    packed = pl.pallas_call(
        functools.partial(pack_kernel, n, tile_lambda.shape[0]),
        out_shape=[
            jax.ShapeDtypeStruct((BLOCK, LANES), F32),
            jax.ShapeDtypeStruct((BLOCK, LANES), F32),
            jax.ShapeDtypeStruct((CORNER, LANES), BF16),
            jax.ShapeDtypeStruct((CORNER, LANES), BF16),
            jax.ShapeDtypeStruct((8, LANES), F32),
        ]
        + [jax.ShapeDtypeStruct((r, LANES), BF16) for r in c_rows],
        in_specs=[away] * len(inputs),
        out_specs=[on_core] * (5 + len(c_rows)),
        scratch_shapes=[
            pltpu.SMEM(x.shape, x.dtype) if x is src_index else pltpu.VMEM(x.shape, x.dtype) for x in inputs
        ]
        + [
            pltpu.SemaphoreType.DMA((len(inputs),)),
            pltpu.VMEM((6, 4, ROWS, LANES), F32),
            pltpu.VMEM((4, ROWS, LANES), F32),
            pltpu.VMEM((4 * ROWS, LANES), F32),
            pltpu.VMEM((CORNER, LANES), F32),
        ],
        compiler_params=pltpu.CompilerParams(vmem_limit_bytes=56 * 1024 * 1024),
        name="pack",
    )(*inputs)
    out_a, out_b, out_d, out_e, own_map = packed[:5]
    out_c = packed[5:]
    chunk = tile_chunk(n)
    tiles = (tile_lambda, tile_mu, tile_buoy)
    out_t = pl.pallas_call(
        functools.partial(route_kernel, n),
        out_shape=jax.ShapeDtypeStruct((n * chunk, LANES), BF16),
        in_specs=[pl.BlockSpec(memory_space=pl.ANY)] + [away] * 4,
        out_specs=on_core,
        scratch_shapes=[pltpu.VMEM(x.shape, x.dtype) for x in tiles]
        + [
            pltpu.SMEM(tile_dest.shape, tile_dest.dtype),
            pltpu.VMEM((n * chunk, LANES), F32),
            pltpu.SemaphoreType.DMA((4,)),
        ],
        compiler_params=pltpu.CompilerParams(vmem_limit_bytes=40 * 1024 * 1024),
        name="route",
    )(own_map, *tiles, tile_dest)

    def permute(array, source_of):
        return lax.ppermute(array, "gx", [(source_of(i), i) for i in range(n)])

    got_c = [permute(c, lambda i, o=o: (i + o) % n) for c, o in zip(out_c, sides)]
    got_d = [permute(out_d, lambda i, o=o: pair_far((i + o) % n, n)) for o in sides]
    got_e = [permute(out_e, lambda i, o=o: pair_near((i + o) % n)) for o in sides]
    got_b = permute(out_b, lambda i: pair_far(i, n))
    got_a = permute(out_a, pair_near)
    got_t = lax.all_to_all(out_t, "gx", split_axis=0, concat_axis=0, tiled=True)

    return pl.pallas_call(
        functools.partial(wave_kernel, n),
        out_shape=[
            jax.ShapeDtypeStruct(velocity.shape, F32),
            jax.ShapeDtypeStruct(stress.shape, F32),
            jax.ShapeDtypeStruct(memory.shape, F32),
        ],
        in_specs=[on_core] * 8 + [scalars] + [on_core] * (5 + 3 * len(sides)),
        out_specs=[on_core] * 3,
        scratch_shapes=[
            pltpu.VMEM((4 * ROWS, LANES), F32),
            pltpu.VMEM((n * chunk, LANES), F32),
            pltpu.VMEM((16 * 32, LANES), BF16),
            pltpu.VMEM((16 * 32, LANES), F32),
            pltpu.VMEM((CORNER, LANES), F32),
            pltpu.VMEM((CORNER, LANES), F32),
            pltpu.VMEM((16, LANES), F32),
        ],
        compiler_params=pltpu.CompilerParams(vmem_limit_bytes=48 * 1024 * 1024),
        name="wave",
    )(*fields, src_index, waves, own_map, got_a, got_b, got_t, *got_c, *got_d, *got_e)


def solution(mesh):
    split = ("groups", "gx")
    whole = P(None, split, None, None, None)
    field = P(split, None, None, None)
    return jax.shard_map(
        body,
        mesh=mesh,
        in_specs=(whole,) * 3
        + (field,) * 5
        + (P(split, None),) * 3
        + (P(split), P(split, None), P(split), P(split, None)),
        out_specs=(whole,) * 3,
        check_vma=False,
    )
```

```python
import functools

import jax
import jax.numpy as jnp
from jax import lax
from jax.experimental import pallas as pl
from jax.experimental.pallas import tpu as pltpu
from jax.sharding import PartitionSpec as P

PY = 8
TY = 8
TZ = 8
courant = 0.25

F32 = jnp.float32
BF16 = jnp.bfloat16
XX, YY, ZZ, XY, XZ, YZ = range(6)
STRESS, VEL, HELD, GAIN, LAME, MU, BUOY = 0, 6, 9, 15, 16, 17, 18
FIELDS = 19
LAST = [("gx", 2), ("gx", 3), ("gy", 3), ("gz", 3), (STRESS + XY, 3), (STRESS + XZ, 3)]
LAST += [(VEL, 2), (VEL, 3), (VEL + 1, 3), (VEL + 2, 3), (BUOY, 2), (BUOY, 3)]
LAST += [(HELD + c, 3) for c in (XX, XY, XZ)] + [(GAIN, 3), (LAME, 3), (MU, 3)]
FIRST = [("gx", 0), ("gy", 0), ("gz", 0), ("gy", 1), ("gz", 1), (STRESS + XX, 0)]
FIRST += [(VEL, 0), (VEL + 1, 0), (VEL + 1, 1), (VEL + 2, 0), (VEL + 2, 1), (BUOY, 0), (BUOY, 1)]
FIRST += [(HELD + XX, 0), ("hy", 0), ("hz", 0), (GAIN, 0), (LAME, 0), (MU, 0)]
BELOW_LAST = [(STRESS + c, 3) for c in range(6) if c != ZZ] + [(VEL, 3), (VEL + 1, 3), (HELD + XY, 3), (GAIN, 3)]
BELOW_LAST = [(f, i, -1) for f, i in BELOW_LAST + [(MU, 3), (BUOY, 3), (STRESS + XY, 2)]] + [(STRESS + XY, 3, -2)]
ABOVE_LAST = [(STRESS + c, 3) for c in range(6)] + [(VEL, 3), (VEL + 2, 3), (HELD + XZ, 3), (GAIN, 3)]
ABOVE_LAST = [(f, i, 0) for f, i in ABOVE_LAST + [(MU, 3), (BUOY, 3), (STRESS + XZ, 2)]] + [(STRESS + XZ, 3, 1)]
BELOW_FIRST = [(STRESS + c, 0) for c in range(6)] + [(VEL + 1, 0), (VEL + 2, 0), (HELD + YZ, 0), (GAIN, 0)]
BELOW_FIRST = [(f, i, -1) for f, i in BELOW_FIRST + [(MU, 0), (BUOY, 0), (STRESS + YZ, 1)]] + [(STRESS + YZ, 0, -2)]
ABOVE_FIRST = [(STRESS + c, 0) for c in range(6)] + [(VEL + c, 0) for c in range(3)] + [(HELD + XX, 0), (HELD + YY, 0)]
ABOVE_FIRST += [(GAIN, 0), (LAME, 0), (MU, 0), (BUOY, 0), (STRESS + XX, 1), (STRESS + YY, 1)]
ABOVE_FIRST = [(f, i, 0) for f, i in ABOVE_FIRST] + [(STRESS + XX, 0, 1), (STRESS + YY, 0, 1)]
BELOW = BELOW_LAST + BELOW_FIRST
ABOVE = ABOVE_LAST + ABOVE_FIRST
ENDS = [(STRESS + YY, 0, 0), (STRESS + XY, 0, -1), (STRESS + YZ, 0, -1)]
ENDS += [("gy", 0, -1), (VEL + 1, 0, -1), (BUOY, 0, -1)]
ENDS += [(STRESS + YY, 3, 0), (STRESS + XY, 3, -1), (STRESS + YZ, 3, -1)]
ENDS += [("gx", 3, 0), (VEL, 3, 0), (BUOY, 3, 0)]
ENDS_MAP = 12
LONGEST = max(len(LAST), len(FIRST))
ROWS = 32
EXT = ROWS + 8
LANES = 128
BLOCK = FIELDS * 8 + 8
CORNER = -(-(max(len(BELOW), len(ABOVE)) + 1) // 16) * 16


def pair_near(i):
    return i ^ 1


def pair_far(i, n):
    return (i - 1) % n if i % 2 == 0 else (i + 1) % n


def is_merged(n):
    return n == 2 * PY


def sides_of(n):
    return [PY] if is_merged(n) else [-PY, PY]


def tile_offsets(n):
    return [k for o in [0] + sides_of(n) for k in (o, o + 1, o - 1)]


def tile_chunk(n):
    return -(-(9 + 7 * len(sides_of(n))) // 16) * 16


def roll(x, by, axis):
    size = x.shape[axis]
    by = by % size
    return x if by == 0 else pltpu.roll(x, by, axis)


def sublane(shape):
    return lax.broadcasted_iota(jnp.int32, shape, 0)


def lane(shape):
    return lax.broadcasted_iota(jnp.int32, shape, 1)


def z_after(a):
    return jnp.where(lane(a.shape) == LANES - 1, 0.0, roll(a, -1, 1))


def z_before(a):
    return jnp.where(lane(a.shape) == 0, 0.0, roll(a, 1, 1))


def place_sources(into, index, wave, step, count):
    into[...] = jnp.zeros_like(into)
    lanes = lane((1, LANES))
    for e in range(count):
        cell = index[e]
        row = lax.shift_right_logical(cell, 7)
        strength = jnp.broadcast_to(wave[step : step + 1, e : e + 1], (1, LANES))
        here = jnp.where(lanes == (cell & (LANES - 1)), strength, 0.0)
        into[pl.ds(row, 1), :] = into[pl.ds(row, 1), :] + here


def pack_kernel(n, per, *refs):
    merged = is_merged(n)
    count = 6 + len(sides_of(n))
    far_refs, outs = refs[:15], refs[15 : 15 + count]
    refs = refs[15 + count :]
    out_a, out_b, out_d, out_e, out_map, out_t = outs[:6]
    out_c = outs[6:]
    near_refs, sems = refs[:15], refs[15]
    held, gain, source, corner, routed = refs[16:]
    copies = [pltpu.make_async_copy(x, y, sems.at[k]) for k, (x, y) in enumerate(zip(far_refs, near_refs))]
    for copy in copies:
        copy.start()
    near_lam, near_mu, near_bu, near_dest, dec, los, index, wave, st, mem, vel, lam, mu, bu, tiles = near_refs
    b = lax.axis_index("gx")
    even = lax.rem(b, 2) == 0
    for copy in copies[:4]:
        copy.wait()
    route_tiles(n, near_lam, near_mu, near_bu, near_dest, routed, out_t)
    for copy in copies[4:8]:
        copy.wait()
    place_sources(source, index, wave, 0, index.shape[0])
    for copy in copies[8:10]:
        copy.wait()
    for i in range(4):
        d = dec[0, i]
        gain[i] = courant * (1.0 - (1.0 - d) * los[0, i])
        kept = courant * d
        for c in range(6):
            value = st[c, 0, i] + kept * mem[c, 0, i]
            if c < 3:
                value = value + source[i * ROWS : (i + 1) * ROWS, :]
            held[c, i] = value
    for copy in copies[10:]:
        copy.wait()

    def get(f, i, rows=slice(None)):
        if f < VEL:
            return st[f, 0, i, rows]
        if f < HELD:
            return vel[f - VEL, 0, i, rows]
        if f < GAIN:
            return held[f - HELD, i, rows]
        if f == GAIN:
            return gain[i, rows]
        return (lam, mu, bu)[f - LAME][0, i, rows]

    sub = sublane((8, LANES))
    top, bottom = slice(0, 8), slice(ROWS - 8, ROWS)

    rows_z = LANES // TZ
    table = tiles[...]
    spots = table.shape[1]
    owner = jnp.where(table >= 0, jnp.floor((table.astype(F32) + 0.5) * (1.0 / per)) + 1.0, 0.0)
    spot = lane((8, spots))
    wide = jnp.where(spot // rows_z == sublane((8, spots)), jnp.broadcast_to(owner, (8, spots)), 0.0)
    spread = (lax.rem(sublane((spots, LANES)), rows_z) == lane((spots, LANES)) // TZ).astype(BF16)
    owners = jnp.dot(wide.astype(BF16), spread, preferred_element_type=F32) - 1.0
    out_map[...] = owners
    last = ROWS // TY - 1

    def prev_y(a):
        return jnp.where(sublane(a.shape) == 0, 0.0, roll(a, 1, 0))

    def next_y(a):
        return jnp.where(sublane(a.shape) == ROWS - 1, 0.0, roll(a, -1, 0))

    def sums(kind, i):
        def s(c, k):
            return held[c, k] if kind[0] == "h" else st[c, 0, k]

        def dy_prev(c):
            return s(c, i) - prev_y(s(c, i))

        def dy_next(c):
            return next_y(s(c, i)) - s(c, i)

        def dz_prev(c):
            return s(c, i) - z_before(s(c, i))

        def dz_next(c):
            return z_after(s(c, i)) - s(c, i)

        if kind == "gx":
            along = s(XX, i + 1) - s(XX, i) if i < 3 else -s(XX, i)
            return along + dy_prev(XY) + dz_prev(XZ)
        cross = XY if kind[1] == "y" else XZ
        along = s(cross, i) - s(cross, i - 1) if i > 0 else s(cross, i)
        if kind[1] == "y":
            return along + dy_next(YY) + dz_prev(YZ)
        return along + dy_prev(YZ) + dz_next(ZZ)

    def entry(f, i):
        return sums(f, i) if isinstance(f, str) else get(f, i)

    def edge_rows(f):
        if f == FIELDS:
            return jnp.broadcast_to(owners[0:1], (8, LANES)), jnp.broadcast_to(owners[last : last + 1], (8, LANES))
        lo, hi = get(f, 0, top), roll(get(f, 0, bottom), 2, 0)
        for i in range(1, 4):
            mine = sub // 2 == i
            lo = jnp.where(mine, roll(get(f, i, top), 2 * i, 0), lo)
            hi = jnp.where(mine, roll(get(f, i, bottom), 2 * i + 2, 0), hi)
        return lo, hi

    for f in range(FIELDS + 1):
        lo, hi = edge_rows(f)
        out_a[f * 8 : f * 8 + 8, :] = jnp.where(even, hi, lo)
        out_b[f * 8 : f * 8 + 8, :] = jnp.where(even, lo, hi)

    def write_corner(out, rows, strip):
        corner[...] = jnp.zeros_like(corner)
        for k, (f, i, r) in enumerate(rows):
            corner[k : k + 1, :] = get(f, i, slice(r % ROWS, r % ROWS + 1))
        corner[len(rows) : len(rows) + 1, :] = owners[strip : strip + 1]
        out[...] = corner[...].astype(BF16)

    @pl.when(even)
    def _():
        write_corner(out_e, BELOW, last)
        write_corner(out_d, ABOVE, 0)

    @pl.when(jnp.logical_not(even))
    def _():
        write_corner(out_e, ABOVE, 0)
        write_corner(out_d, BELOW, last)

    def write_layers(out, which, rest):
        for k, (f, i) in enumerate(which):
            out[k * ROWS : (k + 1) * ROWS, :] = entry(f, i).astype(BF16)
        if rest:
            out[len(which) * ROWS : (len(which) + rest) * ROWS, :] = jnp.zeros((rest * ROWS, LANES), BF16)
        base = (len(which) + rest) * ROWS
        out[base : base + 16, :] = corner[0:16, :].astype(BF16)

    for k, (f, i, r) in enumerate(ENDS):
        row = slice(r % ROWS, r % ROWS + 1)
        corner[k : k + 1, :] = sums(f, i)[row] if isinstance(f, str) else get(f, i, row)
    corner[ENDS_MAP : ENDS_MAP + last + 1, :] = owners[0 : last + 1]
    if merged:

        @pl.when(b < PY)
        def _():
            write_layers(out_c[0], LAST, LONGEST - len(LAST))

        @pl.when(b >= PY)
        def _():
            write_layers(out_c[0], FIRST, LONGEST - len(FIRST))
    else:
        write_layers(out_c[0], LAST, 0)
        write_layers(out_c[1], FIRST, 0)


def route_tiles(n, near_lam, near_mu, near_bu, near_dest, rows, out):
    offsets = tile_offsets(n)
    chunk = tile_chunk(n)
    per = near_lam.shape[0]
    total = n * len(offsets)
    at = lane((1, per))
    stored = jnp.full((1, per), -1, jnp.int32)
    for t in range(per):
        stored = jnp.where(at == t, near_dest[t], stored)
    row = sublane((total, per))
    brick = lax.rem(row, n)
    for k, off in enumerate(offsets):
        brick = jnp.where(row // n == k, brick + off % n, brick)
    brick = jnp.where(brick >= n, brick - n, brick)
    route = (brick == stored).astype(BF16)
    cell, spot = sublane((2 * LANES, LANES)), lane((2 * LANES, LANES))
    half = lax.rem(spot, 64)
    cells = half // 16 * 64 + lax.rem(half, 16)
    low = jnp.logical_and(spot < 64, cell == cells).astype(BF16)
    high = jnp.logical_and(spot >= 64, cell == cells + 48).astype(BF16)
    left = lane((n, LANES)) < 64
    if chunk > 9 + 7 * len(sides_of(n)):
        rows[...] = jnp.zeros_like(rows)

    def put(j, value):
        rows[pl.ds(j, n, stride=chunk), :] = value

    for p, near in enumerate((near_lam, near_mu, near_bu)):
        tile = near[...]
        whole = jnp.dot(route, tile, preferred_element_type=F32)
        first = jnp.dot(route, jnp.dot(tile, low, preferred_element_type=F32).astype(BF16), preferred_element_type=F32)
        final = jnp.dot(route, jnp.dot(tile, high, preferred_element_type=F32).astype(BF16), preferred_element_type=F32)

        def slot(x, k):
            return x[k * n : (k + 1) * n]

        put(2 * p, slot(whole, 0)[:, :LANES])
        put(2 * p + 1, slot(whole, 0)[:, LANES:])
        put(6 + p, slot(first, 1) + slot(final, 2))
        for g in range(len(sides_of(n))):
            side = slot(whole, 3 + 3 * g)
            base = 9 + 7 * g
            if p < 2:
                put(base + p, jnp.where(left, side[:, :LANES], side[:, LANES:]))
            else:
                put(base + 2, side[:, :LANES])
                put(base + 3, side[:, LANES:])
            put(base + 4 + p, slot(first, 4 + 3 * g) + slot(final, 5 + 3 * g))
    out[...] = rows[...].astype(BF16)


def wave_kernel(n, *refs):
    merged = is_merged(n)
    (vel, st, mem, lam, mu, bu, dec, los, index, wave, maps, got_a, got_b, got_t) = refs[:14]
    refs = refs[14:]
    sides = len(sides_of(n))
    got_c, got_d, got_e = refs[:sides], refs[sides : 2 * sides], refs[2 * sides : 3 * sides]
    new_v, new_s, new_m, source, rows_t, spread_rows, tile_rows, near_rows, far_rows, end_rows = refs[3 * sides :]
    b = lax.axis_index("gx")
    even = lax.rem(b, 2) == 0
    first_x = b < PY
    chunk = tile_chunk(n)
    sub = sublane((8, LANES))

    def halo_blocks(near, far, f):
        x = near[f * 8 : f * 8 + 8, :]
        y = far[f * 8 : f * 8 + 8, :]
        return jnp.where(even, x, y), jnp.where(even, y, x)

    def halo_rows(blocks, i):
        after, before = blocks
        return jnp.where(sub < 2, roll(after, -2 * i, 0), roll(before, 6 - 2 * i, 0))

    rows_t[...] = got_t[...].astype(F32)
    col = lane((16, LANES))
    line = sublane((16, LANES))
    on_line = col // TZ == line
    spread = (lax.rem(sublane((LANES, LANES)), TZ) == lax.rem(lane((LANES, LANES)), TZ)).astype(BF16)

    def overlay(row, halves, wanted):
        def take(first, values):
            for s in range(16):
                for h in range(halves):
                    value = rows_t[pl.ds((first + s) * chunk + row + h, 1), :]
                    value = jnp.where(on_line, jnp.broadcast_to(value, (16, LANES)), 0.0)
                    at = (s * halves + h) * 16
                    spread_rows[at : at + 16, :] = value.astype(BF16)
            size = 16 * halves * 16
            tile_rows[0:size, :] = jnp.dot(spread_rows[0:size, :], spread, preferred_element_type=F32)
            done = []
            for value, (_, owner, at) in zip(values, wanted):
                for s in range(16):
                    here = tile_rows[s * halves * 16 + at : s * halves * 16 + at + 8, :]
                    value = jnp.where(owner == (first + s) * 1.0, here, value)
                done.append(value)
            return done

        values = [w[0] for w in wanted]
        if n == 16:
            return take(0, values)
        return lax.fori_loop(0, n // 16, lambda g, v: take(g * 16, v), values)

    column = {}
    rows_y = ROWS // TY

    def own(f, i):
        if f < VEL:
            return st[f, 0, i]
        if f < HELD:
            return vel[f - VEL, 0, i]
        if f < GAIN:
            value = st[f - HELD, 0, i] + courant * dec[0, i] * mem[f - HELD, 0, i]
            if f < HELD + 3:
                value = value + source[i * ROWS : (i + 1) * ROWS, :]
            return value
        if f == GAIN:
            return courant * (1.0 - (1.0 - dec[0, i]) * los[0, i])
        return (lam, mu, bu)[f - LAME][0, i]

    def main_tiles(mains, owners, row, halves, line_of):
        wanted = []
        for i, m in mains.items():
            for p in range(rows_y):
                owner = jnp.broadcast_to(owners[p : p + 1], (8, LANES))
                wanted.append((m[p * 8 : (p + 1) * 8], owner, line_of(i)))
        laid = overlay(row, halves, wanted)
        return {i: jnp.concatenate(laid[k * rows_y : (k + 1) * rows_y], 0) for k, i in enumerate(mains)}

    def halo_tiles(halos, after, before, row):
        zeros = jnp.zeros((8, LANES), F32)
        blocks = overlay(row, 1, [(zeros, after, 0), (zeros, before, 8)])
        covered = jnp.where(sub < 4, after, before) >= 0.0
        return {i: jnp.where(covered, halo_rows(blocks, i), h) for i, h in halos.items()}

    place_sources(source, index, wave, 0, index.shape[0])
    after, before = halo_blocks(got_a, got_b, FIELDS)
    for f in range(FIELDS):
        blocks = halo_blocks(got_a, got_b, f)
        main = {i: own(f, i) for i in range(4)}
        halo = {i: halo_rows(blocks, i) for i in range(4)}
        if f >= LAME:
            p = f - LAME
            main = main_tiles(main, maps[...], 2 * p, 2, lambda i: i * 8)
            halo = halo_tiles(halo, after, before, 6 + p)
        for i in range(4):
            column["own", f, i] = jnp.concatenate([main[i], halo[i]], 0)

    def corner_rows(table, rows, f, i):
        value = None
        for k, (g, j, r) in enumerate(rows):
            if (g, j) == (f, i):
                row = jnp.broadcast_to(table[k : k + 1, :], (8, LANES))
                value = jnp.where(sub == (r % 8), row, 0.0 if value is None else value)
        return value

    no_rows, no_halo = jnp.zeros((ROWS, LANES), F32), jnp.zeros((8, LANES), F32)
    face = {}
    for side, (name, which) in enumerate((("before", LAST), ("after", FIRST))):
        group = 0 if merged else side
        message = got_c[group]
        base = (LONGEST if merged else len(which)) * ROWS
        if merged:
            whole = first_x if name == "after" else jnp.logical_not(first_x)
        if group == side:
            near, far = got_e[group][...].astype(F32), got_d[group][...].astype(F32)
            near_rows[...] = jnp.where(even, near, far)
            far_rows[...] = jnp.where(even, far, near)
            end_rows[...] = message[base : base + 16, :].astype(F32)
        after = jnp.broadcast_to(near_rows[len(ABOVE) : len(ABOVE) + 1, :], (8, LANES))
        before = jnp.broadcast_to(far_rows[len(BELOW) : len(BELOW) + 1, :], (8, LANES))
        owners = end_rows[8:16, :][ENDS_MAP - 8 :]
        row = 9 + 7 * group

        def end_row(f, i, r):
            at = ENDS.index((f, i, r))
            return jnp.broadcast_to(end_rows[at : at + 1, :], (8, LANES))

        def main_rows(f, i):
            if (f, i) not in which:
                return no_rows
            k = which.index((f, i))
            main = message[k * ROWS : (k + 1) * ROWS, :].astype(F32)
            if not merged:
                return main
            only = [no_halo] * rows_y
            if (f, i, 0) in ENDS[3:6] + ENDS[9:12]:
                only[0] = jnp.where(sub == 0, end_row(f, i, 0), 0.0)
            if (f, i, -1) in ENDS[3:6] + ENDS[9:12]:
                only[-1] = jnp.where(sub == 7, end_row(f, i, -1), 0.0)
            return jnp.where(whole, main, jnp.concatenate(only, 0))

        def corner_halo(f, i):
            above = corner_rows(near_rows, ABOVE, f, i)
            below = corner_rows(far_rows, BELOW, f, i)
            if above is None or below is None:
                return no_halo if above is below else (below if above is None else above)
            return jnp.where(sub < 4, above, below)

        edge = 3 if name == "before" else 0
        layers = (2, 3) if name == "before" else (0, 1)
        for f in range(FIELDS):
            present = [i for i in layers if f < VEL or f in range(HELD, GAIN) or (f, i) in which]
            halo = {i: corner_halo(f, i) for i in present}
            main = {i: no_rows if f < VEL else main_rows(f, i) for i in present}
            if f == BUOY:
                main = main_tiles(main, owners, row + 2, 2, lambda i: i * 8)
            elif f >= LAME:
                main = main_tiles(main, owners, row + f - LAME, 1, lambda i: 8 if i else 0)
            if f >= LAME:
                halo = halo_tiles(halo, after, before, row + 4 + f - LAME)
            for i in present:
                column[name, f, i] = jnp.concatenate([main[i], halo[i]], 0)
            if f < VEL and (f, edge) in which:
                face[name, f] = jnp.concatenate([main_rows(f, edge), halo[edge]], 0)
        for f, i in which:
            if not isinstance(f, str):
                continue
            halo = no_halo
            if i == edge and f == "gx":
                halo = jnp.where(sub == 0, -end_row(STRESS + XY, i, -1), 0.0)
            if i == edge and f == "gy":
                halo = jnp.where(sub == 7, end_row(STRESS + YY, i, 0), 0.0)
            if i == edge and f == "gz":
                halo = jnp.where(sub == 0, -end_row(STRESS + YZ, i, -1), 0.0)
            column[name, f, i] = jnp.concatenate([main_rows(f, i), halo], 0)

    def layers_of(f):
        names = [("before", 2), ("before", 3)] + [("own", i) for i in range(4)] + [("after", 0), ("after", 1)]
        return [column.get((name, f, i)) for name, i in names]

    s0 = [layers_of(STRESS + c) for c in range(6)]
    v0 = [layers_of(VEL + c) for c in range(3)]
    held = [layers_of(HELD + c) for c in range(6)]
    gain, lame, shear, buoy = (layers_of(f) for f in (GAIN, LAME, MU, BUOY))

    tall = sublane((EXT, LANES))

    def linked(test):
        def of(step):
            q = lax.rem(b + step + n, n)
            return jnp.where(test(q), 1, 0)

        flags = jnp.where(tall < ROWS, of(0), jnp.where(tall < ROWS + 4, of(1), of(-1)))
        return flags == 1

    link_before = linked(lambda q: q >= PY)
    link_after = linked(lambda q: q < n - PY)

    def x_next(a, l, across=None):
        if l == 1:
            return jnp.where(link_before, a[2], 0.0)
        if l == 5:
            return jnp.where(link_after, a[6] if across is None else across, 0.0)
        return a[l + 1]

    def x_prev(a, l, across=None):
        if l == 2:
            return jnp.where(link_before, a[1] if across is None else across, 0.0)
        if l == 6:
            return jnp.where(link_after, a[5], 0.0)
        return a[l - 1]

    def y_next(a):
        return roll(a, -1, 0)

    def y_prev(a):
        return roll(a, 1, 0)

    z_next, z_prev = z_after, z_before

    def move(v, s, spans, sums, faces):
        new = [[None] * 8 for _ in range(3)]

        def add(d, l, grad):
            if sums[d][l] is not None:
                grad = sums[d][l] + grad
            new[d][l] = v[d][l] + courant * buoy[l] * grad

        for l in spans[0]:
            ahead = x_next(s[XX], l, faces.get(XX))
            add(0, l, (ahead - s[XX][l]) + (s[XY][l] - y_prev(s[XY][l])) + (s[XZ][l] - z_prev(s[XZ][l])))
        for l in spans[1]:
            behind = x_prev(s[XY], l, faces.get(XY))
            add(1, l, (s[XY][l] - behind) + (y_next(s[YY][l]) - s[YY][l]) + (s[YZ][l] - z_prev(s[YZ][l])))
            behind = x_prev(s[XZ], l, faces.get(XZ))
            add(2, l, (s[XZ][l] - behind) + (s[YZ][l] - y_prev(s[YZ][l])) + (z_next(s[ZZ][l]) - s[ZZ][l]))
        return new

    def rates_at(v, l, wanted):
        out = [None] * 6
        ex = v[0][l] - x_prev(v[0], l)
        ey = v[1][l] - y_prev(v[1][l])
        ez = v[2][l] - z_prev(v[2][l])
        spread_part = lame[l] * (ex + ey + ez)
        twice = 2.0 * shear[l]
        for c, e in ((XX, ex), (YY, ey), (ZZ, ez)):
            if c in wanted:
                out[c] = spread_part + twice * e
        if XY in wanted:
            out[XY] = shear[l] * ((y_next(v[0][l]) - v[0][l]) + (x_next(v[1], l) - v[1][l]))
        if XZ in wanted:
            out[XZ] = shear[l] * ((z_next(v[0][l]) - v[0][l]) + (x_next(v[2], l) - v[2][l]))
        if YZ in wanted:
            out[YZ] = shear[l] * ((z_next(v[1][l]) - v[1][l]) + (y_next(v[2][l]) - v[2][l]))
        return out

    faces = {XX: face["after", STRESS + XX], XY: face["before", STRESS + XY], XZ: face["before", STRESS + XZ]}
    v1 = move(v0, s0, (range(0, 7), range(1, 8)), [layers_of(g) for g in ("gx", "gy", "gz")], faces)
    s1 = [[None] * 8 for _ in range(6)]
    m1 = {}
    for l in range(1, 7):
        wanted = (XX, XY, XZ) if l == 1 else range(6)
        rates = rates_at(v1, l, wanted)
        for c in wanted:
            s1[c][l] = held[c][l] + gain[l] * rates[c]
            if 2 <= l < 6:
                d = dec[0, l - 2]
                m1[c, l] = d * mem[c, 0, l - 2] - (1.0 - d) * los[0, l - 2] * rates[c][:ROWS]
    v2 = move(v1, s1, (range(1, 6), range(2, 7)), [layers_of(h) for h in (None, "hy", "hz")], {})
    place_sources(source, index, wave, 1, index.shape[0])
    for l in range(2, 6):
        i = l - 2
        rates = rates_at(v2, l, range(6))
        d = dec[0, i]
        lost = (1.0 - d) * los[0, i]
        for c in range(3):
            new_v[c, 0, i] = v2[c][l][:ROWS]
        for c in range(6):
            rate = rates[c][:ROWS]
            m2 = d * m1[c, l] - lost * rate
            new_m[c, 0, i] = m2
            value = s1[c][l][:ROWS] + courant * (rate + m2)
            if c < 3:
                value = value + source[i * ROWS : (i + 1) * ROWS, :]
            new_s[c, 0, i] = value


def body(
    velocity,
    stress,
    memory,
    lame_lambda,
    lame_mu,
    buoyancy,
    decay,
    loss,
    tile_lambda,
    tile_mu,
    tile_buoy,
    tile_dest,
    brick_tiles,
    src_index,
    src_wave,
):
    n = lax.axis_size("gx")
    merged = is_merged(n)
    sides = sides_of(n)
    chunk = tile_chunk(n)
    on_core = pl.BlockSpec(memory_space=pltpu.VMEM)
    scalars = pl.BlockSpec(memory_space=pltpu.SMEM)
    away = pl.BlockSpec(memory_space=pltpu.HBM)
    waves = src_wave.T
    fields = (velocity, stress, memory, lame_lambda, lame_mu, buoyancy, decay, loss)
    if merged:
        c_rows = [LONGEST * ROWS + 16]
    else:
        c_rows = [len(LAST) * ROWS + 16, len(FIRST) * ROWS + 16]
    tiles = (tile_lambda, tile_mu, tile_buoy)
    inputs = (*tiles, tile_dest, decay, loss, src_index, waves, stress, memory, velocity, lame_lambda, lame_mu, buoyancy, brick_tiles)
    packed = pl.pallas_call(
        functools.partial(pack_kernel, n, tile_lambda.shape[0]),
        out_shape=[
            jax.ShapeDtypeStruct((BLOCK, LANES), F32),
            jax.ShapeDtypeStruct((BLOCK, LANES), F32),
            jax.ShapeDtypeStruct((CORNER, LANES), BF16),
            jax.ShapeDtypeStruct((CORNER, LANES), BF16),
            jax.ShapeDtypeStruct((8, LANES), F32),
            jax.ShapeDtypeStruct((n * chunk, LANES), BF16),
        ]
        + [jax.ShapeDtypeStruct((r, LANES), BF16) for r in c_rows],
        in_specs=[away] * len(inputs),
        out_specs=[on_core] * (6 + len(c_rows)),
        scratch_shapes=[
            pltpu.SMEM(x.shape, x.dtype) if x.ndim == 1 else pltpu.VMEM(x.shape, x.dtype) for x in inputs
        ]
        + [
            pltpu.SemaphoreType.DMA((len(inputs),)),
            pltpu.VMEM((6, 4, ROWS, LANES), F32),
            pltpu.VMEM((4, ROWS, LANES), F32),
            pltpu.VMEM((4 * ROWS, LANES), F32),
            pltpu.VMEM((CORNER, LANES), F32),
            pltpu.VMEM((n * chunk, LANES), F32),
        ],
        compiler_params=pltpu.CompilerParams(vmem_limit_bytes=56 * 1024 * 1024),
        name="pack",
    )(*inputs)
    out_a, out_b, out_d, out_e, own_map, out_t = packed[:6]
    out_c = packed[6:]

    def hold(tiles_in, after, tiles_out):
        pass

    out_t = pl.pallas_call(
        hold,
        out_shape=jax.ShapeDtypeStruct(out_t.shape, out_t.dtype),
        in_specs=[pl.BlockSpec(memory_space=pl.ANY)] * 2,
        out_specs=pl.BlockSpec(memory_space=pl.ANY),
        input_output_aliases={0: 0},
        name="hold",
    )(out_t, own_map)
    def permute(array, source_of):
        return lax.ppermute(array, "gx", [(source_of(i), i) for i in range(n)])

    got_c = [permute(c, lambda i, o=o: (i + o) % n) for c, o in zip(out_c, sides)]
    got_d = [permute(out_d, lambda i, o=o: pair_far((i + o) % n, n)) for o in sides]
    got_e = [permute(out_e, lambda i, o=o: pair_near((i + o) % n)) for o in sides]
    got_b = permute(out_b, lambda i: pair_far(i, n))
    got_a = permute(out_a, pair_near)
    got_t = lax.all_to_all(out_t, "gx", split_axis=0, concat_axis=0, tiled=True)

    return pl.pallas_call(
        functools.partial(wave_kernel, n),
        out_shape=[
            jax.ShapeDtypeStruct(velocity.shape, F32),
            jax.ShapeDtypeStruct(stress.shape, F32),
            jax.ShapeDtypeStruct(memory.shape, F32),
        ],
        in_specs=[on_core] * 8 + [scalars] + [on_core] * (5 + 3 * len(sides)),
        out_specs=[on_core] * 3,
        scratch_shapes=[
            pltpu.VMEM((4 * ROWS, LANES), F32),
            pltpu.VMEM((n * chunk, LANES), F32),
            pltpu.VMEM((16 * 32, LANES), BF16),
            pltpu.VMEM((16 * 32, LANES), F32),
            pltpu.VMEM((CORNER, LANES), F32),
            pltpu.VMEM((CORNER, LANES), F32),
            pltpu.VMEM((16, LANES), F32),
        ],
        compiler_params=pltpu.CompilerParams(vmem_limit_bytes=48 * 1024 * 1024),
        name="wave",
    )(*fields, src_index, waves, own_map, got_a, got_b, got_t, *got_c, *got_d, *got_e)


def solution(mesh):
    split = ("groups", "gx")
    whole = P(None, split, None, None, None)
    field = P(split, None, None, None)
    return jax.shard_map(
        body,
        mesh=mesh,
        in_specs=(whole,) * 3
        + (field,) * 5
        + (P(split, None),) * 3
        + (P(split), P(split, None), P(split), P(split, None)),
        out_specs=(whole,) * 3,
        check_vma=False,
    )
```

```python
import functools

import jax
import jax.numpy as jnp
from jax import lax
from jax.experimental import pallas as pl
from jax.experimental.pallas import tpu as pltpu
from jax.sharding import PartitionSpec as P

PY = 8
TY = 8
TZ = 8
courant = 0.25

F32 = jnp.float32
BF16 = jnp.bfloat16
XX, YY, ZZ, XY, XZ, YZ = range(6)
STRESS, VEL, HELD, GAIN, LAME, MU, BUOY = 0, 6, 9, 15, 16, 17, 18
FIELDS = 19
LAST = [("gx", 2), ("gx", 3), ("gy", 3), ("gz", 3), (STRESS + XY, 3), (STRESS + XZ, 3)]
LAST += [(VEL, 2), (VEL, 3), (VEL + 1, 3), (VEL + 2, 3), (BUOY, 2), (BUOY, 3)]
LAST += [(HELD + c, 3) for c in (XX, XY, XZ)] + [(GAIN, 3), (LAME, 3), (MU, 3)]
FIRST = [("gx", 0), ("gy", 0), ("gz", 0), ("gy", 1), ("gz", 1), (STRESS + XX, 0)]
FIRST += [(VEL, 0), (VEL + 1, 0), (VEL + 1, 1), (VEL + 2, 0), (VEL + 2, 1), (BUOY, 0), (BUOY, 1)]
FIRST += [(HELD + XX, 0), ("hy", 0), ("hz", 0), (GAIN, 0), (LAME, 0), (MU, 0)]
BELOW_LAST = [(STRESS + c, 3) for c in range(6) if c != ZZ] + [(VEL, 3), (VEL + 1, 3), (HELD + XY, 3), (GAIN, 3)]
BELOW_LAST = [(f, i, -1) for f, i in BELOW_LAST + [(MU, 3), (BUOY, 3), (STRESS + XY, 2)]] + [(STRESS + XY, 3, -2)]
ABOVE_LAST = [(STRESS + c, 3) for c in range(6)] + [(VEL, 3), (VEL + 2, 3), (HELD + XZ, 3), (GAIN, 3)]
ABOVE_LAST = [(f, i, 0) for f, i in ABOVE_LAST + [(MU, 3), (BUOY, 3), (STRESS + XZ, 2)]] + [(STRESS + XZ, 3, 1)]
BELOW_FIRST = [(STRESS + c, 0) for c in range(6)] + [(VEL + 1, 0), (VEL + 2, 0), (HELD + YZ, 0), (GAIN, 0)]
BELOW_FIRST = [(f, i, -1) for f, i in BELOW_FIRST + [(MU, 0), (BUOY, 0), (STRESS + YZ, 1)]] + [(STRESS + YZ, 0, -2)]
ABOVE_FIRST = [(STRESS + c, 0) for c in range(6)] + [(VEL + c, 0) for c in range(3)] + [(HELD + XX, 0), (HELD + YY, 0)]
ABOVE_FIRST += [(GAIN, 0), (LAME, 0), (MU, 0), (BUOY, 0), (STRESS + XX, 1), (STRESS + YY, 1)]
ABOVE_FIRST = [(f, i, 0) for f, i in ABOVE_FIRST] + [(STRESS + XX, 0, 1), (STRESS + YY, 0, 1)]
BELOW = BELOW_LAST + BELOW_FIRST
ABOVE = ABOVE_LAST + ABOVE_FIRST
ENDS = [(STRESS + YY, 0, 0), (STRESS + XY, 0, -1), (STRESS + YZ, 0, -1)]
ENDS += [("gy", 0, -1), (VEL + 1, 0, -1), (BUOY, 0, -1)]
ENDS += [(STRESS + YY, 3, 0), (STRESS + XY, 3, -1), (STRESS + YZ, 3, -1)]
ENDS += [("gx", 3, 0), (VEL, 3, 0), (BUOY, 3, 0)]
ENDS_MAP = 12
LONGEST = max(len(LAST), len(FIRST))
ROWS = 32
EXT = ROWS + 8
LANES = 128
BLOCK = FIELDS * 8 + 8
CORNER = -(-(max(len(BELOW), len(ABOVE)) + 1) // 16) * 16


def pair_near(i):
    return i ^ 1


def pair_far(i, n):
    return (i - 1) % n if i % 2 == 0 else (i + 1) % n


def is_merged(n):
    return n == 2 * PY


def sides_of(n):
    return [PY] if is_merged(n) else [-PY, PY]


def tile_offsets(n):
    return [k for o in [0] + sides_of(n) for k in (o, o + 1, o - 1)]


def tile_chunk(n):
    return -(-(9 + 7 * len(sides_of(n))) // 16) * 16


def roll(x, by, axis):
    size = x.shape[axis]
    by = by % size
    return x if by == 0 else pltpu.roll(x, by, axis)


def sublane(shape):
    return lax.broadcasted_iota(jnp.int32, shape, 0)


def lane(shape):
    return lax.broadcasted_iota(jnp.int32, shape, 1)


def z_after(a):
    return jnp.where(lane(a.shape) == LANES - 1, 0.0, roll(a, -1, 1))


def z_before(a):
    return jnp.where(lane(a.shape) == 0, 0.0, roll(a, 1, 1))


def place_sources(index, wave, step):
    count = index.shape[1]
    cells = jnp.broadcast_to(index[...], (LANES, count))
    place = sublane((LANES, count))
    rows = (lax.shift_right_logical(cells, 7) == place).astype(F32)
    at = ((cells & (LANES - 1)) == place).astype(F32)
    left = wave[step : step + 1, :]
    parts = []
    for _ in range(3):
        part = left.astype(BF16).astype(F32)
        parts.append((at * part).astype(BF16))
        left = left - part
    total = None
    for part in parts:
        done = lax.dot_general(rows.astype(BF16), part, (((1,), (1,)), ((), ())), preferred_element_type=F32)
        total = done if total is None else total + done
    return total


def pack_kernel(n, per, *refs):
    merged = is_merged(n)
    sides = len(sides_of(n))
    far_refs, outs, refs = refs[:15], refs[15 : 31 + sides], refs[31 + sides :]
    out_a, out_b, out_d, out_e, out_map, out_t = outs[:6]
    dec, los, st, mem, vel, lam, mu, bu = outs[6:14]
    held, later = outs[14:16]
    out_c = outs[16:]
    near_lam, near_mu, near_bu, near_dest, index, wave, tiles, sems = refs[:8]
    gain, source, corner, ends, routed, routed_out = refs[8:]
    near_refs = (near_lam, near_mu, near_bu, near_dest, dec, los, index, wave, st, mem, vel, lam, mu, bu, tiles)
    b = lax.axis_index("gx")
    even = lax.rem(b, 2) == 0
    first_x = b < PY
    top, bottom = slice(0, 8), slice(ROWS - 8, ROWS)
    copies = {}
    for k in (0, 1, 2, 3, 14, 6, 7, 8, 10, 13, 11, 12, 4, 5, 9):
        copies[k] = pltpu.make_async_copy(far_refs[k], near_refs[k], sems.at[k])
        copies[k].start()

    def arrive(*which):
        for k in which:
            copies[k].wait()

    arrive(0, 1, 2, 3)
    route_tiles(n, near_lam, near_mu, near_bu, near_dest, routed, routed_out)
    leave = pltpu.make_async_copy(routed_out, out_t, sems.at[15])
    leave.start()
    arrive(6, 7, 14)
    source[...] = place_sources(index, wave, 0)
    later[...] = place_sources(index, wave, 1)

    def get(f, i, rows=slice(None)):
        if f < VEL:
            return st[f, 0, i, rows]
        if f < HELD:
            return vel[f - VEL, 0, i, rows]
        if f < GAIN:
            return held[f - HELD, i, rows]
        if f == GAIN:
            return gain[i, rows]
        return (lam, mu, bu)[f - LAME][0, i, rows]

    sub = sublane((8, LANES))

    rows_z = LANES // TZ
    table = tiles[...]
    spots = table.shape[1]
    owner = jnp.where(table >= 0, jnp.floor((table.astype(F32) + 0.5) * (1.0 / per)) + 1.0, 0.0)
    spot = lane((8, spots))
    wide = jnp.where(spot // rows_z == sublane((8, spots)), jnp.broadcast_to(owner, (8, spots)), 0.0)
    spread = (lax.rem(sublane((spots, LANES)), rows_z) == lane((spots, LANES)) // TZ).astype(BF16)
    owners = jnp.dot(wide.astype(BF16), spread, preferred_element_type=F32) - 1.0
    out_map[...] = owners
    last = ROWS // TY - 1

    def prev_y(a):
        return jnp.where(sublane(a.shape) == 0, 0.0, roll(a, 1, 0))

    def next_y(a):
        return jnp.where(sublane(a.shape) == ROWS - 1, 0.0, roll(a, -1, 0))

    def sums(kind, i):
        def s(c, k):
            return held[c, k] if kind[0] == "h" else st[c, 0, k]

        def dy_prev(c):
            return s(c, i) - prev_y(s(c, i))

        def dy_next(c):
            return next_y(s(c, i)) - s(c, i)

        def dz_prev(c):
            return s(c, i) - z_before(s(c, i))

        def dz_next(c):
            return z_after(s(c, i)) - s(c, i)

        if kind == "gx":
            along = s(XX, i + 1) - s(XX, i) if i < 3 else -s(XX, i)
            return along + dy_prev(XY) + dz_prev(XZ)
        cross = XY if kind[1] == "y" else XZ
        along = s(cross, i) - s(cross, i - 1) if i > 0 else s(cross, i)
        if kind[1] == "y":
            return along + dy_next(YY) + dz_prev(YZ)
        return along + dy_prev(YZ) + dz_next(ZZ)

    def entry(f, i):
        return sums(f, i) if isinstance(f, str) else get(f, i)

    def edge_rows(f):
        if f == FIELDS:
            return jnp.broadcast_to(owners[0:1], (8, LANES)), jnp.broadcast_to(owners[last : last + 1], (8, LANES))
        lo, hi = get(f, 0, top), roll(get(f, 0, bottom), 2, 0)
        for i in range(1, 4):
            mine = sub // 2 == i
            lo = jnp.where(mine, roll(get(f, i, top), 2 * i, 0), lo)
            hi = jnp.where(mine, roll(get(f, i, bottom), 2 * i + 2, 0), hi)
        return lo, hi

    def write_edges(which):
        for f in which:
            lo, hi = edge_rows(f)
            out_a[f * 8 : f * 8 + 8, :] = jnp.where(even, hi, lo)
            out_b[f * 8 : f * 8 + 8, :] = jnp.where(even, lo, hi)

    def write_corner(rows, which, strip, at):
        for k, (f, i, r) in enumerate(rows):
            if f in which:
                corner[at + k : at + k + 1, :] = get(f, i, slice(r % ROWS, r % ROWS + 1))
        if FIELDS in which:
            corner[at + len(rows) : at + len(rows) + 1, :] = owners[strip : strip + 1]

    def write_layers(out, entries, which):
        for k, (f, i) in enumerate(entries):
            if f in which:
                out[k * ROWS : (k + 1) * ROWS, :] = entry(f, i).astype(BF16)

    def write_ends(which):
        for k, (f, i, r) in enumerate(ENDS):
            if f in which:
                row = slice(r % ROWS, r % ROWS + 1)
                ends[k : k + 1, :] = sums(f, i)[row] if isinstance(f, str) else get(f, i, row)

    def write(*which):
        write_edges([f for f in which if not isinstance(f, str)])
        write_corner(BELOW, which, last, 0)
        write_corner(ABOVE, which, 0, CORNER)
        write_ends(which)
        if merged:

            @pl.when(first_x)
            def _():
                write_layers(out_c[0], LAST, which)

            @pl.when(jnp.logical_not(first_x))
            def _():
                write_layers(out_c[0], FIRST, which)
        else:
            write_layers(out_c[0], LAST, which)
            write_layers(out_c[1], FIRST, which)

    corner[...] = jnp.zeros_like(corner)
    ends[ENDS_MAP : ENDS_MAP + last + 1, :] = owners[0 : last + 1]
    arrive(8)
    write(FIELDS, *range(STRESS, VEL), "gx", "gy", "gz")
    arrive(10, 13, 11, 12)
    write(*range(VEL, HELD), LAME, MU, BUOY)
    arrive(4, 5)
    for i in range(4):
        gain[i] = courant * (1.0 - (1.0 - dec[0, i]) * los[0, i])
    write(GAIN)
    arrive(9)
    for i in range(4):
        kept = courant * dec[0, i]
        for c in range(6):
            value = st[c, 0, i] + kept * mem[c, 0, i]
            if c < 3:
                value = value + source[i * ROWS : (i + 1) * ROWS, :]
            held[c, i] = value
    write(*range(HELD, GAIN), "hy", "hz")
    below, above = corner[0:CORNER, :].astype(BF16), corner[CORNER : 2 * CORNER, :].astype(BF16)
    out_e[...] = jnp.where(even, below, above)
    out_d[...] = jnp.where(even, above, below)
    for out, entries in zip(out_c, (LAST, FIRST)):
        if merged:
            base = LONGEST * ROWS

            @pl.when(first_x)
            def _():
                rest = (LONGEST - len(LAST)) * ROWS
                out[len(LAST) * ROWS : base, :] = jnp.zeros((rest, LANES), BF16)
        else:
            base = len(entries) * ROWS
        out[base : base + 16, :] = ends[...].astype(BF16)
    leave.wait()


def route_tiles(n, near_lam, near_mu, near_bu, near_dest, rows, out):
    offsets = tile_offsets(n)
    chunk = tile_chunk(n)
    per = near_lam.shape[0]
    total = n * len(offsets)
    at = lane((1, per))
    stored = jnp.full((1, per), -1, jnp.int32)
    for t in range(per):
        stored = jnp.where(at == t, near_dest[t], stored)
    row = sublane((total, per))
    brick = lax.rem(row, n)
    for k, off in enumerate(offsets):
        brick = jnp.where(row // n == k, brick + off % n, brick)
    brick = jnp.where(brick >= n, brick - n, brick)
    route = (brick == stored).astype(BF16)
    cell, spot = sublane((2 * LANES, LANES)), lane((2 * LANES, LANES))
    half = lax.rem(spot, 64)
    cells = half // 16 * 64 + lax.rem(half, 16)
    low = jnp.logical_and(spot < 64, cell == cells).astype(BF16)
    high = jnp.logical_and(spot >= 64, cell == cells + 48).astype(BF16)
    left = lane((n, LANES)) < 64
    if chunk > 9 + 7 * len(sides_of(n)):
        rows[...] = jnp.zeros_like(rows)

    def put(j, value):
        rows[pl.ds(j, n, stride=chunk), :] = value

    for p, near in enumerate((near_lam, near_mu, near_bu)):
        tile = near[...]
        whole = jnp.dot(route, tile, preferred_element_type=F32)
        first = jnp.dot(route, jnp.dot(tile, low, preferred_element_type=F32).astype(BF16), preferred_element_type=F32)
        final = jnp.dot(route, jnp.dot(tile, high, preferred_element_type=F32).astype(BF16), preferred_element_type=F32)

        def slot(x, k):
            return x[k * n : (k + 1) * n]

        put(2 * p, slot(whole, 0)[:, :LANES])
        put(2 * p + 1, slot(whole, 0)[:, LANES:])
        put(6 + p, slot(first, 1) + slot(final, 2))
        for g in range(len(sides_of(n))):
            side = slot(whole, 3 + 3 * g)
            base = 9 + 7 * g
            if p < 2:
                put(base + p, jnp.where(left, side[:, :LANES], side[:, LANES:]))
            else:
                put(base + 2, side[:, :LANES])
                put(base + 3, side[:, LANES:])
            put(base + 4 + p, slot(first, 4 + 3 * g) + slot(final, 5 + 3 * g))
    out[...] = rows[...].astype(BF16)


def halo_blocks(even, near, far, f):
    x = near[f * 8 : f * 8 + 8, :]
    y = far[f * 8 : f * 8 + 8, :]
    return jnp.where(even, x, y), jnp.where(even, y, x)


def halo_rows(blocks, i):
    after, before = blocks
    sub = sublane((8, LANES))
    return jnp.where(sub < 2, roll(after, -2 * i, 0), roll(before, 6 - 2 * i, 0))


def side_messages(n, got_c):
    first_x = lax.axis_index("gx") < PY
    if is_merged(n):
        message, base = got_c[0], LONGEST * ROWS
        return [("before", LAST, message, base, jnp.logical_not(first_x)), ("after", FIRST, message, base, first_x)]
    return [
        (name, which, message, len(which) * ROWS, None)
        for name, which, message in (("before", LAST, got_c[0]), ("after", FIRST, got_c[1]))
    ]


def side_rows(which, message, whole, ends, f, i):
    k = which.index((f, i))
    main = message[k * ROWS : (k + 1) * ROWS, :].astype(F32)
    if whole is None:
        return main
    sub = sublane((8, LANES))
    only = [jnp.zeros((8, LANES), F32)] * (ROWS // 8)
    for e in (3, 4, 5, 9, 10, 11):
        if ENDS[e][:2] == (f, i):
            at = ENDS[e][2] % ROWS
            only[at // 8] = jnp.where(sub == at % 8, jnp.broadcast_to(ends[e : e + 1, :], (8, LANES)), 0.0)
    return jnp.where(whole, main, jnp.concatenate(only, 0))


SIDES = [("before", f, i) for f, i in LAST] + [("after", f, i) for f, i in FIRST]


def side_kernel(n, *refs):
    sides = len(sides_of(n))
    got_c, (side, ends) = refs[:sides], refs[sides:]
    sub = sublane((8, LANES))
    for name, which, message, base, whole in side_messages(n, got_c):
        ends[...] = message[base : base + 16, :].astype(F32)

        def end_row(f, i, r):
            at = ENDS.index((f, i, r))
            return jnp.broadcast_to(ends[at : at + 1, :], (8, LANES))

        edge = 3 if name == "before" else 0
        for f, i in which:
            k = SIDES.index((name, f, i))
            side[k, 0:ROWS] = side_rows(which, message, whole, ends, f, i)
            if isinstance(f, str):
                halo = jnp.zeros((8, LANES), F32)
                if i == edge and f == "gx":
                    halo = jnp.where(sub == 0, -end_row(STRESS + XY, i, -1), 0.0)
                if i == edge and f == "gy":
                    halo = jnp.where(sub == 7, end_row(STRESS + YY, i, 0), 0.0)
                if i == edge and f == "gz":
                    halo = jnp.where(sub == 0, -end_row(STRESS + YZ, i, -1), 0.0)
                side[k, ROWS:EXT] = halo


def line_layout(n):
    at, layout = 0, {}
    spans = [(2 * p, 2) for p in range(3)] + [(6 + p, 1) for p in range(3)]
    for g in range(len(sides_of(n))):
        spans += [(9 + 7 * g, 1), (10 + 7 * g, 1), (11 + 7 * g, 2)] + [(13 + 7 * g + p, 1) for p in range(3)]
    for row, halves in spans:
        layout[row] = at, halves
        at += n * 16 * halves
    return layout, at


def tile_kernel(n, got_t, out, rows_t, spread_rows):
    chunk = tile_chunk(n)
    rows_t[...] = got_t[...].astype(F32)
    on_line = lane((16, LANES)) // TZ == sublane((16, LANES))
    spread = (lax.rem(sublane((LANES, LANES)), TZ) == lax.rem(lane((LANES, LANES)), TZ)).astype(BF16)
    for row, (base, halves) in line_layout(n)[0].items():

        def group(q, _, row=row, base=base, halves=halves):
            for s in range(16):
                for h in range(halves):
                    value = rows_t[pl.ds((q * 16 + s) * chunk + row + h, 1), :]
                    value = jnp.where(on_line, jnp.broadcast_to(value, (16, LANES)), 0.0)
                    at = (s * halves + h) * 16
                    spread_rows[at : at + 16, :] = value.astype(BF16)
            size = 256 * halves
            done = jnp.dot(spread_rows[0:size, :], spread, preferred_element_type=F32)
            out[pl.ds(base + q * size, size), :] = done
            return 0

        if n == 16:
            group(0, 0)
        else:
            lax.fori_loop(0, n // 16, group, 0)


def wave_kernel(n, *refs):
    merged = is_merged(n)
    (vel, st, mem, lam, mu, bu, dec, los, kept, side, source, maps, got_a, got_b, lines) = refs[:15]
    refs = refs[15:]
    sides = len(sides_of(n))
    got_c, got_d, got_e = refs[:sides], refs[sides : 2 * sides], refs[2 * sides : 3 * sides]
    far_outs, refs = refs[3 * sides : 3 * sides + 3], refs[3 * sides + 3 :]
    near_rows, far_rows, end_rows, new_v, new_s, new_m, sems = refs
    b = lax.axis_index("gx")
    even = lax.rem(b, 2) == 0
    sub = sublane((8, LANES))
    layout, _ = line_layout(n)

    def overlay(row, wanted):
        base, halves = layout[row]

        def take(s, values):
            done = []
            for value, (_, owner, at) in zip(values, wanted):
                here = lines[pl.ds(base + s * halves * 16 + at, 8), :]
                done.append(jnp.where(owner == s.astype(F32) if n > 16 else owner == s * 1.0, here, value))
            return done

        values = [w[0] for w in wanted]
        if n == 16:
            for s in range(n):
                values = take(s, values)
            return values
        return lax.fori_loop(0, n, take, values)

    column = {}
    rows_y = ROWS // TY

    def own(f, i):
        if f < VEL:
            return st[f, 0, i]
        if f < HELD:
            return vel[f - VEL, 0, i]
        if f < GAIN:
            return kept[f - HELD, i]
        if f == GAIN:
            return courant * (1.0 - (1.0 - dec[0, i]) * los[0, i])
        return (lam, mu, bu)[f - LAME][0, i]

    def main_tiles(mains, owners, row, line_of):
        wanted = []
        for i, m in mains.items():
            for p in range(rows_y):
                owner = jnp.broadcast_to(owners[p : p + 1], (8, LANES))
                wanted.append((m[p * 8 : (p + 1) * 8], owner, line_of(i)))
        laid = overlay(row, wanted)
        return {i: jnp.concatenate(laid[k * rows_y : (k + 1) * rows_y], 0) for k, i in enumerate(mains)}

    def halo_tiles(halos, after, before, row):
        zeros = jnp.zeros((8, LANES), F32)
        blocks = overlay(row, [(zeros, after, 0), (zeros, before, 8)])
        covered = jnp.where(sub < 4, after, before) >= 0.0
        return {i: jnp.where(covered, halo_rows(blocks, i), h) for i, h in halos.items()}

    after, before = halo_blocks(even, got_a, got_b, FIELDS)
    for f in range(FIELDS):
        blocks = halo_blocks(even, got_a, got_b, f)
        main = {i: own(f, i) for i in range(4)}
        halo = {i: halo_rows(blocks, i) for i in range(4)}
        if f >= LAME:
            p = f - LAME
            main = main_tiles(main, maps[...], 2 * p, lambda i: i * 8)
            halo = halo_tiles(halo, after, before, 6 + p)
        for i in range(4):
            column["own", f, i] = jnp.concatenate([main[i], halo[i]], 0)

    def corner_rows(table, rows, f, i):
        value = None
        for k, (g, j, r) in enumerate(rows):
            if (g, j) == (f, i):
                row = jnp.broadcast_to(table[k : k + 1, :], (8, LANES))
                value = jnp.where(sub == (r % 8), row, 0.0 if value is None else value)
        return value

    no_rows, no_halo = jnp.zeros((ROWS, LANES), F32), jnp.zeros((8, LANES), F32)
    face = {}
    for order, (name, which) in enumerate((("before", LAST), ("after", FIRST))):
        group = 0 if merged else order
        message = got_c[group]
        base = (LONGEST if merged else len(which)) * ROWS
        if group == order:
            near, far = got_e[group][...].astype(F32), got_d[group][...].astype(F32)
            near_rows[...] = jnp.where(even, near, far)
            far_rows[...] = jnp.where(even, far, near)
            end_rows[...] = message[base : base + 16, :].astype(F32)
        after = jnp.broadcast_to(near_rows[len(ABOVE) : len(ABOVE) + 1, :], (8, LANES))
        before = jnp.broadcast_to(far_rows[len(BELOW) : len(BELOW) + 1, :], (8, LANES))
        owners = end_rows[8:16, :][ENDS_MAP - 8 :]
        row = 9 + 7 * group

        def main_rows(f, i):
            return side[SIDES.index((name, f, i)), 0:ROWS] if (f, i) in which else no_rows

        def corner_halo(f, i):
            above = corner_rows(near_rows, ABOVE, f, i)
            below = corner_rows(far_rows, BELOW, f, i)
            if above is None or below is None:
                return no_halo if above is below else (below if above is None else above)
            return jnp.where(sub < 4, above, below)

        edge = 3 if name == "before" else 0
        layers = (2, 3) if name == "before" else (0, 1)
        for f in range(FIELDS):
            present = [i for i in layers if f < VEL or f in range(HELD, GAIN) or (f, i) in which]
            halo = {i: corner_halo(f, i) for i in present}
            main = {i: no_rows if f < VEL else main_rows(f, i) for i in present}
            if f == BUOY:
                main = main_tiles(main, owners, row + 2, lambda i: i * 8)
            elif f >= LAME:
                main = main_tiles(main, owners, row + f - LAME, lambda i: 8 if i else 0)
            if f >= LAME:
                halo = halo_tiles(halo, after, before, row + 4 + f - LAME)
            for i in present:
                column[name, f, i] = jnp.concatenate([main[i], halo[i]], 0)
            if f < VEL and (f, edge) in which:
                face[name, f] = jnp.concatenate([main_rows(f, edge), halo[edge]], 0)
        for f, i in which:
            if isinstance(f, str):
                column[name, f, i] = side[SIDES.index((name, f, i))]

    def layers_of(f):
        names = [("before", 2), ("before", 3)] + [("own", i) for i in range(4)] + [("after", 0), ("after", 1)]
        return [column.get((name, f, i)) for name, i in names]

    s0 = [layers_of(STRESS + c) for c in range(6)]
    v0 = [layers_of(VEL + c) for c in range(3)]
    held = [layers_of(HELD + c) for c in range(6)]
    gain, lame, shear, buoy = (layers_of(f) for f in (GAIN, LAME, MU, BUOY))

    tall = sublane((EXT, LANES))

    def linked(test):
        def of(step):
            q = lax.rem(b + step + n, n)
            return jnp.where(test(q), 1, 0)

        flags = jnp.where(tall < ROWS, of(0), jnp.where(tall < ROWS + 4, of(1), of(-1)))
        return flags == 1

    link_before = linked(lambda q: q >= PY)
    link_after = linked(lambda q: q < n - PY)

    def x_next(a, l, across=None):
        if l == 1:
            return jnp.where(link_before, a[2], 0.0)
        if l == 5:
            return jnp.where(link_after, a[6] if across is None else across, 0.0)
        return a[l + 1]

    def x_prev(a, l, across=None):
        if l == 2:
            return jnp.where(link_before, a[1] if across is None else across, 0.0)
        if l == 6:
            return jnp.where(link_after, a[5], 0.0)
        return a[l - 1]

    def y_next(a):
        return roll(a, -1, 0)

    def y_prev(a):
        return roll(a, 1, 0)

    z_next, z_prev = z_after, z_before

    def move(v, s, spans, sums, faces):
        new = [[None] * 8 for _ in range(3)]

        def add(d, l, grad):
            if sums[d][l] is not None:
                grad = sums[d][l] + grad
            new[d][l] = v[d][l] + courant * buoy[l] * grad

        for l in spans[0]:
            ahead = x_next(s[XX], l, faces.get(XX))
            add(0, l, (ahead - s[XX][l]) + (s[XY][l] - y_prev(s[XY][l])) + (s[XZ][l] - z_prev(s[XZ][l])))
        for l in spans[1]:
            behind = x_prev(s[XY], l, faces.get(XY))
            add(1, l, (s[XY][l] - behind) + (y_next(s[YY][l]) - s[YY][l]) + (s[YZ][l] - z_prev(s[YZ][l])))
            behind = x_prev(s[XZ], l, faces.get(XZ))
            add(2, l, (s[XZ][l] - behind) + (s[YZ][l] - y_prev(s[YZ][l])) + (z_next(s[ZZ][l]) - s[ZZ][l]))
        return new

    def rates_at(v, l, wanted):
        out = [None] * 6
        ex = v[0][l] - x_prev(v[0], l)
        ey = v[1][l] - y_prev(v[1][l])
        ez = v[2][l] - z_prev(v[2][l])
        spread_part = lame[l] * (ex + ey + ez)
        twice = 2.0 * shear[l]
        for c, e in ((XX, ex), (YY, ey), (ZZ, ez)):
            if c in wanted:
                out[c] = spread_part + twice * e
        if XY in wanted:
            out[XY] = shear[l] * ((y_next(v[0][l]) - v[0][l]) + (x_next(v[1], l) - v[1][l]))
        if XZ in wanted:
            out[XZ] = shear[l] * ((z_next(v[0][l]) - v[0][l]) + (x_next(v[2], l) - v[2][l]))
        if YZ in wanted:
            out[YZ] = shear[l] * ((z_next(v[1][l]) - v[1][l]) + (y_next(v[2][l]) - v[2][l]))
        return out

    faces = {XX: face["after", STRESS + XX], XY: face["before", STRESS + XY], XZ: face["before", STRESS + XZ]}
    v1 = move(v0, s0, (range(0, 7), range(1, 8)), [layers_of(g) for g in ("gx", "gy", "gz")], faces)
    s1 = [[None] * 8 for _ in range(6)]
    m1 = {}
    for l in range(1, 7):
        wanted = (XX, XY, XZ) if l == 1 else range(6)
        rates = rates_at(v1, l, wanted)
        for c in wanted:
            s1[c][l] = held[c][l] + gain[l] * rates[c]
            if 2 <= l < 6:
                d = dec[0, l - 2]
                m1[c, l] = d * mem[c, 0, l - 2] - (1.0 - d) * los[0, l - 2] * rates[c][:ROWS]
    v2 = move(v1, s1, (range(1, 6), range(2, 7)), [layers_of(h) for h in (None, "hy", "hz")], {})
    copies = []

    def send(k, i):
        near, far = (new_v, new_s, new_m)[k], far_outs[k]
        copies.append(pltpu.make_async_copy(near.at[:, :, i], far.at[:, :, i], sems.at[k, i]))
        copies[-1].start()

    for i in range(4):
        for c in range(3):
            new_v[c, 0, i] = v2[c][i + 2][:ROWS]
        send(0, i)
    for i in range(4):
        l = i + 2
        rates = rates_at(v2, l, range(6))
        d = dec[0, i]
        lost = (1.0 - d) * los[0, i]
        for c in range(6):
            rate = rates[c][:ROWS]
            m2 = d * m1[c, l] - lost * rate
            new_m[c, 0, i] = m2
            value = s1[c][l][:ROWS] + courant * (rate + m2)
            if c < 3:
                value = value + source[i * ROWS : (i + 1) * ROWS, :]
            new_s[c, 0, i] = value
        send(1, i)
        send(2, i)
    for copy in copies:
        copy.wait()


def body(
    velocity,
    stress,
    memory,
    lame_lambda,
    lame_mu,
    buoyancy,
    decay,
    loss,
    tile_lambda,
    tile_mu,
    tile_buoy,
    tile_dest,
    brick_tiles,
    src_index,
    src_wave,
):
    n = lax.axis_size("gx")
    merged = is_merged(n)
    sides = sides_of(n)
    chunk = tile_chunk(n)
    on_core = pl.BlockSpec(memory_space=pltpu.VMEM)
    away = pl.BlockSpec(memory_space=pltpu.HBM)
    def vmem(*shape):
        return jax.ShapeDtypeStruct(shape, F32)

    waves = src_wave.T
    cells = src_index[None, :]
    fields = (velocity, stress, memory, lame_lambda, lame_mu, buoyancy, decay, loss)
    if merged:
        c_rows = [LONGEST * ROWS + 16]
    else:
        c_rows = [len(LAST) * ROWS + 16, len(FIRST) * ROWS + 16]
    tiles = (tile_lambda, tile_mu, tile_buoy)
    kept = (decay, loss, stress, memory, velocity, lame_lambda, lame_mu, buoyancy)
    inputs = (*tiles, tile_dest, decay, loss, cells, waves, stress, memory, velocity, lame_lambda, lame_mu, buoyancy, brick_tiles)
    inputs = tuple(pltpu.with_memory_space_constraint(x, pltpu.HBM) for x in inputs)
    packed = pl.pallas_call(
        functools.partial(pack_kernel, n, tile_lambda.shape[0]),
        out_shape=[
            jax.ShapeDtypeStruct((BLOCK, LANES), F32),
            jax.ShapeDtypeStruct((BLOCK, LANES), F32),
            jax.ShapeDtypeStruct((CORNER, LANES), BF16),
            jax.ShapeDtypeStruct((CORNER, LANES), BF16),
            jax.ShapeDtypeStruct((8, LANES), F32),
            jax.ShapeDtypeStruct((n * chunk, LANES), BF16),
        ]
        + [jax.ShapeDtypeStruct(x.shape, x.dtype) for x in kept]
        + [vmem(6, 4, ROWS, LANES), vmem(4 * ROWS, LANES)]
        + [jax.ShapeDtypeStruct((r, LANES), BF16) for r in c_rows],
        in_specs=[away] * len(inputs),
        out_specs=[on_core] * 5 + [away] + [on_core] * (10 + len(c_rows)),
        scratch_shapes=[
            pltpu.SMEM(x.shape, x.dtype) if x.ndim == 1 else pltpu.VMEM(x.shape, x.dtype)
            for x in (*tiles, tile_dest, cells, waves, brick_tiles)
        ]
        + [
            pltpu.SemaphoreType.DMA((16,)),
            pltpu.VMEM((4, ROWS, LANES), F32),
            pltpu.VMEM((4 * ROWS, LANES), F32),
            pltpu.VMEM((2 * CORNER, LANES), F32),
            pltpu.VMEM((16, LANES), F32),
            pltpu.VMEM((n * chunk, LANES), F32),
            pltpu.VMEM((n * chunk, LANES), BF16),
        ],
        compiler_params=pltpu.CompilerParams(vmem_limit_bytes=16 * 1024 * 1024),
        name="pack",
    )(*inputs)
    out_a, out_b, out_d, out_e, own_map, out_t = packed[:6]
    held, later = packed[14:16]
    out_c = packed[16:]
    dec, los, st, mem, vel, lam, mu, bu = packed[6:14]
    fields = (vel, st, mem, lam, mu, bu, dec, los)

    def permute(array, source_of):
        return lax.ppermute(array, "gx", [(source_of(i), i) for i in range(n)])

    got_c = [permute(c, lambda i, o=o: (i + o) % n) for c, o in zip(out_c, sides)]
    got_d = [permute(out_d, lambda i, o=o: pair_far((i + o) % n, n)) for o in sides]
    got_e = [permute(out_e, lambda i, o=o: pair_near((i + o) % n)) for o in sides]
    got_b = permute(out_b, lambda i: pair_far(i, n))
    got_a = permute(out_a, pair_near)
    got_t = lax.all_to_all(out_t, "gx", split_axis=0, concat_axis=0, tiled=True)

    side = pl.pallas_call(
        functools.partial(side_kernel, n),
        out_shape=vmem(len(SIDES), EXT, LANES),
        in_specs=[on_core] * len(sides),
        out_specs=on_core,
        scratch_shapes=[pltpu.VMEM((16, LANES), F32)],
        compiler_params=pltpu.CompilerParams(vmem_limit_bytes=16 * 1024 * 1024),
        name="sides",
    )(*got_c)
    lines = pl.pallas_call(
        functools.partial(tile_kernel, n),
        out_shape=vmem(line_layout(n)[1], LANES),
        in_specs=[on_core],
        out_specs=on_core,
        scratch_shapes=[pltpu.VMEM((n * chunk, LANES), F32), pltpu.VMEM((16 * 32, LANES), BF16)],
        compiler_params=pltpu.CompilerParams(vmem_limit_bytes=40 * 1024 * 1024),
        name="tiles",
    )(got_t)
    outs = (velocity, stress, memory)
    return pl.pallas_call(
        functools.partial(wave_kernel, n),
        out_shape=[jax.ShapeDtypeStruct(x.shape, F32) for x in outs],
        in_specs=[on_core] * (15 + 3 * len(sides)),
        out_specs=[away] * 3,
        scratch_shapes=[
            pltpu.VMEM((CORNER, LANES), F32),
            pltpu.VMEM((CORNER, LANES), F32),
            pltpu.VMEM((16, LANES), F32),
        ]
        + [pltpu.VMEM(x.shape, F32) for x in outs]
        + [pltpu.SemaphoreType.DMA((3, 4))],
        compiler_params=pltpu.CompilerParams(vmem_limit_bytes=48 * 1024 * 1024),
        name="wave",
    )(*fields, held, side, later, own_map, got_a, got_b, lines, *got_c, *got_d, *got_e)


def solution(mesh):
    split = ("groups", "gx")
    whole = P(None, split, None, None, None)
    field = P(split, None, None, None)
    return jax.shard_map(
        body,
        mesh=mesh,
        in_specs=(whole,) * 3
        + (field,) * 5
        + (P(split, None),) * 3
        + (P(split), P(split, None), P(split), P(split, None)),
        out_specs=(whole,) * 3,
        check_vma=False,
    )
```

```python
import functools

import jax
import jax.numpy as jnp
from jax import lax
from jax.experimental import pallas as pl
from jax.experimental.pallas import tpu as pltpu
from jax.sharding import PartitionSpec as P

PY = 8
TY = 8
TZ = 8
courant = 0.25

F32 = jnp.float32
BF16 = jnp.bfloat16
XX, YY, ZZ, XY, XZ, YZ = range(6)
STRESS, VEL, HELD, GAIN, LAME, MU, BUOY = 0, 6, 9, 15, 16, 17, 18
FIELDS = 19
LAST = [("gx", 2), ("gx", 3), ("gy", 3), ("gz", 3), (STRESS + XY, 3), (STRESS + XZ, 3)]
LAST += [(VEL, 2), (VEL, 3), (VEL + 1, 3), (VEL + 2, 3), (BUOY, 2), (BUOY, 3)]
LAST += [(HELD + c, 3) for c in (XX, XY, XZ)] + [(GAIN, 3), (LAME, 3), (MU, 3)]
FIRST = [("gx", 0), ("gy", 0), ("gz", 0), ("gy", 1), ("gz", 1), (STRESS + XX, 0)]
FIRST += [(VEL, 0), (VEL + 1, 0), (VEL + 1, 1), (VEL + 2, 0), (VEL + 2, 1), (BUOY, 0), (BUOY, 1)]
FIRST += [(HELD + XX, 0), ("hy", 0), ("hz", 0), (GAIN, 0), (LAME, 0), (MU, 0)]
BELOW_LAST = [(STRESS + c, 3) for c in range(6) if c != ZZ] + [(VEL, 3), (VEL + 1, 3), (HELD + XY, 3), (GAIN, 3)]
BELOW_LAST = [(f, i, -1) for f, i in BELOW_LAST + [(MU, 3), (BUOY, 3), (STRESS + XY, 2)]] + [(STRESS + XY, 3, -2)]
ABOVE_LAST = [(STRESS + c, 3) for c in range(6)] + [(VEL, 3), (VEL + 2, 3), (HELD + XZ, 3), (GAIN, 3)]
ABOVE_LAST = [(f, i, 0) for f, i in ABOVE_LAST + [(MU, 3), (BUOY, 3), (STRESS + XZ, 2)]] + [(STRESS + XZ, 3, 1)]
BELOW_FIRST = [(STRESS + c, 0) for c in range(6)] + [(VEL + 1, 0), (VEL + 2, 0), (HELD + YZ, 0), (GAIN, 0)]
BELOW_FIRST = [(f, i, -1) for f, i in BELOW_FIRST + [(MU, 0), (BUOY, 0), (STRESS + YZ, 1)]] + [(STRESS + YZ, 0, -2)]
ABOVE_FIRST = [(STRESS + c, 0) for c in range(6)] + [(VEL + c, 0) for c in range(3)] + [(HELD + XX, 0), (HELD + YY, 0)]
ABOVE_FIRST += [(GAIN, 0), (LAME, 0), (MU, 0), (BUOY, 0), (STRESS + XX, 1), (STRESS + YY, 1)]
ABOVE_FIRST = [(f, i, 0) for f, i in ABOVE_FIRST] + [(STRESS + XX, 0, 1), (STRESS + YY, 0, 1)]
BELOW = BELOW_LAST + BELOW_FIRST
ABOVE = ABOVE_LAST + ABOVE_FIRST
ENDS = [(STRESS + YY, 0, 0), (STRESS + XY, 0, -1), (STRESS + YZ, 0, -1)]
ENDS += [("gy", 0, -1), (VEL + 1, 0, -1), (BUOY, 0, -1)]
ENDS += [(STRESS + YY, 3, 0), (STRESS + XY, 3, -1), (STRESS + YZ, 3, -1)]
ENDS += [("gx", 3, 0), (VEL, 3, 0), (BUOY, 3, 0)]
ENDS_MAP = 12
LONGEST = max(len(LAST), len(FIRST))
ROWS = 32
EXT = ROWS + 8
LANES = 128
BLOCK = FIELDS * 8 + 8
CORNER = -(-(max(len(BELOW), len(ABOVE)) + 1) // 16) * 16


def pair_near(i):
    return i ^ 1


def pair_far(i, n):
    return (i - 1) % n if i % 2 == 0 else (i + 1) % n


def is_merged(n):
    return n == 2 * PY


def sides_of(n):
    return [PY] if is_merged(n) else [-PY, PY]


def tile_offsets(n):
    return [k for o in [0] + sides_of(n) for k in (o, o + 1, o - 1)]


def tile_chunk(n):
    return -(-(9 + 7 * len(sides_of(n))) // 16) * 16


def roll(x, by, axis):
    size = x.shape[axis]
    by = by % size
    return x if by == 0 else pltpu.roll(x, by, axis)


def sublane(shape):
    return lax.broadcasted_iota(jnp.int32, shape, 0)


def lane(shape):
    return lax.broadcasted_iota(jnp.int32, shape, 1)


def z_after(a):
    return jnp.where(lane(a.shape) == LANES - 1, 0.0, roll(a, -1, 1))


def z_before(a):
    return jnp.where(lane(a.shape) == 0, 0.0, roll(a, 1, 1))


def place_sources(index, wave, step):
    count = index.shape[1]
    cells = jnp.broadcast_to(index[...], (LANES, count))
    place = sublane((LANES, count))
    rows = (lax.shift_right_logical(cells, 7) == place).astype(F32)
    at = ((cells & (LANES - 1)) == place).astype(F32)
    left = wave[step : step + 1, :]
    parts = []
    for _ in range(3):
        part = left.astype(BF16).astype(F32)
        parts.append((at * part).astype(BF16))
        left = left - part
    total = None
    for part in parts:
        done = lax.dot_general(rows.astype(BF16), part, (((1,), (1,)), ((), ())), preferred_element_type=F32)
        total = done if total is None else total + done
    return total


def pack_kernel(n, per, *refs):
    merged = is_merged(n)
    sides = len(sides_of(n))
    far_refs, outs, refs = refs[:15], refs[15 : 31 + sides], refs[31 + sides :]
    out_a, out_b, out_d, out_e, out_map, out_t = outs[:6]
    dec, los, st, mem, vel, lam, mu, bu = outs[6:14]
    held, later = outs[14:16]
    out_c = outs[16:]
    near_lam, near_mu, near_bu, near_dest, index, wave, tiles, sems = refs[:8]
    gain, source, corner, ends, routed, routed_out = refs[8:]
    near_refs = (near_lam, near_mu, near_bu, near_dest, dec, los, index, wave, st, mem, vel, lam, mu, bu, tiles)
    b = lax.axis_index("gx")
    even = lax.rem(b, 2) == 0
    first_x = b < PY
    top, bottom = slice(0, 8), slice(ROWS - 8, ROWS)
    copies = {}
    for k in (0, 1, 2, 3, 14, 6, 7, 8, 10, 13, 11, 12, 4, 5, 9):
        copies[k] = pltpu.make_async_copy(far_refs[k], near_refs[k], sems.at[k])
        copies[k].start()

    def arrive(*which):
        for k in which:
            copies[k].wait()

    arrive(0, 1, 2, 3)
    route_tiles(n, near_lam, near_mu, near_bu, near_dest, routed, routed_out)
    leave = pltpu.make_async_copy(routed_out, out_t, sems.at[15])
    leave.start()
    arrive(6, 7, 14)
    source[...] = place_sources(index, wave, 0)
    later[...] = place_sources(index, wave, 1)

    def get(f, i, rows=slice(None)):
        if f < VEL:
            return st[f, 0, i, rows]
        if f < HELD:
            return vel[f - VEL, 0, i, rows]
        if f < GAIN:
            return held[f - HELD, i, rows]
        if f == GAIN:
            return gain[i, rows]
        return (lam, mu, bu)[f - LAME][0, i, rows]

    sub = sublane((8, LANES))

    rows_z = LANES // TZ
    table = tiles[...]
    spots = table.shape[1]
    owner = jnp.where(table >= 0, jnp.floor((table.astype(F32) + 0.5) * (1.0 / per)) + 1.0, 0.0)
    spot = lane((8, spots))
    wide = jnp.where(spot // rows_z == sublane((8, spots)), jnp.broadcast_to(owner, (8, spots)), 0.0)
    spread = (lax.rem(sublane((spots, LANES)), rows_z) == lane((spots, LANES)) // TZ).astype(BF16)
    owners = jnp.dot(wide.astype(BF16), spread, preferred_element_type=F32) - 1.0
    out_map[...] = owners
    last = ROWS // TY - 1

    def prev_y(a):
        return jnp.where(sublane(a.shape) == 0, 0.0, roll(a, 1, 0))

    def next_y(a):
        return jnp.where(sublane(a.shape) == ROWS - 1, 0.0, roll(a, -1, 0))

    def sums(kind, i):
        def s(c, k):
            return held[c, k] if kind[0] == "h" else st[c, 0, k]

        def dy_prev(c):
            return s(c, i) - prev_y(s(c, i))

        def dy_next(c):
            return next_y(s(c, i)) - s(c, i)

        def dz_prev(c):
            return s(c, i) - z_before(s(c, i))

        def dz_next(c):
            return z_after(s(c, i)) - s(c, i)

        if kind == "gx":
            along = s(XX, i + 1) - s(XX, i) if i < 3 else -s(XX, i)
            return along + dy_prev(XY) + dz_prev(XZ)
        cross = XY if kind[1] == "y" else XZ
        along = s(cross, i) - s(cross, i - 1) if i > 0 else s(cross, i)
        if kind[1] == "y":
            return along + dy_next(YY) + dz_prev(YZ)
        return along + dy_prev(YZ) + dz_next(ZZ)

    def entry(f, i):
        return sums(f, i) if isinstance(f, str) else get(f, i)

    def edge_rows(f):
        if f == FIELDS:
            return jnp.broadcast_to(owners[0:1], (8, LANES)), jnp.broadcast_to(owners[last : last + 1], (8, LANES))
        lo, hi = get(f, 0, top), roll(get(f, 0, bottom), 2, 0)
        for i in range(1, 4):
            mine = sub // 2 == i
            lo = jnp.where(mine, roll(get(f, i, top), 2 * i, 0), lo)
            hi = jnp.where(mine, roll(get(f, i, bottom), 2 * i + 2, 0), hi)
        return lo, hi

    def write_edges(which):
        for f in which:
            lo, hi = edge_rows(f)
            out_a[f * 8 : f * 8 + 8, :] = jnp.where(even, hi, lo)
            out_b[f * 8 : f * 8 + 8, :] = jnp.where(even, lo, hi)

    def write_corner(rows, which, strip, at):
        for k, (f, i, r) in enumerate(rows):
            if f in which:
                corner[at + k : at + k + 1, :] = get(f, i, slice(r % ROWS, r % ROWS + 1))
        if FIELDS in which:
            corner[at + len(rows) : at + len(rows) + 1, :] = owners[strip : strip + 1]

    def write_layers(out, entries, which):
        for k, (f, i) in enumerate(entries):
            if f in which:
                out[k * ROWS : (k + 1) * ROWS, :] = entry(f, i).astype(BF16)

    def write_ends(which):
        for k, (f, i, r) in enumerate(ENDS):
            if f in which:
                row = slice(r % ROWS, r % ROWS + 1)
                ends[k : k + 1, :] = sums(f, i)[row] if isinstance(f, str) else get(f, i, row)

    def write(*which):
        write_edges([f for f in which if not isinstance(f, str)])
        write_corner(BELOW, which, last, 0)
        write_corner(ABOVE, which, 0, CORNER)
        write_ends(which)
        if merged:

            @pl.when(first_x)
            def _():
                write_layers(out_c[0], LAST, which)

            @pl.when(jnp.logical_not(first_x))
            def _():
                write_layers(out_c[0], FIRST, which)
        else:
            write_layers(out_c[0], LAST, which)
            write_layers(out_c[1], FIRST, which)

    corner[...] = jnp.zeros_like(corner)
    ends[ENDS_MAP : ENDS_MAP + last + 1, :] = owners[0 : last + 1]
    arrive(8)
    write(FIELDS, *range(STRESS, VEL), "gx", "gy", "gz")
    arrive(10, 13, 11, 12)
    write(*range(VEL, HELD), LAME, MU, BUOY)
    arrive(4, 5)
    for i in range(4):
        gain[i] = courant * (1.0 - (1.0 - dec[0, i]) * los[0, i])
    write(GAIN)
    arrive(9)
    for i in range(4):
        kept = courant * dec[0, i]
        for c in range(6):
            value = st[c, 0, i] + kept * mem[c, 0, i]
            if c < 3:
                value = value + source[i * ROWS : (i + 1) * ROWS, :]
            held[c, i] = value
    write(*range(HELD, GAIN), "hy", "hz")
    below, above = corner[0:CORNER, :].astype(BF16), corner[CORNER : 2 * CORNER, :].astype(BF16)
    out_e[...] = jnp.where(even, below, above)
    out_d[...] = jnp.where(even, above, below)
    for out, entries in zip(out_c, (LAST, FIRST)):
        if merged:
            base = LONGEST * ROWS

            @pl.when(first_x)
            def _():
                rest = (LONGEST - len(LAST)) * ROWS
                out[len(LAST) * ROWS : base, :] = jnp.zeros((rest, LANES), BF16)
        else:
            base = len(entries) * ROWS
        out[base : base + 16, :] = ends[...].astype(BF16)
    leave.wait()


def route_tiles(n, near_lam, near_mu, near_bu, near_dest, rows, out):
    offsets = tile_offsets(n)
    chunk = tile_chunk(n)
    per = near_lam.shape[0]
    total = n * len(offsets)
    at = lane((1, per))
    stored = jnp.full((1, per), -1, jnp.int32)
    for t in range(per):
        stored = jnp.where(at == t, near_dest[t], stored)
    row = sublane((total, per))
    brick = lax.rem(row, n)
    for k, off in enumerate(offsets):
        brick = jnp.where(row // n == k, brick + off % n, brick)
    brick = jnp.where(brick >= n, brick - n, brick)
    route = (brick == stored).astype(BF16)
    cell, spot = sublane((2 * LANES, LANES)), lane((2 * LANES, LANES))
    half = lax.rem(spot, 64)
    cells = half // 16 * 64 + lax.rem(half, 16)
    ends = (cell == cells + jnp.where(spot < 64, 0, 48)).astype(BF16)
    left = lane((n, LANES)) < 64
    if chunk > 9 + 7 * len(sides_of(n)):
        rows[...] = jnp.zeros_like(rows)

    def put(j, value):
        rows[pl.ds(j, n, stride=chunk), :] = value

    tiles = [near[...] for near in (near_lam, near_mu, near_bu)]
    stacked = jnp.concatenate([tile.astype(F32) for tile in tiles], 0).astype(BF16)
    halves = jnp.dot(stacked, ends, preferred_element_type=F32)
    for p, tile in enumerate(tiles):
        whole = jnp.dot(route, tile, preferred_element_type=F32)
        outer = halves[p * per : (p + 1) * per].astype(BF16)
        outer = jnp.dot(route, outer, preferred_element_type=F32)

        def slot(x, k):
            return x[k * n : (k + 1) * n]

        put(2 * p, slot(whole, 0)[:, :LANES])
        put(2 * p + 1, slot(whole, 0)[:, LANES:])
        put(6 + p, jnp.where(left, slot(outer, 1), slot(outer, 2)))
        for g in range(len(sides_of(n))):
            side = slot(whole, 3 + 3 * g)
            base = 9 + 7 * g
            if p < 2:
                put(base + p, jnp.where(left, side[:, :LANES], side[:, LANES:]))
            else:
                put(base + 2, side[:, :LANES])
                put(base + 3, side[:, LANES:])
            put(base + 4 + p, jnp.where(left, slot(outer, 4 + 3 * g), slot(outer, 5 + 3 * g)))
    out[...] = rows[...].astype(BF16)


def halo_blocks(even, near, far, f):
    x = near[f * 8 : f * 8 + 8, :]
    y = far[f * 8 : f * 8 + 8, :]
    return jnp.where(even, x, y), jnp.where(even, y, x)


def halo_rows(blocks, i):
    after, before = blocks
    sub = sublane((8, LANES))
    return jnp.where(sub < 2, roll(after, -2 * i, 0), roll(before, 6 - 2 * i, 0))


def side_messages(n, got_c):
    first_x = lax.axis_index("gx") < PY
    if is_merged(n):
        message, base = got_c[0], LONGEST * ROWS
        return [("before", LAST, message, base, jnp.logical_not(first_x)), ("after", FIRST, message, base, first_x)]
    return [
        (name, which, message, len(which) * ROWS, None)
        for name, which, message in (("before", LAST, got_c[0]), ("after", FIRST, got_c[1]))
    ]


def side_rows(which, message, whole, ends, f, i):
    k = which.index((f, i))
    main = message[k * ROWS : (k + 1) * ROWS, :].astype(F32)
    if whole is None:
        return main
    sub = sublane((8, LANES))
    only = [jnp.zeros((8, LANES), F32)] * (ROWS // 8)
    for e in (3, 4, 5, 9, 10, 11):
        if ENDS[e][:2] == (f, i):
            at = ENDS[e][2] % ROWS
            only[at // 8] = jnp.where(sub == at % 8, jnp.broadcast_to(ends[e : e + 1, :], (8, LANES)), 0.0)
    return jnp.where(whole, main, jnp.concatenate(only, 0))


PLAIN = GAIN + 1
SIDES = [("before", f, i) for f, i in LAST] + [("after", f, i) for f, i in FIRST]
SIDE_PROPS = [s for s in SIDES if s[1] in (LAME, MU, BUOY)]


def side_kernel(n, *refs):
    sides = len(sides_of(n))
    got_c, (side, ends) = refs[:sides], refs[sides:]
    sub = sublane((8, LANES))
    for name, which, message, base, whole in side_messages(n, got_c):
        ends[...] = message[base : base + 16, :].astype(F32)

        def end_row(f, i, r):
            at = ENDS.index((f, i, r))
            return jnp.broadcast_to(ends[at : at + 1, :], (8, LANES))

        edge = 3 if name == "before" else 0
        for f, i in which:
            k = SIDES.index((name, f, i))
            side[k, 0:ROWS] = side_rows(which, message, whole, ends, f, i)
            if isinstance(f, str):
                halo = jnp.zeros((8, LANES), F32)
                if i == edge and f == "gx":
                    halo = jnp.where(sub == 0, -end_row(STRESS + XY, i, -1), 0.0)
                if i == edge and f == "gy":
                    halo = jnp.where(sub == 7, end_row(STRESS + YY, i, 0), 0.0)
                if i == edge and f == "gz":
                    halo = jnp.where(sub == 0, -end_row(STRESS + YZ, i, -1), 0.0)
                side[k, ROWS:EXT] = halo


def tile_kernel(n, *refs):
    sides = len(sides_of(n))
    (lam, mu, bu, maps, got_t) = refs[:5]
    got_c = refs[5 : 5 + sides]
    own, side, corner, rows_t, spread_rows, tile_rows, ends = refs[5 + sides :]
    chunk = tile_chunk(n)
    rows_t[...] = got_t[...].astype(F32)
    on_line = lane((16, LANES)) // TZ == sublane((16, LANES))
    spread = (lax.rem(sublane((LANES, LANES)), TZ) == lax.rem(lane((LANES, LANES)), TZ)).astype(BF16)

    def lines(first, row, halves):
        for s in range(16):
            for h in range(halves):
                value = rows_t[pl.ds((first + s) * chunk + row + h, 1), :]
                value = jnp.where(on_line, jnp.broadcast_to(value, (16, LANES)), 0.0)
                at = (s * halves + h) * 16
                spread_rows[at : at + 16, :] = value.astype(BF16)
        return jnp.dot(spread_rows[0 : 256 * halves, :], spread, preferred_element_type=F32)

    def overlay(row, halves, wanted):
        def take(first, values):
            tile_rows[0 : 256 * halves, :] = lines(first, row, halves)
            done = []
            for value, (_, owner, at) in zip(values, wanted):
                for s in range(16):
                    here = tile_rows[s * halves * 16 + at : s * halves * 16 + at + 8, :]
                    value = jnp.where(owner == (first + s) * 1.0, here, value)
                done.append(value)
            return done

        values = [w[0] for w in wanted]
        if n == 16:
            return take(0, values)
        return lax.fori_loop(0, n // 16, lambda g, v: take(g * 16, v), values)

    rows_y = ROWS // TY

    def main_tiles(mains, owners, row, halves, line_of):
        wanted = []
        for i, m in mains.items():
            for p in range(rows_y):
                owner = jnp.broadcast_to(owners[p : p + 1], (8, LANES))
                wanted.append((m[p * 8 : (p + 1) * 8], owner, line_of(i)))
        laid = overlay(row, halves, wanted)
        return {i: jnp.concatenate(laid[k * rows_y : (k + 1) * rows_y], 0) for k, i in enumerate(mains)}

    for p, ref in enumerate((lam, mu, bu)):
        main = main_tiles({i: ref[0, i] for i in range(4)}, maps[...], 2 * p, 2, lambda i: i * 8)
        for i in range(4):
            own[p, i] = main[i]
    for at, (name, which, message, base, whole) in enumerate(side_messages(n, got_c)):
        group = 0 if whole is not None else at
        ends[...] = message[base : base + 16, :].astype(F32)
        owners = ends[8:16, :][ENDS_MAP - 8 :]
        row = 9 + 7 * group
        for f in (LAME, MU, BUOY):
            main = {i: side_rows(which, message, whole, ends, f, i) for g, i in which if g == f}
            if f == BUOY:
                main = main_tiles(main, owners, row + 2, 2, lambda i: i * 8)
            else:
                main = main_tiles(main, owners, row + f - LAME, 1, lambda i: 8 if i else 0)
            for i, value in main.items():
                side[SIDE_PROPS.index((name, f, i))] = value
    for g in range(1 + sides):
        for p in range(3):
            row = 6 + 7 * g + p
            if n == 16:
                corner[3 * g + p] = lines(0, row, 1)
            else:

                def spread_group(q, _, g=g, p=p, row=row):
                    corner[3 * g + p, pl.ds(q * 256, 256)] = lines(q * 16, row, 1)
                    return 0

                lax.fori_loop(0, n // 16, spread_group, 0)


def rules(n, lame, shear, buoy):
    b = lax.axis_index("gx")

    tall = sublane((EXT, LANES))

    def linked(test):
        def of(step):
            q = lax.rem(b + step + n, n)
            return jnp.where(test(q), 1, 0)

        flags = jnp.where(tall < ROWS, of(0), jnp.where(tall < ROWS + 4, of(1), of(-1)))
        return flags == 1

    link_before = linked(lambda q: q >= PY)
    link_after = linked(lambda q: q < n - PY)

    def x_next(a, l, across=None):
        if l == 1:
            return jnp.where(link_before, a[2], 0.0)
        if l == 5:
            return jnp.where(link_after, a[6] if across is None else across, 0.0)
        return a[l + 1]

    def x_prev(a, l, across=None):
        if l == 2:
            return jnp.where(link_before, a[1] if across is None else across, 0.0)
        if l == 6:
            return jnp.where(link_after, a[5], 0.0)
        return a[l - 1]

    def y_next(a):
        return roll(a, -1, 0)

    def y_prev(a):
        return roll(a, 1, 0)

    z_next, z_prev = z_after, z_before

    def move(new, v, s, l, spans, sums, faces):
        def add(d, grad):
            if sums[d][l] is not None:
                grad = sums[d][l] + grad
            new[d][l] = v[d][l] + courant * buoy[l] * grad

        if l in spans[0]:
            ahead = x_next(s[XX], l, faces.get(XX))
            add(0, (ahead - s[XX][l]) + (s[XY][l] - y_prev(s[XY][l])) + (s[XZ][l] - z_prev(s[XZ][l])))
        if l in spans[1]:
            behind = x_prev(s[XY], l, faces.get(XY))
            add(1, (s[XY][l] - behind) + (y_next(s[YY][l]) - s[YY][l]) + (s[YZ][l] - z_prev(s[YZ][l])))
            behind = x_prev(s[XZ], l, faces.get(XZ))
            add(2, (s[XZ][l] - behind) + (s[YZ][l] - y_prev(s[YZ][l])) + (z_next(s[ZZ][l]) - s[ZZ][l]))

    def rates_at(v, l, wanted):
        out = [None] * 6
        ex = v[0][l] - x_prev(v[0], l)
        ey = v[1][l] - y_prev(v[1][l])
        ez = v[2][l] - z_prev(v[2][l])
        spread_part = lame[l] * (ex + ey + ez)
        twice = 2.0 * shear[l]
        for c, e in ((XX, ex), (YY, ey), (ZZ, ez)):
            if c in wanted:
                out[c] = spread_part + twice * e
        if XY in wanted:
            out[XY] = shear[l] * ((y_next(v[0][l]) - v[0][l]) + (x_next(v[1], l) - v[1][l]))
        if XZ in wanted:
            out[XZ] = shear[l] * ((z_next(v[0][l]) - v[0][l]) + (x_next(v[2], l) - v[2][l]))
        if YZ in wanted:
            out[YZ] = shear[l] * ((z_next(v[1][l]) - v[1][l]) + (y_next(v[2][l]) - v[2][l]))
        return out

    return move, rates_at, link_before, link_after


def tile_rows_around(n, line_tiles, group, after, before):
    laid = []
    for p in range(3):
        low = high = jnp.zeros((8, LANES), F32)
        for s in range(n):
            low = jnp.where(after == s * 1.0, line_tiles[3 * group + p, s * 16 : s * 16 + 8], low)
            high = jnp.where(before == s * 1.0, line_tiles[3 * group + p, s * 16 + 8 : s * 16 + 16], high)
        laid.append((low, high))
    return laid, jnp.where(sublane((8, LANES)) < 4, after, before) >= 0.0


OUTER = (2, 5)
INNER = (3, 4)


def first_kernel(n, *refs):
    (vel, st, mem, dec, los, kept, side, own_props, line_tiles, got_a, got_b) = refs[:11]
    out_props, out_gain, out_held, out_cross, out_v, out_s, out_m = refs[11:]
    even = lax.rem(lax.axis_index("gx"), 2) == 0
    laid, covered = tile_rows_around(n, line_tiles, 0, *halo_blocks(even, got_a, got_b, FIELDS))
    column = {}
    for f in range(FIELDS):
        blocks = halo_blocks(even, got_a, got_b, f)
        for i in range(4):
            halo = halo_rows(blocks, i)
            if f >= LAME:
                halo = jnp.where(covered, halo_rows(laid[f - LAME], i), halo)
            if f < VEL:
                main = st[f, 0, i]
            elif f < HELD:
                main = vel[f - VEL, 0, i]
            elif f < GAIN:
                main = kept[f - HELD, i]
            elif f == GAIN:
                main = courant * (1.0 - (1.0 - dec[0, i]) * los[0, i])
            else:
                main = own_props[f - LAME, i]
            column[f, i] = jnp.concatenate([main, halo], 0)

    def layers_of(f):
        return [None, None] + [column[f, i] for i in range(4)] + [None, None]

    def face_of(name, c, i):
        return jnp.concatenate([side[SIDES.index((name, STRESS + c, i)), 0:ROWS], jnp.zeros((8, LANES), F32)], 0)

    s0 = [layers_of(STRESS + c) for c in range(6)]
    v0 = [layers_of(VEL + c) for c in range(3)]
    held = [layers_of(HELD + c) for c in range(6)]
    gain, lame, shear, buoy = (layers_of(f) for f in (GAIN, LAME, MU, BUOY))
    move, rates_at, _, _ = rules(n, lame, shear, buoy)
    faces = {XX: face_of("after", XX, 0), XY: face_of("before", XY, 3), XZ: face_of("before", XZ, 3)}
    v1 = [[None] * 8 for _ in range(3)]
    for l in range(2, 6):
        move(v1, v0, s0, l, (range(2, 6), range(2, 6)), [[None] * 8] * 3, faces)
        for c in range(3):
            out_v[c, l - 2] = v1[c][l]
        out_gain[l - 2] = gain[l]
        for p, values in enumerate((lame, shear, buoy)):
            out_props[p, l - 2] = values[l]
    for k, l in enumerate(OUTER):
        for c in range(6):
            out_held[c, k] = held[c][l]
    for k, value in enumerate((s0[XX][2], s0[XY][5], s0[XZ][5])):
        out_cross[k] = value
    for k, l in enumerate(INNER):
        i = l - 2
        rates = rates_at(v1, l, range(6))
        lost = (1.0 - dec[0, i]) * los[0, i]
        for c in range(6):
            out_s[c, k] = held[c][l] + gain[l] * rates[c]
            out_m[c, k] = dec[0, i] * mem[c, 0, i] - lost * rates[c][:ROWS]


def wave_kernel(n, *refs):
    merged = is_merged(n)
    sides = len(sides_of(n))
    (mem, dec, los, side, source, side_props, line_tiles) = refs[:7]
    (own_props, own_gain, own_held, cross, own_v, own_s, own_m) = refs[7:14]
    got_d, got_e = refs[14 : 14 + sides], refs[14 + sides : 14 + 2 * sides]
    refs = refs[14 + 2 * sides :]
    far_outs, (near_rows, far_rows, new_v, new_s, new_m, sems) = refs[:3], refs[3:]
    even = lax.rem(lax.axis_index("gx"), 2) == 0
    sub = sublane((8, LANES))
    no_rows, no_halo = jnp.zeros((ROWS, LANES), F32), jnp.zeros((8, LANES), F32)

    column = {}
    for i in range(4):
        column["own", GAIN, i] = own_gain[i]
        for p in range(3):
            column["own", LAME + p, i] = own_props[p, i]
    for k, l in enumerate(OUTER):
        for c in range(6):
            column["own", HELD + c, l - 2] = own_held[c, k]
    for k, (c, i) in enumerate(((XX, 0), (XY, 3), (XZ, 3))):
        column["own", STRESS + c, i] = cross[k]

    def corner_rows(table, rows, f, i):
        value = None
        for k, (g, j, r) in enumerate(rows):
            if (g, j) == (f, i):
                row = jnp.broadcast_to(table[k : k + 1, :], (8, LANES))
                value = jnp.where(sub == (r % 8), row, 0.0 if value is None else value)
        return value

    face = {}
    for at, (name, which) in enumerate((("before", LAST), ("after", FIRST))):
        group = 0 if merged else at
        if group == at:
            near, far = got_e[group][...].astype(F32), got_d[group][...].astype(F32)
            near_rows[...] = jnp.where(even, near, far)
            far_rows[...] = jnp.where(even, far, near)
            after = jnp.broadcast_to(near_rows[len(ABOVE) : len(ABOVE) + 1, :], (8, LANES))
            before = jnp.broadcast_to(far_rows[len(BELOW) : len(BELOW) + 1, :], (8, LANES))
            laid, covered = tile_rows_around(n, line_tiles, 1 + group, after, before)

        def corner_halo(f, i):
            above = corner_rows(near_rows, ABOVE, f, i)
            below = corner_rows(far_rows, BELOW, f, i)
            if above is None or below is None:
                halo = no_halo if above is below else (below if above is None else above)
            else:
                halo = jnp.where(sub < 4, above, below)
            if f >= LAME:
                halo = jnp.where(covered, halo_rows(laid[f - LAME], i), halo)
            return halo

        edge = 3 if name == "before" else 0
        layers = (2, 3) if name == "before" else (0, 1)
        for f in range(FIELDS):
            for i in layers:
                if not (f < VEL or f in range(HELD, GAIN) or (f, i) in which):
                    continue
                halo = corner_halo(f, i)
                main = no_rows
                if f >= LAME:
                    main = side_props[SIDE_PROPS.index((name, f, i))]
                elif (f, i) in which:
                    main = side[SIDES.index((name, f, i)), 0:ROWS]
                if f < VEL:
                    column[name, f, i] = jnp.concatenate([no_rows, halo], 0)
                    if (f, i) in which:
                        face[name, f] = jnp.concatenate([main, halo], 0)
                else:
                    column[name, f, i] = jnp.concatenate([main, halo], 0)
        for f, i in which:
            if isinstance(f, str):
                column[name, f, i] = side[SIDES.index((name, f, i))]

    def layers_of(f):
        names = [("before", 2), ("before", 3)] + [("own", i) for i in range(4)] + [("after", 0), ("after", 1)]
        return [column.get((name, f, i)) for name, i in names]

    s0 = [layers_of(STRESS + c) for c in range(6)]
    v0 = [layers_of(VEL + c) for c in range(3)]
    held = [layers_of(HELD + c) for c in range(6)]
    gain, lame, shear, buoy = (layers_of(f) for f in (GAIN, LAME, MU, BUOY))

    move, rates_at, link_before, link_after = rules(n, lame, shear, buoy)
    faces = {XX: face["after", STRESS + XX], XY: face["before", STRESS + XY], XZ: face["before", STRESS + XZ]}
    faces = {XX: face["after", STRESS + XX], XY: face["before", STRESS + XY], XZ: face["before", STRESS + XZ]}
    copies = []

    def send(k, i):
        near, far = (new_v, new_s, new_m)[k], far_outs[k]
        copies.append(pltpu.make_async_copy(near.at[:, :, i], far.at[:, :, i], sems.at[k, i]))
        copies[-1].start()

    v1, v2 = ([[None] * 8 for _ in range(3)] for _ in range(2))
    s1 = [[None] * 8 for _ in range(6)]
    m1 = {}
    sums1 = [layers_of(g) for g in ("gx", "gy", "gz")]
    sums2 = [layers_of(h) for h in (None, "hy", "hz")]
    for l in range(2, 6):
        for c in range(3):
            v1[c][l] = own_v[c, l - 2]
    for k, l in enumerate(INNER):
        for c in range(6):
            s1[c][l] = own_s[c, k]
            m1[c, l] = own_m[c, k]

    def at_corner(d, l, link, sign, c):
        more = sign * courant * buoy[l][ROWS:] * jnp.where(link[ROWS:], faces[c][ROWS:], 0.0)
        v1[d][l] = jnp.concatenate([v1[d][l][:ROWS], v1[d][l][ROWS:] + more], 0)

    at_corner(0, 5, link_after, 1.0, XX)
    at_corner(1, 2, link_before, -1.0, XY)
    at_corner(2, 2, link_before, -1.0, XZ)
    for at in range(9):
        move(v1, v0, s0, at, ((0, 1, 6), (1, 6, 7)), sums1, {})
        l = at - 1
        if l in (1, 2, 5, 6):
            wanted = (XX, XY, XZ) if l == 1 else range(6)
            rates = rates_at(v1, l, wanted)
            for c in wanted:
                s1[c][l] = held[c][l] + gain[l] * rates[c]
                if 2 <= l < 6:
                    i = l - 2
                    lost = (1.0 - dec[0, i]) * los[0, i]
                    m1[c, l] = dec[0, i] * mem[c, 0, i] - lost * rates[c][:ROWS]
        l = at - 2
        move(v2, v1, s1, l, (range(1, 6), range(2, 7)), sums2, {})
        if l in range(2, 6):
            for c in range(3):
                new_v[c, 0, l - 2] = v2[c][l][:ROWS]
            send(0, l - 2)
        l = at - 3
        if l in range(2, 6):
            i = l - 2
            rates = rates_at(v2, l, range(6))
            d = dec[0, i]
            lost = (1.0 - d) * los[0, i]
            for c in range(6):
                rate = rates[c][:ROWS]
                m2 = d * m1[c, l] - lost * rate
                new_m[c, 0, i] = m2
                value = s1[c][l][:ROWS] + courant * (rate + m2)
                if c < 3:
                    value = value + source[i * ROWS : (i + 1) * ROWS, :]
                new_s[c, 0, i] = value
            send(1, i)
            send(2, i)
    for copy in copies:
        copy.wait()


def body(
    velocity,
    stress,
    memory,
    lame_lambda,
    lame_mu,
    buoyancy,
    decay,
    loss,
    tile_lambda,
    tile_mu,
    tile_buoy,
    tile_dest,
    brick_tiles,
    src_index,
    src_wave,
):
    n = lax.axis_size("gx")
    merged = is_merged(n)
    sides = sides_of(n)
    chunk = tile_chunk(n)
    on_core = pl.BlockSpec(memory_space=pltpu.VMEM)
    away = pl.BlockSpec(memory_space=pltpu.HBM)
    def vmem(*shape):
        return jax.ShapeDtypeStruct(shape, F32)

    waves = src_wave.T
    cells = src_index[None, :]
    fields = (velocity, stress, memory, lame_lambda, lame_mu, buoyancy, decay, loss)
    if merged:
        c_rows = [LONGEST * ROWS + 16]
    else:
        c_rows = [len(LAST) * ROWS + 16, len(FIRST) * ROWS + 16]
    tiles = (tile_lambda, tile_mu, tile_buoy)
    kept = (decay, loss, stress, memory, velocity, lame_lambda, lame_mu, buoyancy)
    inputs = (*tiles, tile_dest, decay, loss, cells, waves, stress, memory, velocity, lame_lambda, lame_mu, buoyancy, brick_tiles)
    inputs = tuple(pltpu.with_memory_space_constraint(x, pltpu.HBM) for x in inputs)
    packed = pl.pallas_call(
        functools.partial(pack_kernel, n, tile_lambda.shape[0]),
        out_shape=[
            jax.ShapeDtypeStruct((BLOCK, LANES), F32),
            jax.ShapeDtypeStruct((BLOCK, LANES), F32),
            jax.ShapeDtypeStruct((CORNER, LANES), BF16),
            jax.ShapeDtypeStruct((CORNER, LANES), BF16),
            jax.ShapeDtypeStruct((8, LANES), F32),
            jax.ShapeDtypeStruct((n * chunk, LANES), BF16),
        ]
        + [jax.ShapeDtypeStruct(x.shape, x.dtype) for x in kept]
        + [vmem(6, 4, ROWS, LANES), vmem(4 * ROWS, LANES)]
        + [jax.ShapeDtypeStruct((r, LANES), BF16) for r in c_rows],
        in_specs=[away] * len(inputs),
        out_specs=[on_core] * 5 + [away] + [on_core] * (10 + len(c_rows)),
        scratch_shapes=[
            pltpu.SMEM(x.shape, x.dtype) if x.ndim == 1 else pltpu.VMEM(x.shape, x.dtype)
            for x in (*tiles, tile_dest, cells, waves, brick_tiles)
        ]
        + [
            pltpu.SemaphoreType.DMA((16,)),
            pltpu.VMEM((4, ROWS, LANES), F32),
            pltpu.VMEM((4 * ROWS, LANES), F32),
            pltpu.VMEM((2 * CORNER, LANES), F32),
            pltpu.VMEM((16, LANES), F32),
            pltpu.VMEM((n * chunk, LANES), F32),
            pltpu.VMEM((n * chunk, LANES), BF16),
        ],
        compiler_params=pltpu.CompilerParams(vmem_limit_bytes=16 * 1024 * 1024),
        name="pack",
    )(*inputs)
    out_a, out_b, out_d, out_e, own_map, out_t = packed[:6]
    held, later = packed[14:16]
    out_c = packed[16:]
    dec, los, st, mem, vel, lam, mu, bu = packed[6:14]

    def permute(array, source_of):
        return lax.ppermute(array, "gx", [(source_of(i), i) for i in range(n)])

    got_c = [permute(c, lambda i, o=o: (i + o) % n) for c, o in zip(out_c, sides)]
    got_d = [permute(out_d, lambda i, o=o: pair_far((i + o) % n, n)) for o in sides]
    got_e = [permute(out_e, lambda i, o=o: pair_near((i + o) % n)) for o in sides]
    got_b = permute(out_b, lambda i: pair_far(i, n))
    got_a = permute(out_a, pair_near)
    got_t = lax.all_to_all(out_t, "gx", split_axis=0, concat_axis=0, tiled=True)

    side = pl.pallas_call(
        functools.partial(side_kernel, n),
        out_shape=vmem(len(SIDES), EXT, LANES),
        in_specs=[on_core] * len(sides),
        out_specs=on_core,
        scratch_shapes=[pltpu.VMEM((16, LANES), F32)],
        compiler_params=pltpu.CompilerParams(vmem_limit_bytes=16 * 1024 * 1024),
        name="sides",
    )(*got_c)
    own_props, side_props, line_tiles = pl.pallas_call(
        functools.partial(tile_kernel, n),
        out_shape=[
            vmem(3, 4, ROWS, LANES),
            vmem(len(SIDE_PROPS), ROWS, LANES),
            vmem(3 + 3 * len(sides), n * 16, LANES),
        ],
        in_specs=[on_core] * (5 + len(sides)),
        out_specs=[on_core] * 3,
        scratch_shapes=[
            pltpu.VMEM((n * chunk, LANES), F32),
            pltpu.VMEM((16 * 32, LANES), BF16),
            pltpu.VMEM((16 * 32, LANES), F32),
            pltpu.VMEM((16, LANES), F32),
        ],
        compiler_params=pltpu.CompilerParams(vmem_limit_bytes=16 * 1024 * 1024),
        name="tiles",
    )(lam, mu, bu, own_map, got_t, *got_c)
    first = pl.pallas_call(
        functools.partial(first_kernel, n),
        out_shape=[
            vmem(3, 4, EXT, LANES),
            vmem(4, EXT, LANES),
            vmem(6, 2, EXT, LANES),
            vmem(3, EXT, LANES),
            vmem(3, 4, EXT, LANES),
            vmem(6, 2, EXT, LANES),
            vmem(6, 2, ROWS, LANES),
        ],
        in_specs=[on_core] * 11,
        out_specs=[on_core] * 7,
        compiler_params=pltpu.CompilerParams(vmem_limit_bytes=16 * 1024 * 1024),
        name="first",
    )(vel, st, mem, dec, los, held, side, own_props, line_tiles, got_a, got_b)
    outs = (velocity, stress, memory)
    return pl.pallas_call(
        functools.partial(wave_kernel, n),
        out_shape=[jax.ShapeDtypeStruct(x.shape, F32) for x in outs],
        in_specs=[on_core] * (14 + 2 * len(sides)),
        out_specs=[away] * 3,
        scratch_shapes=[
            pltpu.VMEM((CORNER, LANES), F32),
            pltpu.VMEM((CORNER, LANES), F32),
        ]
        + [pltpu.VMEM(x.shape, F32) for x in outs]
        + [pltpu.SemaphoreType.DMA((3, 4))],
        compiler_params=pltpu.CompilerParams(vmem_limit_bytes=48 * 1024 * 1024),
        name="wave",
    )(mem, dec, los, side, later, side_props, line_tiles, *first, *got_d, *got_e)


def solution(mesh):
    split = ("groups", "gx")
    whole = P(None, split, None, None, None)
    field = P(split, None, None, None)
    return jax.shard_map(
        body,
        mesh=mesh,
        in_specs=(whole,) * 3
        + (field,) * 5
        + (P(split, None),) * 3
        + (P(split), P(split, None), P(split), P(split, None)),
        out_specs=(whole,) * 3,
        check_vma=False,
    )
```

```python
import functools

import jax
import jax.numpy as jnp
from jax import lax
from jax.experimental import pallas as pl
from jax.experimental.pallas import tpu as pltpu
from jax.sharding import PartitionSpec as P

PY = 8
TY = 8
TZ = 8
courant = 0.25

F32 = jnp.float32
BF16 = jnp.bfloat16
XX, YY, ZZ, XY, XZ, YZ = range(6)
STRESS, VEL, HELD, GAIN, LAME, MU, BUOY = 0, 6, 9, 15, 16, 17, 18
FIELDS = 19
LAST = [("gx", 2), ("gx", 3), ("gy", 3), ("gz", 3), (STRESS + XY, 3), (STRESS + XZ, 3)]
LAST += [(VEL, 2), (VEL, 3), (VEL + 1, 3), (VEL + 2, 3), (BUOY, 2), (BUOY, 3)]
LAST += [(HELD + c, 3) for c in (XX, XY, XZ)] + [(GAIN, 3), (LAME, 3), (MU, 3)]
FIRST = [("gx", 0), ("gy", 0), ("gz", 0), ("gy", 1), ("gz", 1), (STRESS + XX, 0)]
FIRST += [(VEL, 0), (VEL + 1, 0), (VEL + 1, 1), (VEL + 2, 0), (VEL + 2, 1), (BUOY, 0), (BUOY, 1)]
FIRST += [(HELD + XX, 0), ("hy", 0), ("hz", 0), (GAIN, 0), (LAME, 0), (MU, 0)]
BELOW_LAST = [(STRESS + c, 3) for c in range(6) if c != ZZ] + [(VEL, 3), (VEL + 1, 3), (HELD + XY, 3), (GAIN, 3)]
BELOW_LAST = [(f, i, -1) for f, i in BELOW_LAST + [(MU, 3), (BUOY, 3), (STRESS + XY, 2)]] + [(STRESS + XY, 3, -2)]
ABOVE_LAST = [(STRESS + c, 3) for c in range(6)] + [(VEL, 3), (VEL + 2, 3), (HELD + XZ, 3), (GAIN, 3)]
ABOVE_LAST = [(f, i, 0) for f, i in ABOVE_LAST + [(MU, 3), (BUOY, 3), (STRESS + XZ, 2)]] + [(STRESS + XZ, 3, 1)]
BELOW_FIRST = [(STRESS + c, 0) for c in range(6)] + [(VEL + 1, 0), (VEL + 2, 0), (HELD + YZ, 0), (GAIN, 0)]
BELOW_FIRST = [(f, i, -1) for f, i in BELOW_FIRST + [(MU, 0), (BUOY, 0), (STRESS + YZ, 1)]] + [(STRESS + YZ, 0, -2)]
ABOVE_FIRST = [(STRESS + c, 0) for c in range(6)] + [(VEL + c, 0) for c in range(3)] + [(HELD + XX, 0), (HELD + YY, 0)]
ABOVE_FIRST += [(GAIN, 0), (LAME, 0), (MU, 0), (BUOY, 0), (STRESS + XX, 1), (STRESS + YY, 1)]
ABOVE_FIRST = [(f, i, 0) for f, i in ABOVE_FIRST] + [(STRESS + XX, 0, 1), (STRESS + YY, 0, 1)]
BELOW = BELOW_LAST + BELOW_FIRST
ABOVE = ABOVE_LAST + ABOVE_FIRST
ENDS = [(STRESS + YY, 0, 0), (STRESS + XY, 0, -1), (STRESS + YZ, 0, -1)]
ENDS += [("gy", 0, -1), (VEL + 1, 0, -1), (BUOY, 0, -1)]
ENDS += [(STRESS + YY, 3, 0), (STRESS + XY, 3, -1), (STRESS + YZ, 3, -1)]
ENDS += [("gx", 3, 0), (VEL, 3, 0), (BUOY, 3, 0)]
ENDS_MAP = 12
LONGEST = max(len(LAST), len(FIRST))
ROWS = 32
EXT = ROWS + 8
LANES = 128
BLOCK = FIELDS * 8 + 8
CORNER = -(-(max(len(BELOW), len(ABOVE)) + 1) // 16) * 16


def pair_near(i):
    return i ^ 1


def pair_far(i, n):
    return (i - 1) % n if i % 2 == 0 else (i + 1) % n


def is_merged(n):
    return n == 2 * PY


def sides_of(n):
    return [PY] if is_merged(n) else [-PY, PY]


def tile_offsets(n):
    return [k for o in [0] + sides_of(n) for k in (o, o + 1, o - 1)]


def tile_chunk(n):
    return -(-(9 + 7 * len(sides_of(n))) // 16) * 16


def roll(x, by, axis):
    size = x.shape[axis]
    by = by % size
    return x if by == 0 else pltpu.roll(x, by, axis)


def sublane(shape):
    return lax.broadcasted_iota(jnp.int32, shape, 0)


def lane(shape):
    return lax.broadcasted_iota(jnp.int32, shape, 1)


def z_after(a):
    return jnp.where(lane(a.shape) == LANES - 1, 0.0, roll(a, -1, 1))


def z_before(a):
    return jnp.where(lane(a.shape) == 0, 0.0, roll(a, 1, 1))


def place_sources(index, wave, step):
    count = index.shape[1]
    cells = jnp.broadcast_to(index[...], (LANES, count))
    place = sublane((LANES, count))
    rows = (lax.shift_right_logical(cells, 7) == place).astype(F32)
    at = ((cells & (LANES - 1)) == place).astype(F32)
    left = wave[step : step + 1, :]
    parts = []
    for _ in range(3):
        part = left.astype(BF16).astype(F32)
        parts.append((at * part).astype(BF16))
        left = left - part
    total = None
    for part in parts:
        done = lax.dot_general(rows.astype(BF16), part, (((1,), (1,)), ((), ())), preferred_element_type=F32)
        total = done if total is None else total + done
    return total


def pack_kernel(n, per, *refs):
    merged = is_merged(n)
    sides = len(sides_of(n))
    far_refs, outs, refs = refs[:15], refs[15 : 31 + sides], refs[31 + sides :]
    out_a, out_b, out_d, out_e, out_map, out_t = outs[:6]
    dec, los, st, mem, vel, lam, mu, bu = outs[6:14]
    held, later = outs[14:16]
    out_c = outs[16:]
    near_lam, near_mu, near_bu, near_dest, index, wave, tiles, sems = refs[:8]
    gain, source, corner, ends, routed, routed_out = refs[8:]
    near_refs = (near_lam, near_mu, near_bu, near_dest, dec, los, index, wave, st, mem, vel, lam, mu, bu, tiles)
    b = lax.axis_index("gx")
    even = lax.rem(b, 2) == 0
    first_x = b < PY
    top, bottom = slice(0, 8), slice(ROWS - 8, ROWS)
    copies = {}
    for k in (0, 1, 2, 3, 14, 6, 7, 8, 10, 13, 11, 12, 4, 5, 9):
        copies[k] = pltpu.make_async_copy(far_refs[k], near_refs[k], sems.at[k])
        copies[k].start()

    def arrive(*which):
        for k in which:
            copies[k].wait()

    arrive(0, 1, 2, 3, 6, 7, 14)
    route_tiles(n, near_lam, near_mu, near_bu, near_dest, routed, routed_out)
    source[...] = place_sources(index, wave, 0)
    later[...] = place_sources(index, wave, 1)

    def get(f, i, rows=slice(None)):
        if f < VEL:
            return st[f, 0, i, rows]
        if f < HELD:
            return vel[f - VEL, 0, i, rows]
        if f < GAIN:
            return held[f - HELD, i, rows]
        if f == GAIN:
            return gain[i, rows]
        return (lam, mu, bu)[f - LAME][0, i, rows]

    sub = sublane((8, LANES))

    rows_z = LANES // TZ
    table = tiles[...]
    spots = table.shape[1]
    owner = jnp.where(table >= 0, jnp.floor((table.astype(F32) + 0.5) * (1.0 / per)) + 1.0, 0.0)
    spot = lane((8, spots))
    wide = jnp.where(spot // rows_z == sublane((8, spots)), jnp.broadcast_to(owner, (8, spots)), 0.0)
    spread = (lax.rem(sublane((spots, LANES)), rows_z) == lane((spots, LANES)) // TZ).astype(BF16)
    owners = jnp.dot(wide.astype(BF16), spread, preferred_element_type=F32) - 1.0
    out_map[...] = owners
    last = ROWS // TY - 1

    def prev_y(a):
        return jnp.where(sublane(a.shape) == 0, 0.0, roll(a, 1, 0))

    def next_y(a):
        return jnp.where(sublane(a.shape) == ROWS - 1, 0.0, roll(a, -1, 0))

    def sums(kind, i):
        def s(c, k):
            return held[c, k] if kind[0] == "h" else st[c, 0, k]

        def dy_prev(c):
            return s(c, i) - prev_y(s(c, i))

        def dy_next(c):
            return next_y(s(c, i)) - s(c, i)

        def dz_prev(c):
            return s(c, i) - z_before(s(c, i))

        def dz_next(c):
            return z_after(s(c, i)) - s(c, i)

        if kind == "gx":
            along = s(XX, i + 1) - s(XX, i) if i < 3 else -s(XX, i)
            return along + dy_prev(XY) + dz_prev(XZ)
        cross = XY if kind[1] == "y" else XZ
        along = s(cross, i) - s(cross, i - 1) if i > 0 else s(cross, i)
        if kind[1] == "y":
            return along + dy_next(YY) + dz_prev(YZ)
        return along + dy_prev(YZ) + dz_next(ZZ)

    def entry(f, i):
        return sums(f, i) if isinstance(f, str) else get(f, i)

    def edge_rows(f):
        if f == FIELDS:
            return jnp.broadcast_to(owners[0:1], (8, LANES)), jnp.broadcast_to(owners[last : last + 1], (8, LANES))
        lo, hi = get(f, 0, top), roll(get(f, 0, bottom), 2, 0)
        for i in range(1, 4):
            mine = sub // 2 == i
            lo = jnp.where(mine, roll(get(f, i, top), 2 * i, 0), lo)
            hi = jnp.where(mine, roll(get(f, i, bottom), 2 * i + 2, 0), hi)
        return lo, hi

    def write_edges(which):
        for f in which:
            lo, hi = edge_rows(f)
            out_a[f * 8 : f * 8 + 8, :] = jnp.where(even, hi, lo)
            out_b[f * 8 : f * 8 + 8, :] = jnp.where(even, lo, hi)

    def write_corner(rows, which, strip, at):
        for k, (f, i, r) in enumerate(rows):
            if f in which:
                corner[at + k : at + k + 1, :] = get(f, i, slice(r % ROWS, r % ROWS + 1))
        if FIELDS in which:
            corner[at + len(rows) : at + len(rows) + 1, :] = owners[strip : strip + 1]

    def write_layers(out, entries, which):
        for k, (f, i) in enumerate(entries):
            if f in which:
                out[k * ROWS : (k + 1) * ROWS, :] = entry(f, i).astype(BF16)

    def write_ends(which):
        for k, (f, i, r) in enumerate(ENDS):
            if f in which:
                row = slice(r % ROWS, r % ROWS + 1)
                ends[k : k + 1, :] = sums(f, i)[row] if isinstance(f, str) else get(f, i, row)

    def write(*which):
        write_edges([f for f in which if not isinstance(f, str)])
        write_corner(BELOW, which, last, 0)
        write_corner(ABOVE, which, 0, CORNER)
        write_ends(which)
        if merged:

            @pl.when(first_x)
            def _():
                write_layers(out_c[0], LAST, which)

            @pl.when(jnp.logical_not(first_x))
            def _():
                write_layers(out_c[0], FIRST, which)
        else:
            write_layers(out_c[0], LAST, which)
            write_layers(out_c[1], FIRST, which)

    corner[...] = jnp.zeros_like(corner)
    ends[ENDS_MAP : ENDS_MAP + last + 1, :] = owners[0 : last + 1]
    arrive(8)
    write(FIELDS, *range(STRESS, VEL), "gx", "gy", "gz")
    leave = pltpu.make_async_copy(routed_out, out_t, sems.at[15])
    leave.start()
    arrive(10, 13, 11, 12, 4, 5, 9)
    for i in range(4):
        gain[i] = courant * (1.0 - (1.0 - dec[0, i]) * los[0, i])
    for i in range(4):
        kept = courant * dec[0, i]
        for c in range(6):
            value = st[c, 0, i] + kept * mem[c, 0, i]
            if c < 3:
                value = value + source[i * ROWS : (i + 1) * ROWS, :]
            held[c, i] = value
    write(*range(VEL, FIELDS), "hy", "hz")
    below, above = corner[0:CORNER, :].astype(BF16), corner[CORNER : 2 * CORNER, :].astype(BF16)
    out_e[...] = jnp.where(even, below, above)
    out_d[...] = jnp.where(even, above, below)
    for out, entries in zip(out_c, (LAST, FIRST)):
        if merged:
            base = LONGEST * ROWS

            @pl.when(first_x)
            def _():
                rest = (LONGEST - len(LAST)) * ROWS
                out[len(LAST) * ROWS : base, :] = jnp.zeros((rest, LANES), BF16)
        else:
            base = len(entries) * ROWS
        out[base : base + 16, :] = ends[...].astype(BF16)
    leave.wait()


def route_tiles(n, near_lam, near_mu, near_bu, near_dest, rows, out):
    offsets = tile_offsets(n)
    chunk = tile_chunk(n)
    per = near_lam.shape[0]
    total = n * len(offsets)
    at = lane((1, per))
    stored = jnp.full((1, per), -1, jnp.int32)
    for t in range(per):
        stored = jnp.where(at == t, near_dest[t], stored)
    row = sublane((total, per))
    brick = lax.rem(row, n)
    for k, off in enumerate(offsets):
        brick = jnp.where(row // n == k, brick + off % n, brick)
    brick = jnp.where(brick >= n, brick - n, brick)
    route = (brick == stored).astype(BF16)
    cell, spot = sublane((2 * LANES, LANES)), lane((2 * LANES, LANES))
    half = lax.rem(spot, 64)
    cells = half // 16 * 64 + lax.rem(half, 16)
    ends = (cell == cells + jnp.where(spot < 64, 0, 48)).astype(BF16)
    left = lane((n, LANES)) < 64
    if chunk > 9 + 7 * len(sides_of(n)):
        rows[...] = jnp.zeros_like(rows)

    def put(j, value):
        rows[pl.ds(j, n, stride=chunk), :] = value

    tiles = [near[...] for near in (near_lam, near_mu, near_bu)]
    stacked = jnp.concatenate([tile.astype(F32) for tile in tiles], 0).astype(BF16)
    halves = jnp.dot(stacked, ends, preferred_element_type=F32)
    for p, tile in enumerate(tiles):
        whole = jnp.dot(route, tile, preferred_element_type=F32)
        outer = halves[p * per : (p + 1) * per].astype(BF16)
        outer = jnp.dot(route, outer, preferred_element_type=F32)

        def slot(x, k):
            return x[k * n : (k + 1) * n]

        put(2 * p, slot(whole, 0)[:, :LANES])
        put(2 * p + 1, slot(whole, 0)[:, LANES:])
        put(6 + p, jnp.where(left, slot(outer, 1), slot(outer, 2)))
        for g in range(len(sides_of(n))):
            side = slot(whole, 3 + 3 * g)
            base = 9 + 7 * g
            if p < 2:
                put(base + p, jnp.where(left, side[:, :LANES], side[:, LANES:]))
            else:
                put(base + 2, side[:, :LANES])
                put(base + 3, side[:, LANES:])
            put(base + 4 + p, jnp.where(left, slot(outer, 4 + 3 * g), slot(outer, 5 + 3 * g)))
    out[...] = rows[...].astype(BF16)


def halo_blocks(even, near, far, f):
    x = near[f * 8 : f * 8 + 8, :]
    y = far[f * 8 : f * 8 + 8, :]
    return jnp.where(even, x, y), jnp.where(even, y, x)


def halo_rows(blocks, i):
    after, before = blocks
    sub = sublane((8, LANES))
    return jnp.where(sub < 2, roll(after, -2 * i, 0), roll(before, 6 - 2 * i, 0))


def side_messages(n, got_c):
    first_x = lax.axis_index("gx") < PY
    if is_merged(n):
        message, base = got_c[0], LONGEST * ROWS
        return [("before", LAST, message, base, jnp.logical_not(first_x)), ("after", FIRST, message, base, first_x)]
    return [
        (name, which, message, len(which) * ROWS, None)
        for name, which, message in (("before", LAST, got_c[0]), ("after", FIRST, got_c[1]))
    ]


def side_rows(which, message, whole, ends, f, i):
    k = which.index((f, i))
    main = message[k * ROWS : (k + 1) * ROWS, :].astype(F32)
    if whole is None:
        return main
    sub = sublane((8, LANES))
    only = [jnp.zeros((8, LANES), F32)] * (ROWS // 8)
    for e in (3, 4, 5, 9, 10, 11):
        if ENDS[e][:2] == (f, i):
            at = ENDS[e][2] % ROWS
            only[at // 8] = jnp.where(sub == at % 8, jnp.broadcast_to(ends[e : e + 1, :], (8, LANES)), 0.0)
    return jnp.where(whole, main, jnp.concatenate(only, 0))


PLAIN = GAIN + 1
SIDES = [("before", f, i) for f, i in LAST] + [("after", f, i) for f, i in FIRST]
SIDE_PROPS = [s for s in SIDES if s[1] in (LAME, MU, BUOY)]


def side_kernel(n, *refs):
    sides = len(sides_of(n))
    got_c, (side, ends) = refs[:sides], refs[sides:]
    sub = sublane((8, LANES))
    for name, which, message, base, whole in side_messages(n, got_c):
        ends[...] = message[base : base + 16, :].astype(F32)

        def end_row(f, i, r):
            at = ENDS.index((f, i, r))
            return jnp.broadcast_to(ends[at : at + 1, :], (8, LANES))

        edge = 3 if name == "before" else 0
        for f, i in which:
            k = SIDES.index((name, f, i))
            side[k, 0:ROWS] = side_rows(which, message, whole, ends, f, i)
            if isinstance(f, str):
                halo = jnp.zeros((8, LANES), F32)
                if i == edge and f == "gx":
                    halo = jnp.where(sub == 0, -end_row(STRESS + XY, i, -1), 0.0)
                if i == edge and f == "gy":
                    halo = jnp.where(sub == 7, end_row(STRESS + YY, i, 0), 0.0)
                if i == edge and f == "gz":
                    halo = jnp.where(sub == 0, -end_row(STRESS + YZ, i, -1), 0.0)
                side[k, ROWS:EXT] = halo


def tile_kernel(n, *refs):
    sides = len(sides_of(n))
    (lam, mu, bu, maps, got_t) = refs[:5]
    got_c = refs[5 : 5 + sides]
    own, side, corner, rows_t, spread_rows, tile_rows, ends = refs[5 + sides :]
    chunk = tile_chunk(n)
    rows_t[...] = got_t[...].astype(F32)
    on_line = lane((16, LANES)) // TZ == sublane((16, LANES))
    spread = (lax.rem(sublane((LANES, LANES)), TZ) == lax.rem(lane((LANES, LANES)), TZ)).astype(BF16)

    def lines(first, row, halves):
        for s in range(16):
            for h in range(halves):
                value = rows_t[pl.ds((first + s) * chunk + row + h, 1), :]
                value = jnp.where(on_line, jnp.broadcast_to(value, (16, LANES)), 0.0)
                at = (s * halves + h) * 16
                spread_rows[at : at + 16, :] = value.astype(BF16)
        return jnp.dot(spread_rows[0 : 256 * halves, :], spread, preferred_element_type=F32)

    def overlay(row, halves, wanted):
        def take(first, values):
            tile_rows[0 : 256 * halves, :] = lines(first, row, halves)
            done = []
            for value, (_, owner, at) in zip(values, wanted):
                for s in range(16):
                    here = tile_rows[s * halves * 16 + at : s * halves * 16 + at + 8, :]
                    value = jnp.where(owner == (first + s) * 1.0, here, value)
                done.append(value)
            return done

        values = [w[0] for w in wanted]
        if n == 16:
            return take(0, values)
        return lax.fori_loop(0, n // 16, lambda g, v: take(g * 16, v), values)

    rows_y = ROWS // TY

    def main_tiles(mains, owners, row, halves, line_of):
        wanted = []
        for i, m in mains.items():
            for p in range(rows_y):
                owner = jnp.broadcast_to(owners[p : p + 1], (8, LANES))
                wanted.append((m[p * 8 : (p + 1) * 8], owner, line_of(i)))
        laid = overlay(row, halves, wanted)
        return {i: jnp.concatenate(laid[k * rows_y : (k + 1) * rows_y], 0) for k, i in enumerate(mains)}

    for p, ref in enumerate((lam, mu, bu)):
        main = main_tiles({i: ref[0, i] for i in range(4)}, maps[...], 2 * p, 2, lambda i: i * 8)
        for i in range(4):
            own[p, i] = main[i]
    for at, (name, which, message, base, whole) in enumerate(side_messages(n, got_c)):
        group = 0 if whole is not None else at
        ends[...] = message[base : base + 16, :].astype(F32)
        owners = ends[8:16, :][ENDS_MAP - 8 :]
        row = 9 + 7 * group
        for f in (LAME, MU, BUOY):
            main = {i: side_rows(which, message, whole, ends, f, i) for g, i in which if g == f}
            if f == BUOY:
                main = main_tiles(main, owners, row + 2, 2, lambda i: i * 8)
            else:
                main = main_tiles(main, owners, row + f - LAME, 1, lambda i: 8 if i else 0)
            for i, value in main.items():
                side[SIDE_PROPS.index((name, f, i))] = value
    for g in range(1 + sides):
        for p in range(3):
            row = 6 + 7 * g + p
            if n == 16:
                corner[3 * g + p] = lines(0, row, 1)
            else:

                def spread_group(q, _, g=g, p=p, row=row):
                    corner[3 * g + p, pl.ds(q * 256, 256)] = lines(q * 16, row, 1)
                    return 0

                lax.fori_loop(0, n // 16, spread_group, 0)


def rules(n, lame, shear, buoy):
    b = lax.axis_index("gx")

    tall = sublane((EXT, LANES))

    def linked(test):
        def of(step):
            q = lax.rem(b + step + n, n)
            return jnp.where(test(q), 1, 0)

        flags = jnp.where(tall < ROWS, of(0), jnp.where(tall < ROWS + 4, of(1), of(-1)))
        return flags == 1

    link_before = linked(lambda q: q >= PY)
    link_after = linked(lambda q: q < n - PY)

    def x_next(a, l, across=None):
        if l == 1:
            return jnp.where(link_before, a[2], 0.0)
        if l == 5:
            return jnp.where(link_after, a[6] if across is None else across, 0.0)
        return a[l + 1]

    def x_prev(a, l, across=None):
        if l == 2:
            return jnp.where(link_before, a[1] if across is None else across, 0.0)
        if l == 6:
            return jnp.where(link_after, a[5], 0.0)
        return a[l - 1]

    def y_next(a):
        return roll(a, -1, 0)

    def y_prev(a):
        return roll(a, 1, 0)

    z_next, z_prev = z_after, z_before

    def move(new, v, s, l, spans, sums, faces):
        def add(d, grad):
            if sums[d][l] is not None:
                grad = sums[d][l] + grad
            new[d][l] = v[d][l] + courant * buoy[l] * grad

        if l in spans[0]:
            ahead = x_next(s[XX], l, faces.get(XX))
            add(0, (ahead - s[XX][l]) + (s[XY][l] - y_prev(s[XY][l])) + (s[XZ][l] - z_prev(s[XZ][l])))
        if l in spans[1]:
            behind = x_prev(s[XY], l, faces.get(XY))
            add(1, (s[XY][l] - behind) + (y_next(s[YY][l]) - s[YY][l]) + (s[YZ][l] - z_prev(s[YZ][l])))
            behind = x_prev(s[XZ], l, faces.get(XZ))
            add(2, (s[XZ][l] - behind) + (s[YZ][l] - y_prev(s[YZ][l])) + (z_next(s[ZZ][l]) - s[ZZ][l]))

    def rates_at(v, l, wanted):
        out = [None] * 6
        ex = v[0][l] - x_prev(v[0], l)
        ey = v[1][l] - y_prev(v[1][l])
        ez = v[2][l] - z_prev(v[2][l])
        spread_part = lame[l] * (ex + ey + ez)
        twice = 2.0 * shear[l]
        for c, e in ((XX, ex), (YY, ey), (ZZ, ez)):
            if c in wanted:
                out[c] = spread_part + twice * e
        if XY in wanted:
            out[XY] = shear[l] * ((y_next(v[0][l]) - v[0][l]) + (x_next(v[1], l) - v[1][l]))
        if XZ in wanted:
            out[XZ] = shear[l] * ((z_next(v[0][l]) - v[0][l]) + (x_next(v[2], l) - v[2][l]))
        if YZ in wanted:
            out[YZ] = shear[l] * ((z_next(v[1][l]) - v[1][l]) + (y_next(v[2][l]) - v[2][l]))
        return out

    return move, rates_at, link_before, link_after


def tile_rows_around(n, line_tiles, group, after, before):
    laid = []
    for p in range(3):
        low = high = jnp.zeros((8, LANES), F32)
        for s in range(n):
            low = jnp.where(after == s * 1.0, line_tiles[3 * group + p, s * 16 : s * 16 + 8], low)
            high = jnp.where(before == s * 1.0, line_tiles[3 * group + p, s * 16 + 8 : s * 16 + 16], high)
        laid.append((low, high))
    return laid, jnp.where(sublane((8, LANES)) < 4, after, before) >= 0.0


OUTER = (2, 5)
INNER = (3, 4)


def first_kernel(n, *refs):
    (vel, st, mem, dec, los, kept, side, own_props, line_tiles, got_a, got_b) = refs[:11]
    out_props, out_gain, out_held, out_cross, out_v, out_s, out_m = refs[11:]
    even = lax.rem(lax.axis_index("gx"), 2) == 0
    laid, covered = tile_rows_around(n, line_tiles, 0, *halo_blocks(even, got_a, got_b, FIELDS))
    column = {}
    for f in range(FIELDS):
        blocks = halo_blocks(even, got_a, got_b, f)
        for i in range(4):
            halo = halo_rows(blocks, i)
            if f >= LAME:
                halo = jnp.where(covered, halo_rows(laid[f - LAME], i), halo)
            if f < VEL:
                main = st[f, 0, i]
            elif f < HELD:
                main = vel[f - VEL, 0, i]
            elif f < GAIN:
                main = kept[f - HELD, i]
            elif f == GAIN:
                main = courant * (1.0 - (1.0 - dec[0, i]) * los[0, i])
            else:
                main = own_props[f - LAME, i]
            column[f, i] = jnp.concatenate([main, halo], 0)

    def layers_of(f):
        return [None, None] + [column[f, i] for i in range(4)] + [None, None]

    def face_of(name, c, i):
        return jnp.concatenate([side[SIDES.index((name, STRESS + c, i)), 0:ROWS], jnp.zeros((8, LANES), F32)], 0)

    s0 = [layers_of(STRESS + c) for c in range(6)]
    v0 = [layers_of(VEL + c) for c in range(3)]
    held = [layers_of(HELD + c) for c in range(6)]
    gain, lame, shear, buoy = (layers_of(f) for f in (GAIN, LAME, MU, BUOY))
    move, rates_at, _, _ = rules(n, lame, shear, buoy)
    faces = {XX: face_of("after", XX, 0), XY: face_of("before", XY, 3), XZ: face_of("before", XZ, 3)}
    v1 = [[None] * 8 for _ in range(3)]
    for l in range(2, 6):
        move(v1, v0, s0, l, (range(2, 6), range(2, 6)), [[None] * 8] * 3, faces)
        for c in range(3):
            out_v[c, l - 2] = v1[c][l]
        out_gain[l - 2] = gain[l]
        for p, values in enumerate((lame, shear, buoy)):
            out_props[p, l - 2] = values[l]
    for k, l in enumerate(OUTER):
        for c in range(6):
            out_held[c, k] = held[c][l]
    for k, value in enumerate((s0[XX][2], s0[XY][5], s0[XZ][5])):
        out_cross[k] = value
    for k, l in enumerate(INNER):
        i = l - 2
        rates = rates_at(v1, l, range(6))
        lost = (1.0 - dec[0, i]) * los[0, i]
        for c in range(6):
            out_s[c, k] = held[c][l] + gain[l] * rates[c]
            out_m[c, k] = dec[0, i] * mem[c, 0, i] - lost * rates[c][:ROWS]


def wave_kernel(n, *refs):
    merged = is_merged(n)
    sides = len(sides_of(n))
    (mem, dec, los, side, source, side_props, line_tiles) = refs[:7]
    (own_props, own_gain, own_held, cross, own_v, own_s, own_m) = refs[7:14]
    got_d, got_e = refs[14 : 14 + sides], refs[14 + sides : 14 + 2 * sides]
    refs = refs[14 + 2 * sides :]
    far_outs, (near_rows, far_rows, new_v, new_s, new_m, sems) = refs[:3], refs[3:]
    even = lax.rem(lax.axis_index("gx"), 2) == 0
    sub = sublane((8, LANES))
    no_rows, no_halo = jnp.zeros((ROWS, LANES), F32), jnp.zeros((8, LANES), F32)

    column = {}
    for i in range(4):
        column["own", GAIN, i] = own_gain[i]
        for p in range(3):
            column["own", LAME + p, i] = own_props[p, i]
    for k, l in enumerate(OUTER):
        for c in range(6):
            column["own", HELD + c, l - 2] = own_held[c, k]
    for k, (c, i) in enumerate(((XX, 0), (XY, 3), (XZ, 3))):
        column["own", STRESS + c, i] = cross[k]

    def corner_rows(table, rows, f, i):
        value = None
        for k, (g, j, r) in enumerate(rows):
            if (g, j) == (f, i):
                row = jnp.broadcast_to(table[k : k + 1, :], (8, LANES))
                value = jnp.where(sub == (r % 8), row, 0.0 if value is None else value)
        return value

    face = {}
    for at, (name, which) in enumerate((("before", LAST), ("after", FIRST))):
        group = 0 if merged else at
        if group == at:
            near, far = got_e[group][...].astype(F32), got_d[group][...].astype(F32)
            near_rows[...] = jnp.where(even, near, far)
            far_rows[...] = jnp.where(even, far, near)
            after = jnp.broadcast_to(near_rows[len(ABOVE) : len(ABOVE) + 1, :], (8, LANES))
            before = jnp.broadcast_to(far_rows[len(BELOW) : len(BELOW) + 1, :], (8, LANES))
            laid, covered = tile_rows_around(n, line_tiles, 1 + group, after, before)

        def corner_halo(f, i):
            above = corner_rows(near_rows, ABOVE, f, i)
            below = corner_rows(far_rows, BELOW, f, i)
            if above is None or below is None:
                halo = no_halo if above is below else (below if above is None else above)
            else:
                halo = jnp.where(sub < 4, above, below)
            if f >= LAME:
                halo = jnp.where(covered, halo_rows(laid[f - LAME], i), halo)
            return halo

        edge = 3 if name == "before" else 0
        layers = (2, 3) if name == "before" else (0, 1)
        for f in range(FIELDS):
            for i in layers:
                if not (f < VEL or f in range(HELD, GAIN) or (f, i) in which):
                    continue
                halo = corner_halo(f, i)
                main = no_rows
                if f >= LAME:
                    main = side_props[SIDE_PROPS.index((name, f, i))]
                elif (f, i) in which:
                    main = side[SIDES.index((name, f, i)), 0:ROWS]
                if f < VEL:
                    column[name, f, i] = jnp.concatenate([no_rows, halo], 0)
                    if (f, i) in which:
                        face[name, f] = jnp.concatenate([main, halo], 0)
                else:
                    column[name, f, i] = jnp.concatenate([main, halo], 0)
        for f, i in which:
            if isinstance(f, str):
                column[name, f, i] = side[SIDES.index((name, f, i))]

    def layers_of(f):
        names = [("before", 2), ("before", 3)] + [("own", i) for i in range(4)] + [("after", 0), ("after", 1)]
        return [column.get((name, f, i)) for name, i in names]

    s0 = [layers_of(STRESS + c) for c in range(6)]
    v0 = [layers_of(VEL + c) for c in range(3)]
    held = [layers_of(HELD + c) for c in range(6)]
    gain, lame, shear, buoy = (layers_of(f) for f in (GAIN, LAME, MU, BUOY))

    move, rates_at, link_before, link_after = rules(n, lame, shear, buoy)
    faces = {XX: face["after", STRESS + XX], XY: face["before", STRESS + XY], XZ: face["before", STRESS + XZ]}
    faces = {XX: face["after", STRESS + XX], XY: face["before", STRESS + XY], XZ: face["before", STRESS + XZ]}
    copies = []

    def send(k, i):
        near, far = (new_v, new_s, new_m)[k], far_outs[k]
        copies.append(pltpu.make_async_copy(near.at[:, :, i], far.at[:, :, i], sems.at[k, i]))
        copies[-1].start()

    v1, v2 = ([[None] * 8 for _ in range(3)] for _ in range(2))
    s1 = [[None] * 8 for _ in range(6)]
    m1 = {}
    sums1 = [layers_of(g) for g in ("gx", "gy", "gz")]
    sums2 = [layers_of(h) for h in (None, "hy", "hz")]
    for l in range(2, 6):
        for c in range(3):
            v1[c][l] = own_v[c, l - 2]
    for k, l in enumerate(INNER):
        for c in range(6):
            s1[c][l] = own_s[c, k]
            m1[c, l] = own_m[c, k]

    def at_corner(d, l, link, sign, c):
        more = sign * courant * buoy[l][ROWS:] * jnp.where(link[ROWS:], faces[c][ROWS:], 0.0)
        v1[d][l] = jnp.concatenate([v1[d][l][:ROWS], v1[d][l][ROWS:] + more], 0)

    at_corner(0, 5, link_after, 1.0, XX)
    at_corner(1, 2, link_before, -1.0, XY)
    at_corner(2, 2, link_before, -1.0, XZ)
    for at in range(9):
        move(v1, v0, s0, at, ((0, 1, 6), (1, 6, 7)), sums1, {})
        l = at - 1
        if l in (1, 2, 5, 6):
            wanted = (XX, XY, XZ) if l == 1 else range(6)
            rates = rates_at(v1, l, wanted)
            for c in wanted:
                s1[c][l] = held[c][l] + gain[l] * rates[c]
                if 2 <= l < 6:
                    i = l - 2
                    lost = (1.0 - dec[0, i]) * los[0, i]
                    m1[c, l] = dec[0, i] * mem[c, 0, i] - lost * rates[c][:ROWS]
        l = at - 2
        move(v2, v1, s1, l, (range(1, 6), range(2, 7)), sums2, {})
        if l in range(2, 6):
            for c in range(3):
                new_v[c, 0, l - 2] = v2[c][l][:ROWS]
            send(0, l - 2)
        l = at - 3
        if l in range(2, 6):
            i = l - 2
            rates = rates_at(v2, l, range(6))
            d = dec[0, i]
            lost = (1.0 - d) * los[0, i]
            for c in range(6):
                rate = rates[c][:ROWS]
                m2 = d * m1[c, l] - lost * rate
                new_m[c, 0, i] = m2
                value = s1[c][l][:ROWS] + courant * (rate + m2)
                if c < 3:
                    value = value + source[i * ROWS : (i + 1) * ROWS, :]
                new_s[c, 0, i] = value
            send(1, i)
            send(2, i)
    for copy in copies:
        copy.wait()


def body(
    velocity,
    stress,
    memory,
    lame_lambda,
    lame_mu,
    buoyancy,
    decay,
    loss,
    tile_lambda,
    tile_mu,
    tile_buoy,
    tile_dest,
    brick_tiles,
    src_index,
    src_wave,
):
    n = lax.axis_size("gx")
    merged = is_merged(n)
    sides = sides_of(n)
    chunk = tile_chunk(n)
    on_core = pl.BlockSpec(memory_space=pltpu.VMEM)
    away = pl.BlockSpec(memory_space=pltpu.HBM)
    def vmem(*shape):
        return jax.ShapeDtypeStruct(shape, F32)

    waves = src_wave.T
    cells = src_index[None, :]
    fields = (velocity, stress, memory, lame_lambda, lame_mu, buoyancy, decay, loss)
    if merged:
        c_rows = [LONGEST * ROWS + 16]
    else:
        c_rows = [len(LAST) * ROWS + 16, len(FIRST) * ROWS + 16]
    tiles = (tile_lambda, tile_mu, tile_buoy)
    kept = (decay, loss, stress, memory, velocity, lame_lambda, lame_mu, buoyancy)
    inputs = (*tiles, tile_dest, decay, loss, cells, waves, stress, memory, velocity, lame_lambda, lame_mu, buoyancy, brick_tiles)
    inputs = tuple(pltpu.with_memory_space_constraint(x, pltpu.HBM) for x in inputs)
    packed = pl.pallas_call(
        functools.partial(pack_kernel, n, tile_lambda.shape[0]),
        out_shape=[
            jax.ShapeDtypeStruct((BLOCK, LANES), F32),
            jax.ShapeDtypeStruct((BLOCK, LANES), F32),
            jax.ShapeDtypeStruct((CORNER, LANES), BF16),
            jax.ShapeDtypeStruct((CORNER, LANES), BF16),
            jax.ShapeDtypeStruct((8, LANES), F32),
            jax.ShapeDtypeStruct((n * chunk, LANES), BF16),
        ]
        + [jax.ShapeDtypeStruct(x.shape, x.dtype) for x in kept]
        + [vmem(6, 4, ROWS, LANES), vmem(4 * ROWS, LANES)]
        + [jax.ShapeDtypeStruct((r, LANES), BF16) for r in c_rows],
        in_specs=[away] * len(inputs),
        out_specs=[on_core] * 5 + [away] + [on_core] * (10 + len(c_rows)),
        scratch_shapes=[
            pltpu.SMEM(x.shape, x.dtype) if x.ndim == 1 else pltpu.VMEM(x.shape, x.dtype)
            for x in (*tiles, tile_dest, cells, waves, brick_tiles)
        ]
        + [
            pltpu.SemaphoreType.DMA((16,)),
            pltpu.VMEM((4, ROWS, LANES), F32),
            pltpu.VMEM((4 * ROWS, LANES), F32),
            pltpu.VMEM((2 * CORNER, LANES), F32),
            pltpu.VMEM((16, LANES), F32),
            pltpu.VMEM((n * chunk, LANES), F32),
            pltpu.VMEM((n * chunk, LANES), BF16),
        ],
        compiler_params=pltpu.CompilerParams(vmem_limit_bytes=16 * 1024 * 1024),
        name="pack",
    )(*inputs)
    out_a, out_b, out_d, out_e, own_map, out_t = packed[:6]
    held, later = packed[14:16]
    out_c = packed[16:]
    dec, los, st, mem, vel, lam, mu, bu = packed[6:14]

    def permute(array, source_of):
        return lax.ppermute(array, "gx", [(source_of(i), i) for i in range(n)])

    got_c = [permute(c, lambda i, o=o: (i + o) % n) for c, o in zip(out_c, sides)]
    got_d = [permute(out_d, lambda i, o=o: pair_far((i + o) % n, n)) for o in sides]
    got_e = [permute(out_e, lambda i, o=o: pair_near((i + o) % n)) for o in sides]
    got_b = permute(out_b, lambda i: pair_far(i, n))
    got_a = permute(out_a, pair_near)
    got_t = lax.all_to_all(out_t, "gx", split_axis=0, concat_axis=0, tiled=True)

    side = pl.pallas_call(
        functools.partial(side_kernel, n),
        out_shape=vmem(len(SIDES), EXT, LANES),
        in_specs=[on_core] * len(sides),
        out_specs=on_core,
        scratch_shapes=[pltpu.VMEM((16, LANES), F32)],
        compiler_params=pltpu.CompilerParams(vmem_limit_bytes=16 * 1024 * 1024),
        name="sides",
    )(*got_c)
    own_props, side_props, line_tiles = pl.pallas_call(
        functools.partial(tile_kernel, n),
        out_shape=[
            vmem(3, 4, ROWS, LANES),
            vmem(len(SIDE_PROPS), ROWS, LANES),
            vmem(3 + 3 * len(sides), n * 16, LANES),
        ],
        in_specs=[on_core] * (5 + len(sides)),
        out_specs=[on_core] * 3,
        scratch_shapes=[
            pltpu.VMEM((n * chunk, LANES), F32),
            pltpu.VMEM((16 * 32, LANES), BF16),
            pltpu.VMEM((16 * 32, LANES), F32),
            pltpu.VMEM((16, LANES), F32),
        ],
        compiler_params=pltpu.CompilerParams(vmem_limit_bytes=16 * 1024 * 1024),
        name="tiles",
    )(lam, mu, bu, own_map, got_t, *got_c)
    first = pl.pallas_call(
        functools.partial(first_kernel, n),
        out_shape=[
            vmem(3, 4, EXT, LANES),
            vmem(4, EXT, LANES),
            vmem(6, 2, EXT, LANES),
            vmem(3, EXT, LANES),
            vmem(3, 4, EXT, LANES),
            vmem(6, 2, EXT, LANES),
            vmem(6, 2, ROWS, LANES),
        ],
        in_specs=[on_core] * 11,
        out_specs=[on_core] * 7,
        compiler_params=pltpu.CompilerParams(vmem_limit_bytes=16 * 1024 * 1024),
        name="first",
    )(vel, st, mem, dec, los, held, side, own_props, line_tiles, got_a, got_b)
    outs = (velocity, stress, memory)
    return pl.pallas_call(
        functools.partial(wave_kernel, n),
        out_shape=[jax.ShapeDtypeStruct(x.shape, F32) for x in outs],
        in_specs=[on_core] * (14 + 2 * len(sides)),
        out_specs=[away] * 3,
        scratch_shapes=[
            pltpu.VMEM((CORNER, LANES), F32),
            pltpu.VMEM((CORNER, LANES), F32),
        ]
        + [pltpu.VMEM(x.shape, F32) for x in outs]
        + [pltpu.SemaphoreType.DMA((3, 4))],
        compiler_params=pltpu.CompilerParams(vmem_limit_bytes=48 * 1024 * 1024),
        name="wave",
    )(mem, dec, los, side, later, side_props, line_tiles, *first, *got_d, *got_e)


def solution(mesh):
    split = ("groups", "gx")
    whole = P(None, split, None, None, None)
    field = P(split, None, None, None)
    return jax.shard_map(
        body,
        mesh=mesh,
        in_specs=(whole,) * 3
        + (field,) * 5
        + (P(split, None),) * 3
        + (P(split), P(split, None), P(split), P(split, None)),
        out_specs=(whole,) * 3,
        check_vma=False,
    )
```

```python
import functools

import jax
import jax.numpy as jnp
from jax import lax
from jax.experimental import pallas as pl
from jax.experimental.pallas import tpu as pltpu
from jax.sharding import PartitionSpec as P

PY = 8
TY = 8
TZ = 8
courant = 0.25

F32 = jnp.float32
BF16 = jnp.bfloat16
XX, YY, ZZ, XY, XZ, YZ = range(6)
STRESS, VEL, HELD, GAIN, LAME, MU, BUOY = 0, 6, 9, 15, 16, 17, 18
FIELDS = 19
LAST = [("gx", 2), ("gx", 3), ("gy", 3), ("gz", 3), (STRESS + XY, 3), (STRESS + XZ, 3)]
LAST += [(VEL, 2), (VEL, 3), (VEL + 1, 3), (VEL + 2, 3), (BUOY, 2), (BUOY, 3)]
LAST += [(HELD + c, 3) for c in (XX, XY, XZ)] + [(GAIN, 3), (LAME, 3), (MU, 3)]
FIRST = [("gx", 0), ("gy", 0), ("gz", 0), ("gy", 1), ("gz", 1), (STRESS + XX, 0)]
FIRST += [(VEL, 0), (VEL + 1, 0), (VEL + 1, 1), (VEL + 2, 0), (VEL + 2, 1), (BUOY, 0), (BUOY, 1)]
FIRST += [(HELD + XX, 0), ("hy", 0), ("hz", 0), (GAIN, 0), (LAME, 0), (MU, 0)]
BELOW_LAST = [(STRESS + c, 3) for c in range(6) if c != ZZ] + [(VEL, 3), (VEL + 1, 3), (HELD + XY, 3), (GAIN, 3)]
BELOW_LAST = [(f, i, -1) for f, i in BELOW_LAST + [(MU, 3), (BUOY, 3), (STRESS + XY, 2)]] + [(STRESS + XY, 3, -2)]
ABOVE_LAST = [(STRESS + c, 3) for c in range(6)] + [(VEL, 3), (VEL + 2, 3), (HELD + XZ, 3), (GAIN, 3)]
ABOVE_LAST = [(f, i, 0) for f, i in ABOVE_LAST + [(MU, 3), (BUOY, 3), (STRESS + XZ, 2)]] + [(STRESS + XZ, 3, 1)]
BELOW_FIRST = [(STRESS + c, 0) for c in range(6)] + [(VEL + 1, 0), (VEL + 2, 0), (HELD + YZ, 0), (GAIN, 0)]
BELOW_FIRST = [(f, i, -1) for f, i in BELOW_FIRST + [(MU, 0), (BUOY, 0), (STRESS + YZ, 1)]] + [(STRESS + YZ, 0, -2)]
ABOVE_FIRST = [(STRESS + c, 0) for c in range(6)] + [(VEL + c, 0) for c in range(3)] + [(HELD + XX, 0), (HELD + YY, 0)]
ABOVE_FIRST += [(GAIN, 0), (LAME, 0), (MU, 0), (BUOY, 0), (STRESS + XX, 1), (STRESS + YY, 1)]
ABOVE_FIRST = [(f, i, 0) for f, i in ABOVE_FIRST] + [(STRESS + XX, 0, 1), (STRESS + YY, 0, 1)]
BELOW = BELOW_LAST + BELOW_FIRST
ABOVE = ABOVE_LAST + ABOVE_FIRST
ENDS = [(STRESS + YY, 0, 0), (STRESS + XY, 0, -1), (STRESS + YZ, 0, -1)]
ENDS += [("gy", 0, -1), (VEL + 1, 0, -1), (BUOY, 0, -1)]
ENDS += [(STRESS + YY, 3, 0), (STRESS + XY, 3, -1), (STRESS + YZ, 3, -1)]
ENDS += [("gx", 3, 0), (VEL, 3, 0), (BUOY, 3, 0)]
ENDS_MAP = 12
LONGEST = max(len(LAST), len(FIRST))
ROWS = 32
EXT = ROWS + 8
LANES = 128
BLOCK = FIELDS * 8 + 8
CORNER = -(-(max(len(BELOW), len(ABOVE)) + 1) // 16) * 16


def pair_near(i):
    return i ^ 1


def pair_far(i, n):
    return (i - 1) % n if i % 2 == 0 else (i + 1) % n


def is_merged(n):
    return n == 2 * PY


def sides_of(n):
    return [PY] if is_merged(n) else [-PY, PY]


def tile_offsets(n):
    return [k for o in [0] + sides_of(n) for k in (o, o + 1, o - 1)]


def tile_chunk(n):
    return -(-(9 + 7 * len(sides_of(n))) // 16) * 16


def roll(x, by, axis):
    size = x.shape[axis]
    by = by % size
    return x if by == 0 else pltpu.roll(x, by, axis)


def sublane(shape):
    return lax.broadcasted_iota(jnp.int32, shape, 0)


def lane(shape):
    return lax.broadcasted_iota(jnp.int32, shape, 1)


def z_after(a):
    return jnp.where(lane(a.shape) == LANES - 1, 0.0, roll(a, -1, 1))


def z_before(a):
    return jnp.where(lane(a.shape) == 0, 0.0, roll(a, 1, 1))


def place_sources(index, wave, step):
    count = index.shape[1]
    cells = jnp.broadcast_to(index[...], (LANES, count))
    place = sublane((LANES, count))
    rows = (lax.shift_right_logical(cells, 7) == place).astype(F32)
    at = ((cells & (LANES - 1)) == place).astype(F32)
    left = wave[step : step + 1, :]
    parts = []
    for _ in range(3):
        part = left.astype(BF16).astype(F32)
        parts.append((at * part).astype(BF16))
        left = left - part
    total = None
    for part in parts:
        done = lax.dot_general(rows.astype(BF16), part, (((1,), (1,)), ((), ())), preferred_element_type=F32)
        total = done if total is None else total + done
    return total


def pack_kernel(n, per, *refs):
    merged = is_merged(n)
    sides = len(sides_of(n))
    far_refs, outs, refs = refs[:15], refs[15 : 31 + sides], refs[31 + sides :]
    out_a, out_b, out_d, out_e, out_map, out_t = outs[:6]
    dec, los, st, mem, vel, lam, mu, bu = outs[6:14]
    held, later = outs[14:16]
    out_c = outs[16:]
    near_lam, near_mu, near_bu, near_dest, index, wave, tiles, sems = refs[:8]
    gain, source, corner, ends, routed, routed_out = refs[8:]
    near_refs = (near_lam, near_mu, near_bu, near_dest, dec, los, index, wave, st, mem, vel, lam, mu, bu, tiles)
    b = lax.axis_index("gx")
    even = lax.rem(b, 2) == 0
    first_x = b < PY
    top, bottom = slice(0, 8), slice(ROWS - 8, ROWS)
    copies = {}
    for k in (0, 1, 2, 3, 14, 6, 7, 8, 10, 13, 11, 12, 4, 5, 9):
        copies[k] = pltpu.make_async_copy(far_refs[k], near_refs[k], sems.at[k])
        copies[k].start()

    def arrive(*which):
        for k in which:
            copies[k].wait()

    arrive(0, 1, 2, 3)
    route_tiles(n, near_lam, near_mu, near_bu, near_dest, routed, routed_out)
    leave = pltpu.make_async_copy(routed_out, out_t, sems.at[15])
    leave.start()
    arrive(6, 7, 14)
    source[...] = place_sources(index, wave, 0)
    later[...] = place_sources(index, wave, 1)

    def get(f, i, rows=slice(None)):
        if f < VEL:
            return st[f, 0, i, rows]
        if f < HELD:
            return vel[f - VEL, 0, i, rows]
        if f < GAIN:
            return held[f - HELD, i, rows]
        if f == GAIN:
            return gain[i, rows]
        return (lam, mu, bu)[f - LAME][0, i, rows]

    sub = sublane((8, LANES))

    rows_z = LANES // TZ
    table = tiles[...]
    spots = table.shape[1]
    owner = jnp.where(table >= 0, jnp.floor((table.astype(F32) + 0.5) * (1.0 / per)) + 1.0, 0.0)
    spot = lane((8, spots))
    wide = jnp.where(spot // rows_z == sublane((8, spots)), jnp.broadcast_to(owner, (8, spots)), 0.0)
    spread = (lax.rem(sublane((spots, LANES)), rows_z) == lane((spots, LANES)) // TZ).astype(BF16)
    owners = jnp.dot(wide.astype(BF16), spread, preferred_element_type=F32) - 1.0
    out_map[...] = owners
    last = ROWS // TY - 1

    def prev_y(a):
        return jnp.where(sublane(a.shape) == 0, 0.0, roll(a, 1, 0))

    def next_y(a):
        return jnp.where(sublane(a.shape) == ROWS - 1, 0.0, roll(a, -1, 0))

    def sums(kind, i):
        def s(c, k):
            return held[c, k] if kind[0] == "h" else st[c, 0, k]

        def dy_prev(c):
            return s(c, i) - prev_y(s(c, i))

        def dy_next(c):
            return next_y(s(c, i)) - s(c, i)

        def dz_prev(c):
            return s(c, i) - z_before(s(c, i))

        def dz_next(c):
            return z_after(s(c, i)) - s(c, i)

        if kind == "gx":
            along = s(XX, i + 1) - s(XX, i) if i < 3 else -s(XX, i)
            return along + dy_prev(XY) + dz_prev(XZ)
        cross = XY if kind[1] == "y" else XZ
        along = s(cross, i) - s(cross, i - 1) if i > 0 else s(cross, i)
        if kind[1] == "y":
            return along + dy_next(YY) + dz_prev(YZ)
        return along + dy_prev(YZ) + dz_next(ZZ)

    def entry(f, i):
        return sums(f, i) if isinstance(f, str) else get(f, i)

    def edge_rows(f):
        if f == FIELDS:
            return jnp.broadcast_to(owners[0:1], (8, LANES)), jnp.broadcast_to(owners[last : last + 1], (8, LANES))
        lo, hi = get(f, 0, top), roll(get(f, 0, bottom), 2, 0)
        for i in range(1, 4):
            mine = sub // 2 == i
            lo = jnp.where(mine, roll(get(f, i, top), 2 * i, 0), lo)
            hi = jnp.where(mine, roll(get(f, i, bottom), 2 * i + 2, 0), hi)
        return lo, hi

    def write_edges(which):
        for f in which:
            lo, hi = edge_rows(f)
            out_a[f * 8 : f * 8 + 8, :] = jnp.where(even, hi, lo)
            out_b[f * 8 : f * 8 + 8, :] = jnp.where(even, lo, hi)

    def write_corner(rows, which, strip, at):
        for k, (f, i, r) in enumerate(rows):
            if f in which:
                corner[at + k : at + k + 1, :] = get(f, i, slice(r % ROWS, r % ROWS + 1))
        if FIELDS in which:
            corner[at + len(rows) : at + len(rows) + 1, :] = owners[strip : strip + 1]

    def write_layers(out, entries, which):
        for k, (f, i) in enumerate(entries):
            if f in which:
                out[k * ROWS : (k + 1) * ROWS, :] = entry(f, i).astype(BF16)

    def write_ends(which):
        for k, (f, i, r) in enumerate(ENDS):
            if f in which:
                row = slice(r % ROWS, r % ROWS + 1)
                ends[k : k + 1, :] = sums(f, i)[row] if isinstance(f, str) else get(f, i, row)

    def write(*which):
        write_edges([f for f in which if not isinstance(f, str)])
        write_corner(BELOW, which, last, 0)
        write_corner(ABOVE, which, 0, CORNER)
        write_ends(which)
        if merged:

            @pl.when(first_x)
            def _():
                write_layers(out_c[0], LAST, which)

            @pl.when(jnp.logical_not(first_x))
            def _():
                write_layers(out_c[0], FIRST, which)
        else:
            write_layers(out_c[0], LAST, which)
            write_layers(out_c[1], FIRST, which)

    corner[...] = jnp.zeros_like(corner)
    ends[ENDS_MAP : ENDS_MAP + last + 1, :] = owners[0 : last + 1]
    arrive(8)
    write(FIELDS, *range(STRESS, VEL), "gx", "gy", "gz")
    arrive(10, 13, 11, 12)
    write(*range(VEL, HELD), LAME, MU, BUOY)
    arrive(4, 5)
    for i in range(4):
        gain[i] = courant * (1.0 - (1.0 - dec[0, i]) * los[0, i])
    write(GAIN)
    arrive(9)
    for i in range(4):
        kept = courant * dec[0, i]
        for c in range(6):
            value = st[c, 0, i] + kept * mem[c, 0, i]
            if c < 3:
                value = value + source[i * ROWS : (i + 1) * ROWS, :]
            held[c, i] = value
    write(*range(HELD, GAIN), "hy", "hz")
    below, above = corner[0:CORNER, :].astype(BF16), corner[CORNER : 2 * CORNER, :].astype(BF16)
    out_e[...] = jnp.where(even, below, above)
    out_d[...] = jnp.where(even, above, below)
    for out, entries in zip(out_c, (LAST, FIRST)):
        if merged:
            base = LONGEST * ROWS

            @pl.when(first_x)
            def _():
                rest = (LONGEST - len(LAST)) * ROWS
                out[len(LAST) * ROWS : base, :] = jnp.zeros((rest, LANES), BF16)
        else:
            base = len(entries) * ROWS
        out[base : base + 16, :] = ends[...].astype(BF16)
    leave.wait()


def route_tiles(n, near_lam, near_mu, near_bu, near_dest, rows, out):
    offsets = tile_offsets(n)
    chunk = tile_chunk(n)
    per = near_lam.shape[0]
    total = n * len(offsets)
    at = lane((1, per))
    stored = jnp.full((1, per), -1, jnp.int32)
    for t in range(per):
        stored = jnp.where(at == t, near_dest[t], stored)
    row = sublane((total, per))
    brick = lax.rem(row, n)
    for k, off in enumerate(offsets):
        brick = jnp.where(row // n == k, brick + off % n, brick)
    brick = jnp.where(brick >= n, brick - n, brick)
    route = (brick == stored).astype(BF16)
    part = lane((per, LANES)) // 16

    def outer_cells(tile):
        x, y = tile[:, :LANES], tile[:, LANES:]
        moves = ((x, 0), (x, -48), (y, 32), (y, -16), (x, 16), (x, -32), (y, 48), (y, 0))
        out = x
        for k, (half, by) in enumerate(moves[1:], 1):
            out = jnp.where(part == k, roll(half, by, 1), out)
        return out

    left = lane((n, LANES)) < 64
    if chunk > 9 + 7 * len(sides_of(n)):
        rows[...] = jnp.zeros_like(rows)

    def put(j, value):
        rows[pl.ds(j, n, stride=chunk), :] = value

    tiles = [near[...] for near in (near_lam, near_mu, near_bu)]
    for p, tile in enumerate(tiles):
        whole = jnp.dot(route, tile, preferred_element_type=F32)
        outer = jnp.dot(route, outer_cells(tile.astype(F32)).astype(BF16), preferred_element_type=F32)

        def slot(x, k):
            return x[k * n : (k + 1) * n]

        put(2 * p, slot(whole, 0)[:, :LANES])
        put(2 * p + 1, slot(whole, 0)[:, LANES:])
        put(6 + p, jnp.where(left, slot(outer, 1), slot(outer, 2)))
        for g in range(len(sides_of(n))):
            side = slot(whole, 3 + 3 * g)
            base = 9 + 7 * g
            if p < 2:
                put(base + p, jnp.where(left, side[:, :LANES], side[:, LANES:]))
            else:
                put(base + 2, side[:, :LANES])
                put(base + 3, side[:, LANES:])
            put(base + 4 + p, jnp.where(left, slot(outer, 4 + 3 * g), slot(outer, 5 + 3 * g)))
    out[...] = rows[...].astype(BF16)


def halo_blocks(even, near, far, f):
    x = near[f * 8 : f * 8 + 8, :]
    y = far[f * 8 : f * 8 + 8, :]
    return jnp.where(even, x, y), jnp.where(even, y, x)


def halo_rows(blocks, i):
    after, before = blocks
    sub = sublane((8, LANES))
    return jnp.where(sub < 2, roll(after, -2 * i, 0), roll(before, 6 - 2 * i, 0))


def side_messages(n, got_c):
    first_x = lax.axis_index("gx") < PY
    if is_merged(n):
        message, base = got_c[0], LONGEST * ROWS
        return [("before", LAST, message, base, jnp.logical_not(first_x)), ("after", FIRST, message, base, first_x)]
    return [
        (name, which, message, len(which) * ROWS, None)
        for name, which, message in (("before", LAST, got_c[0]), ("after", FIRST, got_c[1]))
    ]


def side_rows(which, message, whole, ends, f, i):
    k = which.index((f, i))
    main = message[k * ROWS : (k + 1) * ROWS, :].astype(F32)
    if whole is None:
        return main
    sub = sublane((8, LANES))
    only = [jnp.zeros((8, LANES), F32)] * (ROWS // 8)
    for e in (3, 4, 5, 9, 10, 11):
        if ENDS[e][:2] == (f, i):
            at = ENDS[e][2] % ROWS
            only[at // 8] = jnp.where(sub == at % 8, jnp.broadcast_to(ends[e : e + 1, :], (8, LANES)), 0.0)
    return jnp.where(whole, main, jnp.concatenate(only, 0))


PLAIN = GAIN + 1
SIDES = [("before", f, i) for f, i in LAST] + [("after", f, i) for f, i in FIRST]
SIDE_PROPS = [s for s in SIDES if s[1] in (LAME, MU, BUOY)]


def side_kernel(n, *refs):
    sides = len(sides_of(n))
    got_c, (side, ends) = refs[:sides], refs[sides:]
    sub = sublane((8, LANES))
    for name, which, message, base, whole in side_messages(n, got_c):
        ends[...] = message[base : base + 16, :].astype(F32)

        def end_row(f, i, r):
            at = ENDS.index((f, i, r))
            return jnp.broadcast_to(ends[at : at + 1, :], (8, LANES))

        edge = 3 if name == "before" else 0
        for f, i in which:
            k = SIDES.index((name, f, i))
            side[k, 0:ROWS] = side_rows(which, message, whole, ends, f, i)
            if isinstance(f, str):
                halo = jnp.zeros((8, LANES), F32)
                if i == edge and f == "gx":
                    halo = jnp.where(sub == 0, -end_row(STRESS + XY, i, -1), 0.0)
                if i == edge and f == "gy":
                    halo = jnp.where(sub == 7, end_row(STRESS + YY, i, 0), 0.0)
                if i == edge and f == "gz":
                    halo = jnp.where(sub == 0, -end_row(STRESS + YZ, i, -1), 0.0)
                side[k, ROWS:EXT] = halo


def tile_kernel(n, *refs):
    sides = len(sides_of(n))
    (lam, mu, bu, maps, got_t) = refs[:5]
    got_c = refs[5 : 5 + sides]
    own, side, corner, rows_t, spread_rows, tile_rows, ends = refs[5 + sides :]
    chunk = tile_chunk(n)
    rows_t[...] = got_t[...].astype(F32)
    on_line = lane((16, LANES)) // TZ == sublane((16, LANES))
    spread = (lax.rem(sublane((LANES, LANES)), TZ) == lax.rem(lane((LANES, LANES)), TZ)).astype(BF16)

    def lines(first, row, halves):
        for s in range(16):
            for h in range(halves):
                value = rows_t[pl.ds((first + s) * chunk + row + h, 1), :]
                value = jnp.where(on_line, jnp.broadcast_to(value, (16, LANES)), 0.0)
                at = (s * halves + h) * 16
                spread_rows[at : at + 16, :] = value.astype(BF16)
        return jnp.dot(spread_rows[0 : 256 * halves, :], spread, preferred_element_type=F32)

    def overlay(row, halves, wanted):
        def take(first, values):
            tile_rows[0 : 256 * halves, :] = lines(first, row, halves)
            done = []
            for value, (_, owner, at) in zip(values, wanted):
                for s in range(16):
                    here = tile_rows[s * halves * 16 + at : s * halves * 16 + at + 8, :]
                    value = jnp.where(owner == (first + s) * 1.0, here, value)
                done.append(value)
            return done

        values = [w[0] for w in wanted]
        if n == 16:
            return take(0, values)
        return lax.fori_loop(0, n // 16, lambda g, v: take(g * 16, v), values)

    rows_y = ROWS // TY

    def main_tiles(mains, owners, row, halves, line_of):
        wanted = []
        for i, m in mains.items():
            for p in range(rows_y):
                owner = jnp.broadcast_to(owners[p : p + 1], (8, LANES))
                wanted.append((m[p * 8 : (p + 1) * 8], owner, line_of(i)))
        laid = overlay(row, halves, wanted)
        return {i: jnp.concatenate(laid[k * rows_y : (k + 1) * rows_y], 0) for k, i in enumerate(mains)}

    for p, ref in enumerate((lam, mu, bu)):
        main = main_tiles({i: ref[0, i] for i in range(4)}, maps[...], 2 * p, 2, lambda i: i * 8)
        for i in range(4):
            own[p, i] = main[i]
    for at, (name, which, message, base, whole) in enumerate(side_messages(n, got_c)):
        group = 0 if whole is not None else at
        ends[...] = message[base : base + 16, :].astype(F32)
        owners = ends[8:16, :][ENDS_MAP - 8 :]
        row = 9 + 7 * group
        for f in (LAME, MU, BUOY):
            main = {i: side_rows(which, message, whole, ends, f, i) for g, i in which if g == f}
            if f == BUOY:
                main = main_tiles(main, owners, row + 2, 2, lambda i: i * 8)
            else:
                main = main_tiles(main, owners, row + f - LAME, 1, lambda i: 8 if i else 0)
            for i, value in main.items():
                side[SIDE_PROPS.index((name, f, i))] = value
    for g in range(1 + sides):
        for p in range(3):
            row = 6 + 7 * g + p
            if n == 16:
                corner[3 * g + p] = lines(0, row, 1)
            else:

                def spread_group(q, _, g=g, p=p, row=row):
                    corner[3 * g + p, pl.ds(q * 256, 256)] = lines(q * 16, row, 1)
                    return 0

                lax.fori_loop(0, n // 16, spread_group, 0)


def rules(n, lame, shear, buoy):
    b = lax.axis_index("gx")

    tall = sublane((EXT, LANES))

    def linked(test):
        def of(step):
            q = lax.rem(b + step + n, n)
            return jnp.where(test(q), 1, 0)

        flags = jnp.where(tall < ROWS, of(0), jnp.where(tall < ROWS + 4, of(1), of(-1)))
        return flags == 1

    link_before = linked(lambda q: q >= PY)
    link_after = linked(lambda q: q < n - PY)

    def x_next(a, l, across=None):
        if l == 1:
            return jnp.where(link_before, a[2], 0.0)
        if l == 5:
            return jnp.where(link_after, a[6] if across is None else across, 0.0)
        return a[l + 1]

    def x_prev(a, l, across=None):
        if l == 2:
            return jnp.where(link_before, a[1] if across is None else across, 0.0)
        if l == 6:
            return jnp.where(link_after, a[5], 0.0)
        return a[l - 1]

    def y_next(a):
        return roll(a, -1, 0)

    def y_prev(a):
        return roll(a, 1, 0)

    z_next, z_prev = z_after, z_before

    def move(new, v, s, l, spans, sums, faces):
        def add(d, grad):
            if sums[d][l] is not None:
                grad = sums[d][l] + grad
            new[d][l] = v[d][l] + courant * buoy[l] * grad

        if l in spans[0]:
            ahead = x_next(s[XX], l, faces.get(XX))
            add(0, (ahead - s[XX][l]) + (s[XY][l] - y_prev(s[XY][l])) + (s[XZ][l] - z_prev(s[XZ][l])))
        if l in spans[1]:
            behind = x_prev(s[XY], l, faces.get(XY))
            add(1, (s[XY][l] - behind) + (y_next(s[YY][l]) - s[YY][l]) + (s[YZ][l] - z_prev(s[YZ][l])))
            behind = x_prev(s[XZ], l, faces.get(XZ))
            add(2, (s[XZ][l] - behind) + (s[YZ][l] - y_prev(s[YZ][l])) + (z_next(s[ZZ][l]) - s[ZZ][l]))

    def rates_at(v, l, wanted):
        out = [None] * 6
        ex = v[0][l] - x_prev(v[0], l)
        ey = v[1][l] - y_prev(v[1][l])
        ez = v[2][l] - z_prev(v[2][l])
        spread_part = lame[l] * (ex + ey + ez)
        twice = 2.0 * shear[l]
        for c, e in ((XX, ex), (YY, ey), (ZZ, ez)):
            if c in wanted:
                out[c] = spread_part + twice * e
        if XY in wanted:
            out[XY] = shear[l] * ((y_next(v[0][l]) - v[0][l]) + (x_next(v[1], l) - v[1][l]))
        if XZ in wanted:
            out[XZ] = shear[l] * ((z_next(v[0][l]) - v[0][l]) + (x_next(v[2], l) - v[2][l]))
        if YZ in wanted:
            out[YZ] = shear[l] * ((z_next(v[1][l]) - v[1][l]) + (y_next(v[2][l]) - v[2][l]))
        return out

    return move, rates_at, link_before, link_after


def tile_rows_around(n, line_tiles, group, after, before):
    laid = []
    for p in range(3):
        low = high = jnp.zeros((8, LANES), F32)
        for s in range(n):
            low = jnp.where(after == s * 1.0, line_tiles[3 * group + p, s * 16 : s * 16 + 8], low)
            high = jnp.where(before == s * 1.0, line_tiles[3 * group + p, s * 16 + 8 : s * 16 + 16], high)
        laid.append((low, high))
    return laid, jnp.where(sublane((8, LANES)) < 4, after, before) >= 0.0


OUTER = (2, 5)
INNER = (3, 4)


def first_kernel(n, *refs):
    (vel, st, mem, dec, los, kept, side, own_props, line_tiles, got_a, got_b) = refs[:11]
    out_props, out_gain, out_held, out_cross, out_v, out_s, out_m = refs[11:]
    even = lax.rem(lax.axis_index("gx"), 2) == 0
    laid, covered = tile_rows_around(n, line_tiles, 0, *halo_blocks(even, got_a, got_b, FIELDS))
    column = {}
    for f in range(FIELDS):
        blocks = halo_blocks(even, got_a, got_b, f)
        for i in range(4):
            halo = halo_rows(blocks, i)
            if f >= LAME:
                halo = jnp.where(covered, halo_rows(laid[f - LAME], i), halo)
            if f < VEL:
                main = st[f, 0, i]
            elif f < HELD:
                main = vel[f - VEL, 0, i]
            elif f < GAIN:
                main = kept[f - HELD, i]
            elif f == GAIN:
                main = courant * (1.0 - (1.0 - dec[0, i]) * los[0, i])
            else:
                main = own_props[f - LAME, i]
            column[f, i] = jnp.concatenate([main, halo], 0)

    def layers_of(f):
        return [None, None] + [column[f, i] for i in range(4)] + [None, None]

    def face_of(name, c, i):
        return jnp.concatenate([side[SIDES.index((name, STRESS + c, i)), 0:ROWS], jnp.zeros((8, LANES), F32)], 0)

    s0 = [layers_of(STRESS + c) for c in range(6)]
    v0 = [layers_of(VEL + c) for c in range(3)]
    held = [layers_of(HELD + c) for c in range(6)]
    gain, lame, shear, buoy = (layers_of(f) for f in (GAIN, LAME, MU, BUOY))
    move, rates_at, _, _ = rules(n, lame, shear, buoy)
    faces = {XX: face_of("after", XX, 0), XY: face_of("before", XY, 3), XZ: face_of("before", XZ, 3)}
    v1 = [[None] * 8 for _ in range(3)]
    for l in range(2, 6):
        move(v1, v0, s0, l, (range(2, 6), range(2, 6)), [[None] * 8] * 3, faces)
        for c in range(3):
            out_v[c, l - 2] = v1[c][l]
        out_gain[l - 2] = gain[l]
        for p, values in enumerate((lame, shear, buoy)):
            out_props[p, l - 2] = values[l]
    for k, l in enumerate(OUTER):
        for c in range(6):
            out_held[c, k] = held[c][l]
    for k, value in enumerate((s0[XX][2], s0[XY][5], s0[XZ][5])):
        out_cross[k] = value
    for k, l in enumerate(INNER):
        i = l - 2
        rates = rates_at(v1, l, range(6))
        lost = (1.0 - dec[0, i]) * los[0, i]
        for c in range(6):
            out_s[c, k] = held[c][l] + gain[l] * rates[c]
            out_m[c, k] = dec[0, i] * mem[c, 0, i] - lost * rates[c][:ROWS]


def wave_kernel(n, *refs):
    merged = is_merged(n)
    sides = len(sides_of(n))
    (mem, dec, los, side, source, side_props, line_tiles) = refs[:7]
    (own_props, own_gain, own_held, cross, own_v, own_s, own_m) = refs[7:14]
    got_d, got_e = refs[14 : 14 + sides], refs[14 + sides : 14 + 2 * sides]
    refs = refs[14 + 2 * sides :]
    far_outs, (near_rows, far_rows, new_v, new_s, new_m, sems) = refs[:3], refs[3:]
    even = lax.rem(lax.axis_index("gx"), 2) == 0
    sub = sublane((8, LANES))
    no_rows, no_halo = jnp.zeros((ROWS, LANES), F32), jnp.zeros((8, LANES), F32)

    column = {}
    for i in range(4):
        column["own", GAIN, i] = own_gain[i]
        for p in range(3):
            column["own", LAME + p, i] = own_props[p, i]
    for k, l in enumerate(OUTER):
        for c in range(6):
            column["own", HELD + c, l - 2] = own_held[c, k]
    for k, (c, i) in enumerate(((XX, 0), (XY, 3), (XZ, 3))):
        column["own", STRESS + c, i] = cross[k]

    def corner_rows(table, rows, f, i):
        value = None
        for k, (g, j, r) in enumerate(rows):
            if (g, j) == (f, i):
                row = jnp.broadcast_to(table[k : k + 1, :], (8, LANES))
                value = jnp.where(sub == (r % 8), row, 0.0 if value is None else value)
        return value

    face = {}
    for at, (name, which) in enumerate((("before", LAST), ("after", FIRST))):
        group = 0 if merged else at
        if group == at:
            near, far = got_e[group][...].astype(F32), got_d[group][...].astype(F32)
            near_rows[...] = jnp.where(even, near, far)
            far_rows[...] = jnp.where(even, far, near)
            after = jnp.broadcast_to(near_rows[len(ABOVE) : len(ABOVE) + 1, :], (8, LANES))
            before = jnp.broadcast_to(far_rows[len(BELOW) : len(BELOW) + 1, :], (8, LANES))
            laid, covered = tile_rows_around(n, line_tiles, 1 + group, after, before)

        def corner_halo(f, i):
            above = corner_rows(near_rows, ABOVE, f, i)
            below = corner_rows(far_rows, BELOW, f, i)
            if above is None or below is None:
                halo = no_halo if above is below else (below if above is None else above)
            else:
                halo = jnp.where(sub < 4, above, below)
            if f >= LAME:
                halo = jnp.where(covered, halo_rows(laid[f - LAME], i), halo)
            return halo

        edge = 3 if name == "before" else 0
        layers = (2, 3) if name == "before" else (0, 1)
        for f in range(FIELDS):
            for i in layers:
                if not (f < VEL or f in range(HELD, GAIN) or (f, i) in which):
                    continue
                halo = corner_halo(f, i)
                main = no_rows
                if f >= LAME:
                    main = side_props[SIDE_PROPS.index((name, f, i))]
                elif (f, i) in which:
                    main = side[SIDES.index((name, f, i)), 0:ROWS]
                if f < VEL:
                    column[name, f, i] = jnp.concatenate([no_rows, halo], 0)
                    if (f, i) in which:
                        face[name, f] = jnp.concatenate([main, halo], 0)
                else:
                    column[name, f, i] = jnp.concatenate([main, halo], 0)
        for f, i in which:
            if isinstance(f, str):
                column[name, f, i] = side[SIDES.index((name, f, i))]

    def layers_of(f):
        names = [("before", 2), ("before", 3)] + [("own", i) for i in range(4)] + [("after", 0), ("after", 1)]
        return [column.get((name, f, i)) for name, i in names]

    s0 = [layers_of(STRESS + c) for c in range(6)]
    v0 = [layers_of(VEL + c) for c in range(3)]
    held = [layers_of(HELD + c) for c in range(6)]
    gain, lame, shear, buoy = (layers_of(f) for f in (GAIN, LAME, MU, BUOY))

    move, rates_at, link_before, link_after = rules(n, lame, shear, buoy)
    faces = {XX: face["after", STRESS + XX], XY: face["before", STRESS + XY], XZ: face["before", STRESS + XZ]}
    faces = {XX: face["after", STRESS + XX], XY: face["before", STRESS + XY], XZ: face["before", STRESS + XZ]}
    copies = []

    def send(k, i):
        near, far = (new_v, new_s, new_m)[k], far_outs[k]
        copies.append(pltpu.make_async_copy(near.at[:, :, i], far.at[:, :, i], sems.at[k, i]))
        copies[-1].start()

    v1, v2 = ([[None] * 8 for _ in range(3)] for _ in range(2))
    s1 = [[None] * 8 for _ in range(6)]
    m1 = {}
    sums1 = [layers_of(g) for g in ("gx", "gy", "gz")]
    sums2 = [layers_of(h) for h in (None, "hy", "hz")]
    for l in range(2, 6):
        for c in range(3):
            v1[c][l] = own_v[c, l - 2]
    for k, l in enumerate(INNER):
        for c in range(6):
            s1[c][l] = own_s[c, k]
            m1[c, l] = own_m[c, k]

    def at_corner(d, l, link, sign, c):
        more = sign * courant * buoy[l][ROWS:] * jnp.where(link[ROWS:], faces[c][ROWS:], 0.0)
        v1[d][l] = jnp.concatenate([v1[d][l][:ROWS], v1[d][l][ROWS:] + more], 0)

    at_corner(0, 5, link_after, 1.0, XX)
    at_corner(1, 2, link_before, -1.0, XY)
    at_corner(2, 2, link_before, -1.0, XZ)
    for at in range(9):
        move(v1, v0, s0, at, ((0, 1, 6), (1, 6, 7)), sums1, {})
        l = at - 1
        if l in (1, 2, 5, 6):
            wanted = (XX, XY, XZ) if l == 1 else range(6)
            rates = rates_at(v1, l, wanted)
            for c in wanted:
                s1[c][l] = held[c][l] + gain[l] * rates[c]
                if 2 <= l < 6:
                    i = l - 2
                    lost = (1.0 - dec[0, i]) * los[0, i]
                    m1[c, l] = dec[0, i] * mem[c, 0, i] - lost * rates[c][:ROWS]
        l = at - 2
        move(v2, v1, s1, l, (range(1, 6), range(2, 7)), sums2, {})
        if l in range(2, 6):
            for c in range(3):
                new_v[c, 0, l - 2] = v2[c][l][:ROWS]
            send(0, l - 2)
        l = at - 3
        if l in range(2, 6):
            i = l - 2
            rates = rates_at(v2, l, range(6))
            d = dec[0, i]
            lost = (1.0 - d) * los[0, i]
            for c in range(6):
                rate = rates[c][:ROWS]
                m2 = d * m1[c, l] - lost * rate
                new_m[c, 0, i] = m2
                value = s1[c][l][:ROWS] + courant * (rate + m2)
                if c < 3:
                    value = value + source[i * ROWS : (i + 1) * ROWS, :]
                new_s[c, 0, i] = value
            send(1, i)
            send(2, i)
    for copy in copies:
        copy.wait()


def body(
    velocity,
    stress,
    memory,
    lame_lambda,
    lame_mu,
    buoyancy,
    decay,
    loss,
    tile_lambda,
    tile_mu,
    tile_buoy,
    tile_dest,
    brick_tiles,
    src_index,
    src_wave,
):
    n = lax.axis_size("gx")
    merged = is_merged(n)
    sides = sides_of(n)
    chunk = tile_chunk(n)
    on_core = pl.BlockSpec(memory_space=pltpu.VMEM)
    away = pl.BlockSpec(memory_space=pltpu.HBM)
    def vmem(*shape):
        return jax.ShapeDtypeStruct(shape, F32)

    waves = src_wave.T
    cells = src_index[None, :]
    fields = (velocity, stress, memory, lame_lambda, lame_mu, buoyancy, decay, loss)
    if merged:
        c_rows = [LONGEST * ROWS + 16]
    else:
        c_rows = [len(LAST) * ROWS + 16, len(FIRST) * ROWS + 16]
    tiles = (tile_lambda, tile_mu, tile_buoy)
    kept = (decay, loss, stress, memory, velocity, lame_lambda, lame_mu, buoyancy)
    inputs = (*tiles, tile_dest, decay, loss, cells, waves, stress, memory, velocity, lame_lambda, lame_mu, buoyancy, brick_tiles)
    inputs = tuple(pltpu.with_memory_space_constraint(x, pltpu.HBM) for x in inputs)
    packed = pl.pallas_call(
        functools.partial(pack_kernel, n, tile_lambda.shape[0]),
        out_shape=[
            jax.ShapeDtypeStruct((BLOCK, LANES), F32),
            jax.ShapeDtypeStruct((BLOCK, LANES), F32),
            jax.ShapeDtypeStruct((CORNER, LANES), BF16),
            jax.ShapeDtypeStruct((CORNER, LANES), BF16),
            jax.ShapeDtypeStruct((8, LANES), F32),
            jax.ShapeDtypeStruct((n * chunk, LANES), BF16),
        ]
        + [jax.ShapeDtypeStruct(x.shape, x.dtype) for x in kept]
        + [vmem(6, 4, ROWS, LANES), vmem(4 * ROWS, LANES)]
        + [jax.ShapeDtypeStruct((r, LANES), BF16) for r in c_rows],
        in_specs=[away] * len(inputs),
        out_specs=[on_core] * 5 + [away] + [on_core] * (10 + len(c_rows)),
        scratch_shapes=[
            pltpu.SMEM(x.shape, x.dtype) if x.ndim == 1 else pltpu.VMEM(x.shape, x.dtype)
            for x in (*tiles, tile_dest, cells, waves, brick_tiles)
        ]
        + [
            pltpu.SemaphoreType.DMA((16,)),
            pltpu.VMEM((4, ROWS, LANES), F32),
            pltpu.VMEM((4 * ROWS, LANES), F32),
            pltpu.VMEM((2 * CORNER, LANES), F32),
            pltpu.VMEM((16, LANES), F32),
            pltpu.VMEM((n * chunk, LANES), F32),
            pltpu.VMEM((n * chunk, LANES), BF16),
        ],
        compiler_params=pltpu.CompilerParams(vmem_limit_bytes=16 * 1024 * 1024),
        name="pack",
    )(*inputs)
    out_a, out_b, out_d, out_e, own_map, out_t = packed[:6]
    held, later = packed[14:16]
    out_c = packed[16:]
    dec, los, st, mem, vel, lam, mu, bu = packed[6:14]

    def permute(array, source_of):
        return lax.ppermute(array, "gx", [(source_of(i), i) for i in range(n)])

    got_c = [permute(c, lambda i, o=o: (i + o) % n) for c, o in zip(out_c, sides)]
    got_d = [permute(out_d, lambda i, o=o: pair_far((i + o) % n, n)) for o in sides]
    got_e = [permute(out_e, lambda i, o=o: pair_near((i + o) % n)) for o in sides]
    got_b = permute(out_b, lambda i: pair_far(i, n))
    got_a = permute(out_a, pair_near)
    got_t = lax.all_to_all(out_t, "gx", split_axis=0, concat_axis=0, tiled=True)

    side = pl.pallas_call(
        functools.partial(side_kernel, n),
        out_shape=vmem(len(SIDES), EXT, LANES),
        in_specs=[on_core] * len(sides),
        out_specs=on_core,
        scratch_shapes=[pltpu.VMEM((16, LANES), F32)],
        compiler_params=pltpu.CompilerParams(vmem_limit_bytes=16 * 1024 * 1024),
        name="sides",
    )(*got_c)
    own_props, side_props, line_tiles = pl.pallas_call(
        functools.partial(tile_kernel, n),
        out_shape=[
            vmem(3, 4, ROWS, LANES),
            vmem(len(SIDE_PROPS), ROWS, LANES),
            vmem(3 + 3 * len(sides), n * 16, LANES),
        ],
        in_specs=[on_core] * (5 + len(sides)),
        out_specs=[on_core] * 3,
        scratch_shapes=[
            pltpu.VMEM((n * chunk, LANES), F32),
            pltpu.VMEM((16 * 32, LANES), BF16),
            pltpu.VMEM((16 * 32, LANES), F32),
            pltpu.VMEM((16, LANES), F32),
        ],
        compiler_params=pltpu.CompilerParams(vmem_limit_bytes=16 * 1024 * 1024),
        name="tiles",
    )(lam, mu, bu, own_map, got_t, *got_c)
    first = pl.pallas_call(
        functools.partial(first_kernel, n),
        out_shape=[
            vmem(3, 4, EXT, LANES),
            vmem(4, EXT, LANES),
            vmem(6, 2, EXT, LANES),
            vmem(3, EXT, LANES),
            vmem(3, 4, EXT, LANES),
            vmem(6, 2, EXT, LANES),
            vmem(6, 2, ROWS, LANES),
        ],
        in_specs=[on_core] * 11,
        out_specs=[on_core] * 7,
        compiler_params=pltpu.CompilerParams(vmem_limit_bytes=16 * 1024 * 1024),
        name="first",
    )(vel, st, mem, dec, los, held, side, own_props, line_tiles, got_a, got_b)
    outs = (velocity, stress, memory)
    return pl.pallas_call(
        functools.partial(wave_kernel, n),
        out_shape=[jax.ShapeDtypeStruct(x.shape, F32) for x in outs],
        in_specs=[on_core] * (14 + 2 * len(sides)),
        out_specs=[away] * 3,
        scratch_shapes=[
            pltpu.VMEM((CORNER, LANES), F32),
            pltpu.VMEM((CORNER, LANES), F32),
        ]
        + [pltpu.VMEM(x.shape, F32) for x in outs]
        + [pltpu.SemaphoreType.DMA((3, 4))],
        compiler_params=pltpu.CompilerParams(vmem_limit_bytes=48 * 1024 * 1024),
        name="wave",
    )(mem, dec, los, side, later, side_props, line_tiles, *first, *got_d, *got_e)


def solution(mesh):
    split = ("groups", "gx")
    whole = P(None, split, None, None, None)
    field = P(split, None, None, None)
    return jax.shard_map(
        body,
        mesh=mesh,
        in_specs=(whole,) * 3
        + (field,) * 5
        + (P(split, None),) * 3
        + (P(split), P(split, None), P(split), P(split, None)),
        out_specs=(whole,) * 3,
        check_vma=False,
    )
```
